32 devices in a mesh: var: 4 (over x, core), ty: 2 (over y), tx: 4 (over z).
Axes of the slice: x: 2, y: 2, z: 4, core: 2. Of those that a mesh axis runs over, the one named last changes fastest.
Arguments:
- features: bfloat16 [128, 128, 180], P('ty', 'tx'), may hold values from -6 to 6
- labels: int32 [128, 128], P('ty', 'tx'), may hold values from 1 to 4
- qkv_weight: bfloat16 [2, 180, 540], replicated, may hold values from -0.4375 to 0.4375
- proj_weight: bfloat16 [2, 180, 180], replicated, may hold values from -0.4375 to 0.4375
- up_weight: bfloat16 [2, 180, 360], replicated, may hold values from -0.4375 to 0.4375
- down_weight: bfloat16 [2, 360, 180], replicated, may hold values from -0.3125 to 0.3125
- swin_bias: float32 [2, 6, 225], replicated, may hold values from -340 to 340
- recon_weight: bfloat16 [9, 180, 48], replicated, may hold values from -0.3125 to 0.3125
- refine_qkv: bfloat16 [48, 144], replicated, may hold values from -0.875 to 0.875
- refine_proj: bfloat16 [48, 48], replicated, may hold values from -0.875 to 0.875
- refine_bias: float32 [2, 225], replicated, may hold values from -340 to 340
Outputs:
- restored: float32 [3, 512, 512], P(None, 'ty', 'tx')
The draws below stay inside these ranges and needn't reach their ends.
All inputs are finite; a program needn't handle non-finite values.
Results may differ from the reference program's by a relative error of at most 0.015.
Values may be sent and summed in bfloat16 or wider, within the bound.
No kernel may reach another device: no remote copies, remote signals or barrier semaphores. Data moves between devices by JAX's collectives and lax.ppermute only.
A program may use at most 128 MiB of HBM per device.

```python
import jax
import jax.numpy as jnp
from jax import lax

C = 180
HEADS = 6
HID = 360
WIN = 8
SHIFT = 4
SCALE = 4
OUTC = 48
RHEADS = 2
IMAGE = 128


def drawn_bias(key, leading):
    count = (2 * WIN - 1) * (2 * WIN - 1)
    sample = jax.random.normal(jax.random.fold_in(key, 13), leading + (count,), jnp.float32)
    return 1.5 * jnp.clip(sample, -3.0, 3.0)


def draw_swin_bias(key, part):
    return drawn_bias(key, (2, HEADS))


def draw_refine_bias(key, part):
    return drawn_bias(key, (RHEADS,))


def band_steps(key):
    positions = jnp.arange(IMAGE, dtype=jnp.int32)
    cuts = jax.random.randint(key, (IMAGE,), 0, 24) == 0
    cuts = cuts | (positions == IMAGE // 2)
    cuts = jnp.where(positions == 0, False, cuts)
    return jnp.cumsum(cuts.astype(jnp.int32))


def draw_labels(key, part):
    row_band = band_steps(jax.random.fold_in(key, 21))
    col_band = band_steps(jax.random.fold_in(key, 22))
    return (1 + (row_band[:, None] + 2 * col_band[None, :]) % 4).astype(jnp.int32)


def steps_of(key, dims, shards, least, high):
    factor_of, own = 1.0, jax.random.fold_in(key, 6)
    for dim, blocks in shards:
        draws = jnp.exp(jax.random.uniform(jax.random.fold_in(own, dim), (blocks,), jnp.float32, least / len(shards), high / len(shards)))
        factor_of = factor_of * jnp.repeat(draws, dims[dim] // blocks).reshape([-1 if axis == dim else 1 for axis in range(len(dims))])
    return factor_of


def normal_values(stream_key, shape, scale, reach, pieces=(), held_as=jnp.bfloat16):
    values = jax.random.normal(stream_key, shape, jnp.float32) * scale
    if len(pieces) > 0:
        values = steps_of(stream_key, shape, pieces, -0.22, 0.18) * values
    return jnp.clip(values, min=-reach, max=reach).astype(held_as)


def setup_inputs(seed: int = 0) -> dict:
    seeds = jax.random.split(jax.random.key(seed), 12)
    return {
        "features": normal_values(seeds[0], (IMAGE, IMAGE, C), 1.0, 6.0, ((0, 2), (1, 4))),
        "labels": draw_labels(jax.random.fold_in(seeds[11], 71), 0),
        "qkv_weight": normal_values(seeds[2], (2, C, 3 * C), C ** -0.5, 0.4375),
        "proj_weight": normal_values(seeds[3], (2, C, C), C ** -0.5, 0.4375),
        "up_weight": normal_values(seeds[4], (2, C, HID), C ** -0.5, 0.4375),
        "down_weight": normal_values(seeds[5], (2, HID, C), HID ** -0.5, 0.3125),
        "swin_bias": draw_swin_bias(jax.random.fold_in(seeds[11], 71), 0),
        "recon_weight": normal_values(seeds[7], (9, C, OUTC), (9 * C // 4) ** -0.5, 0.3125),
        "refine_qkv": normal_values(seeds[8], (OUTC, 3 * OUTC), OUTC ** -0.5, 0.875),
        "refine_proj": normal_values(seeds[9], (OUTC, OUTC), OUTC ** -0.5, 0.875),
        "refine_bias": draw_refine_bias(jax.random.fold_in(seeds[11], 71), 0),
    }


EPSILON = 1e-05
MASKED = -1e+30

def normalize(values):
    values = values.astype(jnp.float32)
    average = lax.optimization_barrier(jnp.mean(values, axis=-1, keepdims=True))
    centred = values - average
    spread = lax.optimization_barrier(jnp.mean(centred * centred, axis=-1, keepdims=True))
    return centred * lax.rsqrt(spread + EPSILON)

def to_windows(grid):
    leading, height, breadth, channels = grid.shape
    grid = grid.reshape(leading, height // WIN, WIN, breadth // WIN, WIN, channels)
    grid = grid.transpose(0, 1, 3, 2, 4, 5)
    return grid.reshape(leading, height // WIN * (breadth // WIN), WIN * WIN, channels)

def from_windows(windows, height, breadth):
    leading, window_count, cells, channels = windows.shape
    windows = windows.reshape(leading, height // WIN, breadth // WIN, WIN, WIN, channels)
    windows = windows.transpose(0, 1, 3, 2, 4, 5)
    return windows.reshape(leading, height, breadth, channels)

def bias_table(offset_table, variant_codes):
    position = jnp.arange(WIN * WIN, dtype=jnp.int32)
    row_step = (position // WIN)[:, None] - (position // WIN)[None, :]
    across = (position % WIN)[:, None] - (position % WIN)[None, :]
    transpose_bit = (variant_codes // 4)[:, None, None]
    flip_rows = (variant_codes // 2 % 2)[:, None, None]
    flip_cols = (variant_codes % 2)[:, None, None]
    row_moved = jnp.where(flip_rows == 1, -row_step, row_step)
    col_moved = jnp.where(flip_cols == 1, -across, across)
    leading_step = jnp.where(transpose_bit == 1, col_moved, row_moved)
    trailing_step = jnp.where(transpose_bit == 1, row_moved, col_moved)
    table_index = (leading_step + WIN - 1) * (2 * WIN - 1) + trailing_step + WIN - 1
    slots = jnp.arange((2 * WIN - 1) * (2 * WIN - 1), dtype=jnp.int32)
    one_hot = (table_index[..., None] == slots).astype(jnp.float32)
    return jnp.einsum('vqkt,ht->vhqk', one_hot, offset_table, precision=lax.Precision.HIGHEST)

def attend(normed, region, w_qkv, w_proj, bias_grid):
    head_count = bias_grid.shape[1]
    leading, window_count, cells, channels = normed.shape
    head_width = channels // head_count
    projected = jnp.einsum('lnsc,ce->lnse', normed.astype(jnp.float32), w_qkv.astype(jnp.float32)).astype(jnp.bfloat16)
    projected = projected.reshape(leading, window_count, cells, 3, head_count, head_width)
    queries = projected[:, :, :, 0].astype(jnp.float32)
    key_part = projected[:, :, :, 1].astype(jnp.float32)
    value_part = projected[:, :, :, 2]
    scores = jnp.einsum('lnqhd,lnkhd->lnhqk', queries, key_part)
    scores = scores * head_width ** (-0.5) + bias_grid[:, None]
    matches = region[:, None, :, None] == region[:, None, None, :]
    scores = jnp.where(matches[None], scores, MASKED)
    largest = lax.optimization_barrier(jnp.max(scores, axis=-1, keepdims=True))
    weights = jnp.exp(scores - largest)
    probabilities = (weights / lax.optimization_barrier(jnp.sum(weights, axis=-1, keepdims=True))).astype(jnp.bfloat16)
    value_part = jnp.broadcast_to(value_part, (probabilities.shape[0],) + value_part.shape[1:])
    mixed = jnp.einsum('lnhqk,lnkhd->lnqhd', probabilities.astype(jnp.float32), value_part.astype(jnp.float32)).astype(jnp.bfloat16)
    mixed = mixed.reshape(probabilities.shape[0], window_count, cells, channels)
    return jnp.einsum('lnsc,ce->lnse', mixed.astype(jnp.float32), w_proj.astype(jnp.float32))

def attention_half(tokens, region, w_qkv, w_proj, bias_grid):
    height, breadth = (tokens.shape[1], tokens.shape[2])
    windows = to_windows(tokens)
    region_windows = to_windows(region[None, :, :, None])[0, :, :, 0]
    normed = normalize(windows).astype(jnp.bfloat16)
    branch = attend(normed, region_windows, w_qkv, w_proj, bias_grid)
    result = (windows.astype(jnp.float32) + branch).astype(jnp.bfloat16)
    return from_windows(result, height, breadth)

def feed_forward(tokens, w_up, w_down):
    normed = normalize(tokens).astype(jnp.bfloat16)
    hidden = jnp.einsum('...c,ce->...e', normed.astype(jnp.float32), w_up.astype(jnp.float32))
    hidden = jax.nn.gelu(hidden, approximate=False).astype(jnp.bfloat16)
    output = tokens.astype(jnp.float32) + jnp.einsum('...e,ec->...c', hidden.astype(jnp.float32), w_down.astype(jnp.float32))
    return output.astype(jnp.bfloat16)

def reconstruct(padded, kernels, height, breadth):
    accumulated = jnp.zeros((padded.shape[0], height, breadth, kernels.shape[-1]), jnp.float32)
    for kernel_spot in range(9):
        spot_row, spot_col = (kernel_spot // 3, kernel_spot % 3)
        window = padded[:, spot_row:spot_row + height, spot_col:spot_col + breadth]
        accumulated = accumulated + jnp.einsum('vrcd,vde->vrce', window.astype(jnp.float32), kernels[:, kernel_spot].astype(jnp.float32))
    return accumulated

def forward(picture, transpose_bit, flip_rows, flip_cols):
    picture = jnp.where(flip_rows == 1, jnp.flip(picture, 0), picture)
    picture = jnp.where(flip_cols == 1, jnp.flip(picture, 1), picture)
    return jnp.where(transpose_bit == 1, jnp.swapaxes(picture, 0, 1), picture)

def reference(features, labels, qkv_weight, proj_weight, up_weight, down_weight, swin_bias, recon_weight, refine_qkv, refine_proj, refine_bias):
    extent = features.shape[0]
    identity = jnp.zeros((1,), jnp.int32)
    first_bias = bias_table(swin_bias[0], identity)
    second_bias = bias_table(swin_bias[1], identity)

    def one_variant(accumulated, variant_code):
        transpose_bit = variant_code // 4
        flip_rows = variant_code // 2 % 2
        flip_cols = variant_code % 2
        picture = forward(features, transpose_bit, flip_rows, flip_cols)
        region = forward(labels, transpose_bit, flip_rows, flip_cols)
        block_one = attention_half(picture[None], region, qkv_weight[0], proj_weight[0], first_bias)
        block_one = feed_forward(block_one, up_weight[0], down_weight[0])
        padded = jnp.pad(block_one, ((0, 0), (SHIFT, SHIFT), (SHIFT, SHIFT), (0, 0)))
        padded_region = jnp.pad(region, SHIFT)
        block_two = attention_half(padded, padded_region, qkv_weight[1], proj_weight[1], second_bias)
        block_two = feed_forward(block_two[:, SHIFT:-SHIFT, SHIFT:-SHIFT], up_weight[1], down_weight[1])
        bordered = jnp.pad(block_two, ((0, 0), (1, 1), (1, 1), (0, 0)))
        convolved = reconstruct(bordered, recon_weight[None], extent, extent)[0]
        upscaled = convolved.reshape(extent, extent, 3, SCALE, SCALE).transpose(2, 0, 3, 1, 4)
        upscaled = upscaled.reshape(3, SCALE * extent, SCALE * extent)
        upscaled = jnp.where(transpose_bit == 1, jnp.swapaxes(upscaled, 1, 2), upscaled)
        upscaled = jnp.where(flip_rows == 1, jnp.flip(upscaled, 1), upscaled)
        upscaled = jnp.where(flip_cols == 1, jnp.flip(upscaled, 2), upscaled)
        return (accumulated + upscaled, variant_code)
    start_sum = jnp.zeros((3, SCALE * extent, SCALE * extent), jnp.float32)
    accumulated, leftover = lax.scan(one_variant, start_sum, jnp.arange(8, dtype=jnp.int32))
    average = accumulated / 8.0
    grid = average.reshape(3, extent, SCALE, extent, SCALE).transpose(1, 3, 0, 2, 4)
    grid = grid.reshape(extent, extent, 3 * SCALE * SCALE)
    windows = to_windows(grid[None])
    region_windows = to_windows(labels[None, :, :, None])[0, :, :, 0]
    normed = normalize(windows).astype(jnp.bfloat16)
    refine_grid = bias_table(refine_bias, identity)
    refined = windows + attend(normed, region_windows, refine_qkv, refine_proj, refine_grid)
    refined = from_windows(refined, extent, extent)[0]
    picture = refined.reshape(extent, extent, 3, SCALE, SCALE).transpose(2, 0, 3, 1, 4)
    return picture.reshape(3, SCALE * extent, SCALE * extent)
```

```python
import functools

import jax
import jax.numpy as jnp
from jax import lax
from jax.experimental import pallas as pl
from jax.experimental.pallas import tpu as pltpu
from jax.sharding import PartitionSpec as P

WIN = 8
CELLS = WIN * WIN
SHIFT = 4
SCALE = 4
VAR_DEV = 2
LANES = 128
HEAD_ROWS = 32
CLASSES = 4
SIDE = 2 * WIN - 1

EPSILON = 1e-05
LOG2E = 1.4426950408889634
BIG = float(2.0**100)
ERF_TANH = (
    7.97884207935252e-01,
    3.63342879e-02,
    -3.31288562e-05,
    -5.52410746e-05,
    3.96927395e-06,
    -1.33457816e-07,
    1.80588519e-09,
)

NN = (((1,), (0,)), ((), ()))
NT = (((1,), (1,)), ((), ()))


def dot(a, b, dims=NN):
    return lax.dot_general(a, b, dims, preferred_element_type=jnp.float32)


def gelu(x):
    square = x * x
    series = jnp.full_like(square, ERF_TANH[-1])
    for factor in ERF_TANH[-2::-1]:
        series = series * square + factor
    half = 0.5 * x
    return half + half * jnp.tanh(x * series)


def normalize(x, channels):
    inside = lax.broadcasted_iota(jnp.int32, (1, x.shape[1]), 1) < channels
    x = jnp.where(inside, x, 0.0)
    mean = jnp.sum(x, axis=1, keepdims=True) * (1.0 / channels)
    centred = jnp.where(inside, x - mean, 0.0)
    spread = jnp.sum(centred * centred, axis=1, keepdims=True) * (1.0 / channels)
    return centred * lax.rsqrt(spread + EPSILON)


def label_columns(x, channels):
    lane = lax.broadcasted_iota(jnp.int32, (1, x.shape[1]), 1) - channels
    in_class = (lane >= 0) & (lane < CLASSES)
    flag = lane == CLASSES
    key_gain = jnp.where(in_class, 1.0, jnp.where(flag, -1.0, 0.0))
    key_side = x * key_gain + jnp.where(flag, 1.0, 0.0)
    query_side = x * jnp.where(in_class, BIG, 0.0) + jnp.where(in_class | flag, -BIG, 0.0)
    return key_side, query_side


def head_masks(heads, width, channels, lanes):
    lane = lax.broadcasted_iota(jnp.int32, (1, lanes), 1)
    return [
        ((lane >= h * width) & (lane < (h + 1) * width)) | (lane >= channels) for h in range(heads)
    ]


def expand_bias(rows_ref, bias_ref, variant, first_head, heads):
    lane = lax.broadcasted_iota(jnp.int32, (WIN, LANES), 1)
    for pair in range(heads // 2):
        even = rows_ref[variant, first_head + 2 * pair]
        odd = rows_ref[variant, first_head + 2 * pair + 1]
        for key_row in range(WIN):
            start = (WIN - 1 - key_row) * WIN
            left = pltpu.roll(even, (LANES - start) % LANES, 1)
            right = pltpu.roll(odd, (LANES - start + CELLS) % LANES, 1)
            bias_ref[
                variant, key_row * WIN : (key_row + 1) * WIN, pair * LANES : (pair + 1) * LANES
            ] = jnp.where(lane < CELLS, left, right)


def soft(scores):
    largest = jnp.max(scores, axis=0, keepdims=True)
    return jnp.exp2(scores - largest).astype(jnp.bfloat16)


def mix_pair(values, first, second, heads, ones_row):
    zero = jnp.zeros((CELLS, LANES), jnp.bfloat16)
    lane = lax.broadcasted_iota(jnp.int32, (HEAD_ROWS, 2 * LANES), 1) % LANES
    mixed = []
    for pair in range(heads // 2):
        cut = slice(pair * LANES, (pair + 1) * LANES)
        stationary = jnp.concatenate(
            [
                jnp.concatenate([first[:, cut], zero], axis=1),
                jnp.concatenate([zero, second[:, cut]], axis=1),
            ],
            axis=0,
        )
        result = dot(values[pair * CELLS : (pair + 1) * CELLS], stationary)
        joined = jnp.where(lane < CELLS, result[:HEAD_ROWS], result[HEAD_ROWS:])
        mixed.append(joined * pl.reciprocal(joined[ones_row : ones_row + 1]))
    return mixed


def attend_pairs(x, n, scale, heads, w_qk, w_vt, pairs, key_bias):
    channels = heads * (w_vt.shape[0] // heads - 2)
    lanes = x.shape[1]
    projected = dot(n, w_qk)
    key_side, query_side = label_columns(x, channels)
    queries = (projected[:, :lanes] * scale + query_side).astype(jnp.bfloat16)
    keys = (projected[:, lanes:] + key_side).astype(jnp.bfloat16)
    values = dot(w_vt, n, NT)
    row = lax.broadcasted_iota(jnp.int32, values.shape, 0) % HEAD_ROWS
    values = jnp.where(row == channels // heads, 1.0, values).astype(jnp.bfloat16)
    masks = head_masks(heads, channels // heads, channels, lanes)
    scores = []
    for group in range(x.shape[0] // CELLS):
        q = queries[group * CELLS : (group + 1) * CELLS]
        stacked = jnp.concatenate([jnp.where(m, q, jnp.zeros_like(q)) for m in masks], axis=0)
        scores.append(dot(keys[group * CELLS : (group + 1) * CELLS], stacked, NT))
    outputs = []
    pad = jnp.zeros((LANES - heads // 2 * HEAD_ROWS, 2 * LANES), jnp.float32)
    for pair, first_bias, second_bias in pairs:
        first = soft(scores[2 * pair] + key_bias(first_bias))
        second = soft(scores[2 * pair + 1] + key_bias(second_bias))
        mixed = mix_pair(
            values[:, pair * LANES : (pair + 1) * LANES], first, second, heads, channels // heads
        )
        block = jnp.concatenate(mixed + [pad], axis=0).astype(jnp.bfloat16)
        for half in range(2):
            turned = block[:, half * LANES : (half + 1) * LANES].T
            outputs.append(jnp.concatenate([turned[:CELLS], turned[CELLS:]], axis=1))
    return jnp.concatenate(outputs, axis=0)


def feed_forward(h, channels, w_up, w_down):
    n = normalize(h, channels).astype(jnp.bfloat16)
    hidden = gelu(dot(n, w_up)).astype(jnp.bfloat16)
    return h + dot(hidden, w_down)


def round_bf16(x):
    return x.astype(jnp.bfloat16).astype(jnp.float32)


def first_kernel(
    heads, channels, x_ref, rows_ref, w_qk, w_vt, w_proj, w_up, w_down, y_ref, bias_ref
):
    @pl.when(pl.program_id(0) == 0)
    def _():
        for variant in range(VAR_DEV):
            expand_bias(rows_ref, bias_ref, variant, 0, heads)

    grid = x_ref[...].astype(jnp.float32)
    breadth, lanes = grid.shape[1:]
    count = breadth // WIN
    x = jnp.concatenate(
        [grid[:, w * WIN : (w + 1) * WIN].reshape(CELLS, lanes) for w in range(count)], axis=0
    )
    n = normalize(x, channels).astype(jnp.bfloat16)
    scale = (channels // heads) ** -0.5 * LOG2E
    pairs = [(pair, v, v) for v in range(VAR_DEV) for pair in range(count // 2)]
    o = attend_pairs(x, n, scale, heads, w_qk[...], w_vt[...], pairs, lambda v: bias_ref[v])
    branch = dot(o, w_proj[...])
    h = round_bf16(jnp.concatenate([x] * VAR_DEV, axis=0) + branch)
    y = feed_forward(h, channels, w_up[...], w_down[...])
    y = y.reshape(VAR_DEV, count, WIN, WIN, lanes)
    for v in range(VAR_DEV):
        y_ref[v] = jnp.concatenate([y[v, w] for w in range(count)], axis=1).astype(jnp.bfloat16)


def second_kernel(
    heads,
    channels,
    own_ref,
    top_ref,
    bottom_ref,
    left_ref,
    right_ref,
    rows_ref,
    w_qk,
    w_vt,
    w_proj,
    w_up,
    w_down,
    w_recon,
    out_ref,
    padded,
    bias_ref,
    acc,
):
    step = pl.program_id(0)
    height, breadth, lanes = own_ref.shape[1:]
    tall, wide = height + 2 * SHIFT, breadth + 2 * SHIFT
    count = wide // WIN

    @pl.when(step == 0)
    def _():
        for v in range(VAR_DEV):
            expand_bias(rows_ref, bias_ref, v, heads, heads)
            padded[v, 0:SHIFT, SHIFT : SHIFT + breadth] = top_ref[v].astype(jnp.float32)
            padded[v, tall - SHIFT : tall, SHIFT : SHIFT + breadth] = bottom_ref[v].astype(
                jnp.float32
            )
            for r in range(0, height, WIN):
                padded[v, SHIFT + r : SHIFT + r + WIN, SHIFT : SHIFT + breadth] = own_ref[
                    v, r : r + WIN
                ].astype(jnp.float32)
            for r in range(0, tall, WIN):
                cut = slice(r * SHIFT, (r + WIN) * SHIFT)
                padded[v, r : r + WIN, 0:SHIFT] = (
                    left_ref[v, cut].astype(jnp.float32).reshape(WIN, SHIFT, lanes)
                )
                padded[v, r : r + WIN, wide - SHIFT : wide] = (
                    right_ref[v, cut].astype(jnp.float32).reshape(WIN, SHIFT, lanes)
                )
        acc[...] = jnp.zeros_like(acc)

    base = pl.multiple_of(step * WIN, WIN)
    grids = [padded[v, pl.ds(base, WIN)] for v in range(VAR_DEV)]
    x = jnp.concatenate(
        [
            grids[v][:, w * WIN : (w + 1) * WIN].reshape(CELLS, lanes)
            for w in range(count)
            for v in range(VAR_DEV)
        ],
        axis=0,
    )
    n = normalize(x, channels).astype(jnp.bfloat16)
    scale = (channels // heads) ** -0.5 * LOG2E
    pairs = [(pair, 0, 1) for pair in range(count)]
    o = attend_pairs(x, n, scale, heads, w_qk[...], w_vt[...], pairs, lambda v: bias_ref[v])
    h = round_bf16(x + dot(o, w_proj[...]))
    y = feed_forward(h, channels, w_up[...], w_down[...])
    valid = x[:, channels + CLASSES : channels + CLASSES + 1]
    y = (y * valid).astype(jnp.bfloat16)
    total = None
    for v in range(VAR_DEV):
        tokens = jnp.concatenate(
            [y[(VAR_DEV * w + v) * CELLS : (VAR_DEV * w + v + 1) * CELLS] for w in range(count)],
            axis=0,
        )
        part = dot(tokens, w_recon[v])
        total = part if total is None else total + part
    total = total.reshape(count, WIN, WIN, 3 * lanes)
    for e in range(3):
        for w in range(count):
            acc[pl.ds(base + 2 - e, WIN), w * WIN : (w + 1) * WIN] += total[
                w, :, :, e * lanes : (e + 1) * lanes
            ]

    @pl.when(step == pl.num_programs(0) - 1)
    def _():
        out_channels = out_ref.shape[1]
        for strip in range(height // WIN):
            rows = slice(1 + SHIFT + strip * WIN, 1 + SHIFT + (strip + 1) * WIN)
            middle = acc[rows, SHIFT : SHIFT + breadth, :LANES]
            middle = pltpu.roll(middle.reshape(WIN * breadth, LANES), LANES - out_channels, 1)
            result = (
                acc[rows, SHIFT - 1 : SHIFT - 1 + breadth, :LANES]
                + middle.reshape(WIN, breadth, LANES)
                + acc[rows, SHIFT + 1 : SHIFT + 1 + breadth, LANES : 2 * LANES]
            )
            tokens = jnp.concatenate(
                [
                    result[:, w * WIN : (w + 1) * WIN].reshape(CELLS, LANES)
                    for w in range(breadth // WIN)
                ],
                axis=0,
            )
            out_ref[strip] = tokens.T[:out_channels].astype(jnp.bfloat16)


def third_kernel(heads, parts_ref, x_ref, rows_ref, w_qk, w_vt, w_projt, out_ref, bias_ref, final):
    expand_bias(rows_ref, bias_ref, 0, rows_ref.shape[1] - heads, heads)
    sources, strips, channels, strip_tokens = parts_ref.shape
    lanes = x_ref.shape[-1]
    breadth = strip_tokens // WIN
    width = channels // heads
    label_lane = w_qk.shape[1] // 2
    z = jnp.concatenate(
        [
            sum(parts_ref[s, strip].astype(jnp.float32) for s in range(sources))
            for strip in range(strips)
        ],
        axis=1,
    ) * (1.0 / (sources * VAR_DEV))
    mean = jnp.sum(z, axis=0, keepdims=True) * (1.0 / channels)
    centred = z - mean
    spread = jnp.sum(centred * centred, axis=0, keepdims=True) * (1.0 / channels)
    normed = centred * lax.rsqrt(spread + EPSILON)
    nt = normed.astype(jnp.bfloat16)
    tall = jnp.concatenate(
        [normed, jnp.zeros((LANES - channels, normed.shape[1]), jnp.float32)], axis=0
    )
    n = tall.T.astype(jnp.bfloat16)
    labels = x_ref[...].astype(jnp.float32)
    x = jnp.concatenate(
        [
            labels[s * WIN : (s + 1) * WIN, w * WIN : (w + 1) * WIN].reshape(CELLS, lanes)
            for s in range(strips)
            for w in range(breadth // WIN)
        ],
        axis=0,
    )
    spare = lanes - label_lane
    del spare
    lane = lax.broadcasted_iota(jnp.int32, (1, lanes), 1)
    x = jnp.where(lane >= LABEL_LANE(lanes), x, 0.0)
    key_side, query_side = label_columns(x, LABEL_LANE(lanes))
    projected = dot(n, w_qk[...])
    queries = (projected[:, :lanes] * (width**-0.5 * LOG2E) + query_side).astype(jnp.bfloat16)
    keys = (projected[:, lanes:] + key_side).astype(jnp.bfloat16)
    values = dot(w_vt[...], nt)
    row = lax.broadcasted_iota(jnp.int32, values.shape, 0) % HEAD_ROWS
    values = jnp.where(row == width, 1.0, values).astype(jnp.bfloat16)
    masks = head_masks(heads, width, LABEL_LANE(lanes), lanes)
    probabilities = []
    for group in range(x.shape[0] // CELLS):
        q = queries[group * CELLS : (group + 1) * CELLS]
        stacked = jnp.concatenate([jnp.where(m, q, jnp.zeros_like(q)) for m in masks], axis=0)
        scores = dot(keys[group * CELLS : (group + 1) * CELLS], stacked, NT)
        probabilities.append(soft(scores + bias_ref[0]))
    lane128 = lax.broadcasted_iota(jnp.int32, (channels, LANES), 1)
    branches = []
    for pair in range(len(probabilities) // 2):
        mixed = mix_pair(
            values[:, pair * LANES : (pair + 1) * LANES],
            probabilities[2 * pair],
            probabilities[2 * pair + 1],
            heads,
            width,
        )[0].astype(jnp.bfloat16)
        both = dot(w_projt[...], mixed)
        even, odd = both[:channels], both[channels:]
        sides = []
        for half in range(2):
            cut = slice(half * LANES, (half + 1) * LANES)
            sides.append(even[:, cut] + pltpu.roll(odd[:, cut], CELLS, 1))
        branches.append(jnp.where(lane128 < CELLS, sides[0], pltpu.roll(sides[1], CELLS, 1)))
    refined = (z + jnp.concatenate(branches, axis=1)).astype(jnp.bfloat16)
    stacked = jnp.concatenate(
        [refined[:, s * strip_tokens : (s + 1) * strip_tokens] for s in range(strips)], axis=0
    )
    token = lax.broadcasted_iota(jnp.int32, (strip_tokens, WIN * breadth * SCALE), 0)
    place = lax.broadcasted_iota(jnp.int32, (strip_tokens, WIN * breadth * SCALE), 1)
    cell = place // SCALE
    source = (cell % breadth // WIN) * CELLS + (cell // breadth) * WIN + cell % WIN
    spread_matrix = jnp.where(token == source, 1.0, 0.0).astype(jnp.bfloat16)
    wide = dot(stacked, spread_matrix)
    sub = lax.broadcasted_iota(jnp.int32, wide.shape, 1) % SCALE
    own = lax.broadcasted_iota(jnp.int32, wide.shape, 0) % SCALE
    wide = jnp.where(sub == own, wide, 0.0).astype(jnp.bfloat16)
    folded_rows = wide.shape[0] // SCALE
    pick_row = lax.broadcasted_iota(jnp.int32, (folded_rows, wide.shape[0]), 0)
    pick_col = lax.broadcasted_iota(jnp.int32, (folded_rows, wide.shape[0]), 1)
    pick = jnp.where(pick_col // SCALE == pick_row, 1.0, 0.0).astype(jnp.bfloat16)
    folded = dot(pick, wide)
    colours = channels // (SCALE * SCALE)
    row_lanes = breadth * SCALE
    for s in range(strips):
        for c in range(colours):
            first = (s * colours + c) * SCALE
            for y in range(WIN):
                start = (s * WIN + y) * SCALE
                final[c, start : start + SCALE] = folded[
                    first : first + SCALE, y * row_lanes : (y + 1) * row_lanes
                ]
    out_ref[...] = final[...].astype(jnp.bfloat16)


def LABEL_LANE(lanes):
    return 180 * lanes // 256


def shifted(strip, axis, step):
    count = lax.axis_size(axis)
    pairs = [(i, i + step) for i in range(count) if 0 <= i + step < count]
    return lax.ppermute(strip, axis, pairs)


def variant_steps(codes, row_step, col_step):
    shape = (-1,) + (1,) * row_step.ndim
    turn = (codes // 4).reshape(shape) == 1
    row = jnp.where((codes // 2 % 2).reshape(shape) == 1, -row_step, row_step)
    col = jnp.where((codes % 2).reshape(shape) == 1, -col_step, col_step)
    return jnp.where(turn, col, row), jnp.where(turn, row, col)


def bias_rows(tables, codes):
    place = jnp.arange(LANES, dtype=jnp.int32)
    row_step = jnp.broadcast_to((place // WIN - (WIN - 1))[None, :], (WIN, LANES))
    key_col = jnp.arange(WIN, dtype=jnp.int32)[:, None]
    col_step = (place % WIN)[None, :] - key_col
    lead, trail = variant_steps(codes, row_step, col_step)
    index = (lead + WIN - 1) * SIDE + trail + WIN - 1
    slots = jnp.arange(SIDE * SIDE, dtype=jnp.int32)
    one_hot = (index[:, None] == slots[None, :, None, None]).astype(jnp.float32)
    return jnp.einsum("ht,vtkp->vhkp", tables, one_hot, precision=lax.Precision.HIGHEST)


def variant_recon(kernel, codes, rows, lanes):
    spot = jnp.arange(9, dtype=jnp.int32)
    out = kernel.shape[-1]
    lead, trail = variant_steps(codes, spot // 3 - 1, spot % 3 - 1)
    source = (lead + 1) * 3 + trail + 1
    pick_place = (source[:, :, None] == spot).astype(jnp.bfloat16)
    channel = jnp.arange(out, dtype=jnp.int32)
    colour = channel // (SCALE * SCALE)
    turn = (codes // 4)[:, None] == 1
    sub_row = jnp.broadcast_to(channel % (SCALE * SCALE) // SCALE, (codes.shape[0], out))
    sub_col = jnp.broadcast_to(channel % SCALE, (codes.shape[0], out))
    sub_row = jnp.where((codes // 2 % 2)[:, None] == 1, SCALE - 1 - sub_row, sub_row)
    sub_col = jnp.where((codes % 2)[:, None] == 1, SCALE - 1 - sub_col, sub_col)
    anchor_row = jnp.where(turn, sub_col, sub_row)
    anchor_col = jnp.where(turn, sub_row, sub_col)
    anchor = colour * SCALE * SCALE + anchor_row * SCALE + anchor_col
    pick_channel = (channel[None, :, None] == anchor[:, None, :]).astype(jnp.bfloat16)
    placed = jnp.einsum("vpq,qcs->vpcs", pick_place, kernel)
    placed = jnp.einsum("vpcs,vso->vpco", placed, pick_channel)
    placed = placed.reshape(codes.shape[0], 3, 3, kernel.shape[1], out)
    blank = jnp.zeros_like(placed[:, :, 0])
    joined = jnp.concatenate([placed[:, :, 0], placed[:, :, 1]], axis=-1)
    joined = jnp.pad(joined, ((0, 0),) * 3 + ((0, LANES - 2 * out),))
    last = jnp.pad(placed[:, :, 2], ((0, 0),) * 3 + ((0, lanes - LANES - out),))
    del blank
    joined = jnp.concatenate([joined, last], axis=-1)
    joined = joined.transpose(0, 2, 1, 3).reshape(codes.shape[0], kernel.shape[1], 3 * lanes)
    return jnp.pad(joined, ((0, 0), (0, rows - kernel.shape[1]), (0, 0)))


def pad_to(array, *shape):
    return jnp.pad(array, [(0, want - have) for have, want in zip(array.shape, shape)])


def head_rows(weight, heads):
    channels = weight.shape[0]
    split = weight.T.reshape(heads, weight.shape[1] // heads, channels)
    return pad_to(split, heads, HEAD_ROWS, channels).reshape(heads * HEAD_ROWS, channels)


def local(
    features,
    labels,
    qkv_weight,
    proj_weight,
    up_weight,
    down_weight,
    swin_bias,
    recon_weight,
    refine_qkv,
    refine_proj,
    refine_bias,
):
    height, breadth, channels = features.shape
    heads = swin_bias.shape[1]
    out_channels = recon_weight.shape[-1]
    refine_heads = refine_bias.shape[0]
    lanes = -(-(channels + CLASSES + 1) // LANES) * LANES
    hidden = -(-up_weight.shape[-1] // LANES) * LANES
    codes = lax.axis_index("var") * VAR_DEV + jnp.arange(VAR_DEV, dtype=jnp.int32)

    lane = jnp.arange(lanes - channels, dtype=jnp.int32)
    marks = (labels[:, :, None] == lane + 1) & (lane < CLASSES) | (lane == CLASSES)
    x = jnp.concatenate([features, marks.astype(jnp.bfloat16)], axis=-1)

    tables = jnp.concatenate([swin_bias[0], swin_bias[1], refine_bias], axis=0) * LOG2E
    rows = bias_rows(tables[: 2 * heads], codes)
    refine_rows = bias_rows(tables[2 * heads :], jnp.zeros((1,), jnp.int32))

    def qk(weight, rows):
        size = weight.shape[1] // 3
        return jnp.concatenate(
            [
                pad_to(weight[:, :size], rows, lanes),
                pad_to(weight[:, size : 2 * size], rows, lanes),
            ],
            axis=1,
        )

    def proj(weight):
        split = weight.reshape(heads // 2, 2, channels // heads, channels)
        split = jnp.pad(split, ((0, 0), (0, 0), (0, HEAD_ROWS - channels // heads), (0, 0)))
        split = split.transpose(1, 0, 2, 3).reshape(2, heads // 2 * HEAD_ROWS, channels)
        return pad_to(split, 2, LANES, lanes).reshape(2 * LANES, lanes)

    blocks = []
    for i in range(2):
        blocks.append(
            (
                qk(qkv_weight[i], lanes),
                pad_to(
                    head_rows(qkv_weight[i][:, 2 * channels :], heads), heads * HEAD_ROWS, lanes
                ),
                proj(proj_weight[i]),
                pad_to(up_weight[i], lanes, hidden),
                pad_to(down_weight[i], hidden, lanes),
            )
        )
    recon = variant_recon(recon_weight, codes, lanes, lanes)

    whole = lambda a: pl.BlockSpec(a.shape, lambda *i: (0,) * a.ndim)
    params = pltpu.CompilerParams(
        dimension_semantics=("arbitrary",), vmem_limit_bytes=56 * 1024 * 1024
    )
    y1 = pl.pallas_call(
        functools.partial(first_kernel, heads, channels),
        grid=(height // WIN,),
        in_specs=[
            pl.BlockSpec((WIN, breadth, lanes), lambda i: (i, 0, 0)),
            whole(rows),
            *[whole(w) for w in blocks[0]],
        ],
        out_specs=pl.BlockSpec((VAR_DEV, WIN, breadth, lanes), lambda i: (0, i, 0, 0)),
        out_shape=jax.ShapeDtypeStruct((VAR_DEV, height, breadth, lanes), jnp.bfloat16),
        scratch_shapes=[pltpu.VMEM((VAR_DEV, CELLS, heads * CELLS), jnp.float32)],
        compiler_params=params,
        name="block_one",
    )(x, rows, *blocks[0])

    top = shifted(y1[:, height - SHIFT :], "ty", 1)
    bottom = shifted(y1[:, :SHIFT], "ty", -1)
    sides = []
    for cut, step in ((slice(breadth - SHIFT, breadth), 1), (slice(0, SHIFT), -1)):
        strip = jnp.concatenate([top[:, :, cut], y1[:, :, cut], bottom[:, :, cut]], axis=1)
        sides.append(shifted(strip.reshape(VAR_DEV, -1, lanes), "tx", step))

    operands = (y1, top, bottom, *sides, rows, *blocks[1], recon)
    partial = pl.pallas_call(
        functools.partial(second_kernel, heads, channels),
        grid=((height + 2 * SHIFT) // WIN,),
        in_specs=[whole(a) for a in operands],
        out_specs=pl.BlockSpec(
            (height // WIN, out_channels, WIN * breadth), lambda i: (0, 0, 0)
        ),
        out_shape=jax.ShapeDtypeStruct(
            (height // WIN, out_channels, WIN * breadth), jnp.bfloat16
        ),
        scratch_shapes=[
            pltpu.VMEM((VAR_DEV, height + 2 * SHIFT, breadth + 2 * SHIFT, lanes), jnp.float32),
            pltpu.VMEM((VAR_DEV, CELLS, heads * CELLS), jnp.float32),
            pltpu.VMEM((height + 2 * SHIFT + WIN, breadth + 2 * SHIFT, lanes), jnp.float32),
        ],
        compiler_params=params,
        name="block_two",
    )(*operands)

    sharers = lax.axis_size("var")
    strips = height // WIN // sharers
    parts = lax.all_to_all(
        partial.reshape(sharers, strips, out_channels, WIN * breadth), "var", 0, 0
    )
    part_x = lax.dynamic_slice_in_dim(
        x, lax.axis_index("var") * strips * WIN, strips * WIN, axis=0
    )
    w_qk = qk(refine_qkv, LANES)
    w_vt = head_rows(refine_qkv[:, 2 * out_channels :], refine_heads)
    w_projt = refine_proj.T.reshape(out_channels, refine_heads, out_channels // refine_heads)
    w_projt = pad_to(w_projt, out_channels, refine_heads, HEAD_ROWS)
    w_projt = w_projt.transpose(1, 0, 2).reshape(refine_heads * out_channels, HEAD_ROWS)
    colours = out_channels // (SCALE * SCALE)
    final = (colours, strips * WIN * SCALE, breadth * SCALE)
    operands = (parts, part_x, refine_rows, w_qk, w_vt, w_projt)
    strip = pl.pallas_call(
        functools.partial(third_kernel, refine_heads),
        grid=(1,),
        in_specs=[whole(a) for a in operands],
        out_specs=pl.BlockSpec(final, lambda i: (0, 0, 0)),
        out_shape=jax.ShapeDtypeStruct(final, jnp.bfloat16),
        scratch_shapes=[
            pltpu.VMEM((1, CELLS, refine_heads * CELLS), jnp.float32),
            pltpu.VMEM(final, jnp.float32),
        ],
        compiler_params=params,
        name="refinement",
    )(*operands)
    gathered = lax.all_gather(strip, "var", axis=0)
    picture = gathered.transpose(1, 0, 2, 3).reshape(colours, height * SCALE, breadth * SCALE)
    return picture.astype(jnp.float32)


def solution(mesh):
    placed = (P("ty", "tx", None), P("ty", "tx"), P(), P(), P(), P(), P(), P(), P(), P(), P())
    return jax.shard_map(
        local, mesh=mesh, in_specs=placed, out_specs=P(None, "ty", "tx"), check_vma=False
    )
```

```python
import functools

import jax
import jax.numpy as jnp
from jax import lax
from jax.experimental import pallas as pl
from jax.experimental.pallas import tpu as pltpu
from jax.sharding import PartitionSpec as P

WIN = 8
CELLS = WIN * WIN
SHIFT = 4
SCALE = 4
VAR_DEV = 2
LANES = 128
HEAD_ROWS = 32
CLASSES = 4
MARKS = CLASSES + 2
SIDE = 2 * WIN - 1

EPSILON = 1e-05
LOG2E = 1.4426950408889634
BIG = float(2.0**100)
ERF_TANH = (
    7.97884207935252e-01,
    3.63342879e-02,
    -3.31288562e-05,
    -5.52410746e-05,
    3.96927395e-06,
    -1.33457816e-07,
    1.80588519e-09,
)

NN = (((1,), (0,)), ((), ()))
NT = (((1,), (1,)), ((), ()))
F32 = jnp.float32
BF16 = jnp.bfloat16


def dot(a, b, dims=NN):
    return lax.dot_general(a, b, dims, preferred_element_type=F32)


def iota(shape, dim):
    return lax.broadcasted_iota(jnp.int32, shape, dim)


def round_up(size, multiple):
    return -(-size // multiple) * multiple


def one_hot(condition):
    return jnp.where(condition, 1.0, 0.0).astype(BF16)


def exact(a, b, dims=NN):
    return dot(a, b, dims).astype(BF16)


def pad_matrix(rows, size):
    return one_hot(iota((rows, size), 0) == iota((rows, size), 1))


def head_matrix(rows, size, heads, width, first=0):
    row = iota((rows, size), 0)
    unit = row % HEAD_ROWS
    source = first + row // HEAD_ROWS * width + unit
    keep = (unit < width) & (row < heads * HEAD_ROWS)
    return one_hot(keep & (iota((rows, size), 1) == source))


def query_labels(rows, lanes, first_row, first_lane):
    row = iota((rows, lanes), 0) - first_row
    lane = iota((rows, lanes), 1) - first_lane
    is_class = (row >= 0) & (row < CLASSES)
    is_pad = row == CLASSES
    same = is_class & (row == lane)
    always = lane == CLASSES + 1
    return jnp.where(same, BIG, 0.0) - jnp.where(always & (is_class | is_pad), BIG, 0.0)


def key_labels(rows, lanes, first_row, first_lane):
    row = iota((rows, lanes), 0) - first_row
    lane = iota((rows, lanes), 1) - first_lane
    is_class = (lane >= 0) & (lane < CLASSES)
    is_pad = lane == CLASSES
    add = is_class & (row == lane) | is_pad & (row == CLASSES + 1)
    return jnp.where(add, 1.0, 0.0) - jnp.where(is_pad & (row == CLASSES), 1.0, 0.0)


def bias_rows(table, turn, flip_rows, flip_cols):
    shape = (1, WIN * LANES)
    lane = iota(shape, 1)
    row_step = lane % LANES // WIN - (WIN - 1)
    col_step = lane % WIN - lane // LANES
    row_step = jnp.where(flip_rows, -row_step, row_step)
    col_step = jnp.where(flip_cols, -col_step, col_step)
    lead = jnp.where(turn, col_step, row_step)
    trail = jnp.where(turn, row_step, col_step)
    index = (lead + WIN - 1) * SIDE + trail + WIN - 1
    pick = one_hot(iota((table.shape[1], WIN * LANES), 0) == index)
    rest = table * LOG2E
    parts = []
    for _ in range(3):
        parts.append(rest.astype(BF16))
        rest = rest - parts[-1].astype(F32)
    moved = dot(jnp.concatenate(parts, axis=0), pick)
    size = table.shape[0]
    return moved[:size] + moved[size : 2 * size] + moved[2 * size :]


def bias_grid(rows, rows_ref, store):
    heads = rows.shape[0]
    for key_col in range(WIN):
        rows_ref[0:heads, key_col, :] = rows[:, key_col * LANES : (key_col + 1) * LANES]
    half = iota((WIN, LANES), 1)
    for pair in range(heads // 2):
        even, odd = rows_ref[2 * pair], rows_ref[2 * pair + 1]
        for key_row in range(WIN):
            start = (WIN - 1 - key_row) * WIN
            left = pltpu.roll(even, (LANES - start) % LANES, 1)
            right = pltpu.roll(odd, (LANES - start + CELLS) % LANES, 1)
            store(key_row, pair, jnp.where(half < CELLS, left, right))


def prepare_kernel(
    heads,
    channels,
    codes_ref,
    packed_ref,
    swin_bias_ref,
    recon_ref,
    refine_qkv_ref,
    refine_proj_ref,
    refine_bias_ref,
    qvt_out,
    key_out,
    proj_out,
    up_out,
    down_out,
    recon_out,
    bias_out,
    refine_qvt_out,
    refine_key_out,
    refine_proj_out,
    refine_bias_out,
    rows_ref,
    tables_ref,
):
    blocks = packed_ref.shape[0]
    width = channels // heads
    lanes = key_out.shape[1]
    hidden = up_out.shape[2]
    head_rows = heads * HEAD_ROWS
    mark_rows = head_rows + 16
    picked = head_matrix(lanes, lanes, heads, width)
    shape = (2 * LANES, lanes)
    row = iota(shape, 0)
    head, unit = row % LANES // HEAD_ROWS * 2 + row // LANES, row % HEAD_ROWS
    proj_rows = one_hot((head < heads) & (unit < width) & (iota(shape, 1) == head * width + unit))
    identity = one_hot(iota((hidden, hidden), 0) == iota((hidden, hidden), 1))
    query_add = query_labels(mark_rows, lanes, head_rows, channels)
    key_add = key_labels(lanes, lanes, channels, head_rows)
    for i in range(blocks):
        at = [0]

        def piece(size):
            at[0] += size
            return packed_ref[i, :, at[0] - size : at[0]]

        query, key, value, proj = (piece(lanes) for _ in range(4))
        qvt_out[i, :mark_rows] = (dot(picked[:mark_rows], query, NT) + query_add).astype(BF16)
        qvt_out[i, mark_rows:] = exact(picked[:head_rows], value, NT)
        key_out[i] = (dot(key, picked, NT) + key_add).astype(BF16)
        proj_out[i] = exact(proj_rows, proj)
        up_out[i] = piece(hidden)
        down_out[i] = exact(identity, piece(hidden), NT)

    taps, out, _ = recon_ref.shape
    kernel = recon_ref[...].reshape(taps * out, channels)
    pad = one_hot(iota((lanes, channels), 0) == iota((lanes, channels), 1))
    for i in range(blocks):
        tables_ref[i * heads : (i + 1) * heads] = swin_bias_ref[:, i]
    for v in range(VAR_DEV):
        code = codes_ref[v]
        turn, flip_rows, flip_cols = code // 4 == 1, code // 2 % 2 == 1, code % 2 == 1
        rows = bias_rows(tables_ref[: blocks * heads], turn, flip_rows, flip_cols)
        tables = [rows[i * heads : (i + 1) * heads] for i in range(blocks)]
        for i in range(blocks):

            def store(key_row, pair, value):
                bias_out[
                    i,
                    v,
                    key_row * WIN : (key_row + 1) * WIN,
                    pair * LANES : (pair + 1) * LANES,
                ] = value

            bias_grid(tables[i], rows_ref, store)
        shape = (3 * lanes, 1)
        row = iota(shape, 0)
        row_step = row // lanes - 1
        lane = row % lanes
        col_step = jnp.where(lane >= LANES, 1, jnp.where(lane >= out, 0, -1))
        channel = jnp.where(lane >= LANES, lane - LANES, jnp.where(lane >= out, lane - out, lane))
        row_step = jnp.where(flip_rows, -row_step, row_step)
        col_step = jnp.where(flip_cols, -col_step, col_step)
        tap = (jnp.where(turn, col_step, row_step) + 1) * 3
        tap = tap + jnp.where(turn, row_step, col_step) + 1
        sub_row = channel % (SCALE * SCALE) // SCALE
        sub_col = channel % SCALE
        sub_row = jnp.where(flip_rows, SCALE - 1 - sub_row, sub_row)
        sub_col = jnp.where(flip_cols, SCALE - 1 - sub_col, sub_col)
        source = channel // (SCALE * SCALE) * SCALE * SCALE
        source = source + jnp.where(turn, sub_col, sub_row) * SCALE
        source = tap * out + source + jnp.where(turn, sub_row, sub_col)
        source = jnp.where(channel < out, source, -1)
        moved = exact(one_hot(iota((3 * lanes, taps * out), 1) == source), kernel)
        recon_out[v] = exact(pad, moved, NT)

    refine_heads = refine_bias_ref.shape[0]
    refine_width = out // refine_heads
    never = codes_ref[0] < 0
    rows = bias_rows(refine_bias_ref[...], never, never, never)

    def store_refine(key_row, pair, value):
        refine_bias_out[key_row * WIN : (key_row + 1) * WIN] = value

    bias_grid(rows, rows_ref, store_refine)
    refine_rows = refine_heads * HEAD_ROWS
    values = head_matrix(refine_rows, 3 * out, refine_heads, refine_width, 2 * out)
    queries = head_matrix(refine_rows + 16, 3 * out, refine_heads, refine_width)
    keys = head_matrix(LANES, 3 * out, refine_heads, refine_width, out)
    out_pad = one_hot(iota((LANES, out), 0) == iota((LANES, out), 1))
    weight = refine_qkv_ref[...]
    mark = channels % LANES
    refine_qvt_out[: refine_rows + 16] = (
        dot(exact(queries, weight, NT), out_pad, NT)
        + query_labels(refine_rows + 16, LANES, refine_rows, mark)
    ).astype(BF16)
    refine_qvt_out[refine_rows + 16 :] = exact(exact(values, weight, NT), out_pad, NT)
    refine_key_out[...] = (
        dot(out_pad, exact(keys, weight, NT), NT) + key_labels(LANES, LANES, mark, refine_rows)
    ).astype(BF16)
    for h in range(refine_heads):
        shape = (LANES, out)
        row = iota(shape, 0)
        rows = one_hot((row < refine_width) & (iota(shape, 1) == row + h * refine_width))
        square = dot(exact(rows, refine_proj_ref[...]), out_pad, NT)
        refine_proj_out[h * out : (h + 1) * out] = square.T[:out].astype(BF16)


def gelu(x):
    square = x * x
    series = jnp.full_like(square, ERF_TANH[-1])
    for factor in ERF_TANH[-2::-1]:
        series = series * square + factor
    half = 0.5 * x
    return half + half * jnp.tanh(x * series)


def normalize(x, channels):
    inside = iota((1, x.shape[1]), 1) < channels
    mean = jnp.sum(jnp.where(inside, x, 0.0), axis=1, keepdims=True) * (1.0 / channels)
    centred = jnp.where(inside, x - mean, 0.0)
    spread = jnp.sum(centred * centred, axis=1, keepdims=True) * (1.0 / channels)
    return jnp.where(inside, centred * lax.rsqrt(spread + EPSILON), x).astype(BF16)


def split_queries(queries, heads):
    pairs = heads // 2
    head_rows = heads * HEAD_ROWS
    left = iota((1, LANES), 1) < CELLS
    turned = pltpu.roll(queries, CELLS, 1).astype(BF16)
    queries = queries.astype(BF16)
    depth = round_up(queries.shape[0], LANES)
    zero = jnp.zeros((HEAD_ROWS, LANES), BF16)
    results = []
    for even, odd in ((queries, turned), (turned, queries)):
        marks = jnp.where(left, even[head_rows:], odd[head_rows:])
        columns = []
        for pair in range(pairs):
            at = pair * 2 * HEAD_ROWS
            rows = [zero] * heads
            rows[2 * pair] = jnp.where(left, even[at : at + HEAD_ROWS], zero)
            rows[2 * pair + 1] = jnp.where(left, zero, odd[at + HEAD_ROWS : at + 2 * HEAD_ROWS])
            rows.append(marks)
            rows.append(jnp.zeros((depth - queries.shape[0], LANES), BF16))
            columns.append(jnp.concatenate(rows, axis=0))
        results.append(jnp.concatenate(columns, axis=1) if pairs > 1 else columns[0])
    return results


def heads_of(n, scale, heads, width, w_qvt, w_key):
    mark_rows = heads * HEAD_ROWS + 16
    both = dot(w_qvt, n, NT)
    row = iota((mark_rows, 1), 0)
    queries = both[:mark_rows] * jnp.where(row < heads * HEAD_ROWS, scale, 1.0)
    values = both[mark_rows:]
    row = iota((heads * HEAD_ROWS, 1), 0) % HEAD_ROWS
    values = jnp.where(row == width, 1.0, values).astype(BF16)
    keys = dot(n, w_key).astype(BF16)
    scores = []
    for place in range(n.shape[0] // LANES):
        cut = slice(place * LANES, (place + 1) * LANES)
        for half, stationary in enumerate(split_queries(queries[:, cut], heads)):
            at = place * LANES + half * CELLS
            scores.append(dot(keys[at : at + CELLS], stationary))
    return scores, values


def soft(scores):
    largest = jnp.max(scores, axis=0, keepdims=True)
    return jnp.exp2(scores - largest).astype(BF16)


def mix_pair(values, first, second, heads, ones_row):
    zero = jnp.zeros((CELLS, LANES), BF16)
    lane = iota((HEAD_ROWS, 2 * LANES), 1) % LANES
    mixed = []
    for pair in range(heads // 2):
        cut = slice(pair * LANES, (pair + 1) * LANES)
        stationary = jnp.concatenate(
            [
                jnp.concatenate([first[:, cut], zero], axis=1),
                jnp.concatenate([zero, second[:, cut]], axis=1),
            ],
            axis=0,
        )
        result = dot(values[pair * CELLS : (pair + 1) * CELLS], stationary)
        joined = jnp.where(lane < CELLS, result[:HEAD_ROWS], result[HEAD_ROWS:])
        mixed.append(joined * pl.reciprocal(joined[ones_row : ones_row + 1]))
    return mixed


def swin_block(x, pairs, heads, channels, bias, w_qvt, w_key, w_proj, w_up, w_down):
    width = channels // heads
    n = normalize(x, channels)
    scale = width**-0.5 * LOG2E
    scores, values = heads_of(n, scale, heads, width, w_qvt[...], w_key[...])
    pad = jnp.zeros((LANES - heads // 2 * HEAD_ROWS, 2 * LANES), F32)
    weights = [
        (soft(scores[2 * place] + bias(a)), soft(scores[2 * place + 1] + bias(b)))
        for place, a, b in pairs
    ]
    blocks = []
    for (place, _, _), (first, second) in zip(pairs, weights):
        cut = slice(place * LANES, (place + 1) * LANES)
        mixed = mix_pair(values[:, cut], first, second, heads, width)
        blocks.append(jnp.concatenate(mixed + [pad], axis=0).astype(BF16))
    outputs = []
    for block in blocks:
        for half in range(2):
            turned = block[:, half * LANES : (half + 1) * LANES].T
            outputs.append(jnp.concatenate([turned[:CELLS], turned[CELLS:]], axis=1))
    outputs = jnp.concatenate(outputs, axis=0)
    places = [place for place, _, _ in pairs]
    if places != list(range(x.shape[0] // LANES)):
        x = jnp.concatenate([x[place * LANES : (place + 1) * LANES] for place in places], axis=0)
    h = (x + dot(outputs, w_proj[...])).astype(BF16).astype(F32)
    hidden = gelu(dot(normalize(h, channels), w_up[...])).astype(BF16)
    y = h + dot(hidden, w_down[...])
    return [y[i * LANES : (i + 1) * LANES] for i in range(len(pairs))]


def windows_of(grid):
    lanes = grid.shape[2]
    return jnp.concatenate(
        [
            grid[:, w * WIN : (w + 1) * WIN].reshape(CELLS, lanes)
            for w in range(grid.shape[1] // WIN)
        ],
        axis=0,
    )


def first_kernel(
    heads, channels, ends, xa_ref, xb_ref, labels_ref, bias_ref, *refs
):
    *weights, y_ref, left_ref, right_ref = refs[:8]
    held, side = refs[-2:]
    step = pl.program_id(0)
    breadth = xa_ref.shape[1]
    count = breadth // WIN
    tokens, lanes = held.shape
    part = tokens // 2
    rows_total = labels_ref.shape[1]
    strips = (0, rows_total // WIN - 1) if ends else (2 * step + 1, 2 * step + 2)
    for k, ref in enumerate((xa_ref, xb_ref)):
        held[k * part : (k + 1) * part, :channels] = windows_of(ref[...].astype(F32))
    token = iota((tokens, rows_total), 0)
    strip = jnp.where(token < part, strips[0], strips[1])
    at_row = strip * WIN + token % CELLS // WIN == iota((tokens, rows_total), 1)
    by_row = dot(one_hot(at_row), labels_ref[...].astype(F32).astype(BF16), NT)
    token = iota((tokens, breadth), 0)
    at_col = token % part // CELLS * WIN + token % WIN == iota((tokens, breadth), 1)
    label = dot(jnp.where(at_col, by_row, 0.0).astype(BF16), jnp.ones((breadth, LANES), BF16))
    lane = iota((tokens, LANES), 1) - channels % LANES
    marks = jnp.where(
        (label == (lane + 1).astype(F32)) & (lane < CLASSES)
        | (lane >= CLASSES) & (lane < MARKS),
        1.0,
        0.0,
    )
    tail = jnp.where(lane < 0, held[:, lanes - LANES :], marks)
    x = jnp.concatenate([held[:, : lanes - LANES], tail], axis=1)
    places = tokens // LANES
    pairs = [(place, v, v) for v in range(VAR_DEV) for place in range(places)]
    results = swin_block(x, pairs, heads, channels, lambda v: bias_ref[v], *weights)
    for v in range(VAR_DEV):
        for k in range(2):
            windows = []
            for w in range(count):
                group = k * count + w
                block = results[v * places + group // 2]
                at = group % 2 * CELLS
                windows.append(block[at : at + CELLS].reshape(WIN, WIN, lanes))
            y_ref[v, k * WIN : (k + 1) * WIN] = jnp.concatenate(windows, axis=1).astype(BF16)
            at = k * WIN * SHIFT
            for r in range(WIN):
                rows = slice(at + r * SHIFT, at + (r + 1) * SHIFT)
                side[0, rows] = windows[0][r, :SHIFT]
                side[1, rows] = windows[-1][r, SHIFT:]
        left_ref[v] = side[0].astype(BF16)
        right_ref[v] = side[1].astype(BF16)
    if ends:
        top_ref, bottom_ref = refs[8:10]
        top_ref[...] = y_ref[:, :SHIFT]
        bottom_ref[...] = y_ref[:, 2 * WIN - SHIFT :]


def place_rows(store, ends_ref, middle_ref, v):
    store(0, ends_ref[v, :WIN])
    for r in range(0, middle_ref.shape[1], WIN):
        store(WIN + r, middle_ref[v, r : r + WIN])
    store(WIN + middle_ref.shape[1], ends_ref[v, WIN:])


def inner_kernel(
    heads, channels, group, ends_ref, middle_ref, bias_ref, *refs
):
    *weights, y_ref, marks_ref, held, x_held = refs
    height, breadth, lanes = held.shape
    count = breadth // WIN - 1

    @pl.when(pl.program_id(0) == 0)
    def _():
        for v in range(VAR_DEV):

            def store(first, rows):
                rows = rows.astype(F32)
                held[first : first + WIN] = rows
                if v == 0:
                    marks_ref[first // WIN] = windows_of(rows[:, :, lanes - LANES :]).astype(BF16)

            place_rows(store, ends_ref, middle_ref, v)
            for strip in range(height // WIN - 1):
                rows = slice(strip * WIN + SHIFT, (strip + 1) * WIN + SHIFT)
                for w in range(count):
                    at = SHIFT + w * WIN
                    x_held[strip * count + w, v] = held[rows, at : at + WIN].reshape(CELLS, lanes)

    base = pl.program_id(0) * group
    x = x_held[pl.ds(base, group)].reshape(group * VAR_DEV * CELLS, lanes)
    pairs = [(w, 0, 1) for w in range(group)]
    results = swin_block(x, pairs, heads, channels, lambda v: bias_ref[v], *weights)
    for w in range(group):
        y_ref[w] = results[w].astype(BF16).reshape(VAR_DEV, CELLS, lanes)


def outer_kernel(
    heads,
    channels,
    group,
    ends_ref,
    middle_ref,
    top_ref,
    bottom_ref,
    left_ref,
    right_ref,
    inner_ref,
    bias_ref,
    *refs,
):
    *weights, w_recon, out_ref, rows_held, sides_held, x_held, y_held, acc = refs
    lanes = middle_ref.shape[3]
    height, breadth = middle_ref.shape[1] + 2 * WIN, middle_ref.shape[2]
    tall, wide = height + 2 * SHIFT, breadth + 2 * SHIFT
    strips, count = tall // WIN, wide // WIN
    always = iota((1, lanes), 1) == channels + CLASSES + 1

    def marked(received):
        return jnp.where(always, 1.0, received.astype(F32))

    for v in range(VAR_DEV):
        for end in range(2):
            outside, inside = (0, SHIFT) if end == 0 else (SHIFT, 0)
            corner = 0 if end == 0 else (tall - SHIFT) * SHIFT
            received = top_ref if end == 0 else bottom_ref
            first = 0 if end == 0 else 2 * WIN - SHIFT
            across = slice(SHIFT, SHIFT + breadth)
            rows_held[outside : outside + SHIFT, across] = marked(received[v])
            rows_held[inside : inside + SHIFT, across] = ends_ref[
                v, first : first + SHIFT
            ].astype(F32)
            side_first = SHIFT * SHIFT if end == 0 else (tall - 2 * SHIFT) * SHIFT
            for ref, at in ((left_ref, 0), (right_ref, wide - SHIFT)):
                for rows, start in ((outside, corner), (inside, side_first)):
                    piece = marked(ref[v, start : start + SHIFT * SHIFT])
                    rows_held[rows : rows + SHIFT, at : at + SHIFT] = piece.reshape(
                        SHIFT, SHIFT, lanes
                    )
            for w in range(count):
                x_held[end * count + w, v] = rows_held[:, w * WIN : (w + 1) * WIN].reshape(
                    CELLS, lanes
                )

        def store(first, rows):
            sides_held[first : first + WIN, :WIN] = rows[:, :WIN].astype(F32)
            sides_held[first : first + WIN, WIN:] = rows[:, breadth - WIN :].astype(F32)

        place_rows(store, ends_ref, middle_ref, v)
        for strip in range(1, strips - 1):
            rows = slice(strip * WIN - SHIFT, (strip + 1) * WIN - SHIFT)
            cut = slice(strip * WIN * SHIFT, (strip + 1) * WIN * SHIFT)
            for end in range(2):
                ref = left_ref if end == 0 else right_ref
                piece = marked(ref[v, cut]).reshape(WIN, SHIFT, lanes)
                at = 0 if end == 0 else WIN + SHIFT
                own = sides_held[rows, at : at + SHIFT]
                both = [piece, own] if end == 0 else [own, piece]
                slot = 2 * count + 2 * (strip - 1) + end
                x_held[slot, v] = jnp.concatenate(both, axis=1).reshape(CELLS, lanes)

    slots = x_held.shape[0]

    def border(step, carry):
        x = x_held[pl.ds(step * group, group)].reshape(group * VAR_DEV * CELLS, lanes)
        pairs = [(w, 0, 1) for w in range(group)]
        results = swin_block(x, pairs, heads, channels, lambda v: bias_ref[v], *weights)
        at = channels + CLASSES
        for w in range(group):
            block = x[w * LANES : (w + 1) * LANES]
            y = results[w] * block[:, at : at + 1]
            y_held[step * group + w] = y.astype(BF16).reshape(VAR_DEV, CELLS, lanes)
        return carry

    lax.fori_loop(0, slots // group, border, 0)

    acc[...] = jnp.zeros_like(acc)

    def scatter(strip, windows):
        total = None
        for v in range(VAR_DEV):
            part = dot(jnp.concatenate(windows(v), axis=0), w_recon[v])
            total = part if total is None else total + part
        total = total.reshape(count, WIN, WIN, 3 * lanes)
        for e in range(3):
            for w in range(count):
                acc[pl.ds(strip * WIN + 2 - e, WIN), w * WIN : (w + 1) * WIN] += total[
                    w, :, :, e * lanes : (e + 1) * lanes
                ]

    def middle(strip, carry):
        slot = 2 * count + 2 * (strip - 1)
        first = (strip - 1) * (count - 2)
        scatter(
            strip,
            lambda v: [
                y_held[slot, v],
                *[inner_ref[first + w, v] for w in range(count - 2)],
                y_held[slot + 1, v],
            ],
        )
        return carry

    scatter(0, lambda v: [y_held[w, v] for w in range(count)])
    lax.fori_loop(1, strips - 1, middle, 0)
    scatter(strips - 1, lambda v: [y_held[count + w, v] for w in range(count)])

    out_channels = out_ref.shape[1]

    def finish(strip, carry):
        rows = pl.ds(1 + SHIFT + strip * WIN, WIN)
        centre = acc[rows, SHIFT : SHIFT + breadth, :LANES]
        centre = pltpu.roll(centre.reshape(WIN * breadth, LANES), LANES - out_channels, 1)
        result = (
            acc[rows, SHIFT - 1 : SHIFT - 1 + breadth, :LANES]
            + centre.reshape(WIN, breadth, LANES)
            + acc[rows, SHIFT + 1 : SHIFT + 1 + breadth, LANES : 2 * LANES]
        )
        out_ref[strip] = windows_of(result).T[:out_channels].astype(BF16)
        return carry

    lax.fori_loop(0, height // WIN, finish, 0)


def refine_kernel(
    heads, first_mark, place_ref, parts_ref, marks_ref, bias_ref, w_qvt, w_key, w_projt, out_ref, final
):
    sources, strips, channels, strip_tokens = parts_ref.shape
    breadth = strip_tokens // WIN
    width = channels // heads
    z = jnp.concatenate(
        [
            sum(parts_ref[s, strip].astype(F32) for s in range(sources))
            for strip in range(strips)
        ],
        axis=1,
    ) * (1.0 / (sources * VAR_DEV))
    mean = jnp.sum(z, axis=0, keepdims=True) * (1.0 / channels)
    centred = z - mean
    spread = jnp.sum(centred * centred, axis=0, keepdims=True) * (1.0 / channels)
    normed = centred * lax.rsqrt(spread + EPSILON)
    tall = jnp.concatenate([normed, jnp.zeros((LANES - channels, normed.shape[1]), F32)], axis=0)
    marks = jnp.concatenate([marks_ref[s].astype(F32) for s in range(strips)], axis=0)
    lane = iota((1, LANES), 1)
    is_mark = (lane >= first_mark) & (lane < first_mark + MARKS)
    n = jnp.where(is_mark, marks, tall.T).astype(BF16)
    scores, values = heads_of(
        n, width**-0.5 * LOG2E, heads, width, w_qvt[...], w_key[...]
    )
    probabilities = [soft(s + bias_ref[...]) for s in scores]
    lane = iota((channels, LANES), 1)
    branches = []
    for pair in range(len(probabilities) // 2):
        mixed = mix_pair(
            values[:, pair * LANES : (pair + 1) * LANES],
            probabilities[2 * pair],
            probabilities[2 * pair + 1],
            heads,
            width,
        )[0].astype(BF16)
        both = dot(w_projt[...][:, :HEAD_ROWS], mixed)
        even, odd = both[:channels], both[channels:]
        halves = []
        for half in range(2):
            cut = slice(half * LANES, (half + 1) * LANES)
            halves.append(even[:, cut] + pltpu.roll(odd[:, cut], CELLS, 1))
        branches.append(jnp.where(lane < CELLS, halves[0], pltpu.roll(halves[1], CELLS, 1)))
    refined = (z + jnp.concatenate(branches, axis=1)).astype(BF16)
    stacked = jnp.concatenate(
        [refined[:, s * strip_tokens : (s + 1) * strip_tokens] for s in range(strips)], axis=0
    )
    shape = (strip_tokens, WIN * breadth * SCALE)
    cell = iota(shape, 1) // SCALE
    source = (cell % breadth // WIN) * CELLS + (cell // breadth) * WIN + cell % WIN
    wide = dot(stacked, one_hot(iota(shape, 0) == source))
    own = iota(wide.shape, 1) % SCALE == iota(wide.shape, 0) % SCALE
    wide = jnp.where(own, wide, 0.0).astype(BF16)
    shape = (wide.shape[0] // SCALE, wide.shape[0])
    folded = dot(one_hot(iota(shape, 1) // SCALE == iota(shape, 0)), wide)
    colours = channels // (SCALE * SCALE)
    row_lanes = breadth * SCALE
    for s in range(strips):
        for c in range(colours):
            first = (s * colours + c) * SCALE
            for y in range(WIN):
                start = (s * WIN + y) * SCALE
                final[c, start : start + SCALE] = folded[
                    first : first + SCALE, y * row_lanes : (y + 1) * row_lanes
                ]
    out_ref[...] = final[...].astype(BF16)


def exchanged(last, first, axis):
    count = lax.axis_size(axis)
    up = [(i, i + 1) for i in range(count - 1)]
    down = [(i + 1, i) for i in range(count - 1)]
    if count != 2:
        return lax.ppermute(last, axis, up), lax.ppermute(first, axis, down)
    at_start = lax.axis_index(axis) == 0
    received = lax.ppermute(jnp.where(at_start, last, first), axis, up + down)
    zero = jnp.zeros_like(received)
    return jnp.where(at_start, zero, received), jnp.where(at_start, received, zero)


def whole(a):
    return pl.BlockSpec(a.shape, lambda *i: (0,) * a.ndim)


def params():
    return pltpu.CompilerParams(
        dimension_semantics=("arbitrary",), vmem_limit_bytes=56 * 1024 * 1024
    )


def local(
    features,
    labels,
    qkv_weight,
    proj_weight,
    up_weight,
    down_weight,
    swin_bias,
    recon_weight,
    refine_qkv,
    refine_proj,
    refine_bias,
):
    height, breadth, channels = features.shape
    heads = swin_bias.shape[1]
    out_channels = recon_weight.shape[-1]
    refine_heads = refine_bias.shape[0]
    lanes = round_up(channels + MARKS, LANES)
    hidden = round_up(up_weight.shape[-1], LANES)
    position = lax.axis_index("var")
    codes = position * VAR_DEV + jnp.arange(VAR_DEV, dtype=jnp.int32)

    def widen(weight, size):
        return jnp.pad(weight, ((0, 0), (0, lanes - channels), (0, size - weight.shape[2])))

    packed = jnp.concatenate(
        [
            *[
                widen(qkv_weight[:, :, i * channels : (i + 1) * channels], lanes)
                for i in range(3)
            ],
            widen(proj_weight, lanes),
            widen(up_weight, hidden),
            widen(jnp.swapaxes(down_weight, 1, 2), hidden),
        ],
        axis=2,
    )
    operands = (
        codes,
        packed,
        jnp.swapaxes(swin_bias, 0, 1),
        jnp.swapaxes(recon_weight, 1, 2),
        refine_qkv,
        refine_proj,
        refine_bias,
    )
    head_rows, refine_rows = heads * HEAD_ROWS, refine_heads * HEAD_ROWS
    shapes = [
        ((2, 2 * head_rows + 16, lanes), BF16),
        ((2, lanes, lanes), BF16),
        ((2, 2 * LANES, lanes), BF16),
        ((2, lanes, hidden), BF16),
        ((2, hidden, lanes), BF16),
        ((VAR_DEV, lanes, 3 * lanes), BF16),
        ((2, VAR_DEV, CELLS, heads * CELLS), F32),
        ((2 * refine_rows + 16, LANES), BF16),
        ((LANES, LANES), BF16),
        ((refine_heads * out_channels, LANES), BF16),
        ((CELLS, refine_heads * CELLS), F32),
    ]
    shapes = [jax.ShapeDtypeStruct(*s) for s in shapes]
    prepared = pl.pallas_call(
        functools.partial(prepare_kernel, heads, channels),
        grid=(1,),
        in_specs=[pl.BlockSpec(memory_space=pltpu.SMEM)] + [whole(a) for a in operands[1:]],
        out_specs=[whole(s) for s in shapes],
        out_shape=shapes,
        scratch_shapes=[
            pltpu.VMEM((heads, WIN, LANES), F32),
            pltpu.VMEM((round_up(2 * heads, 8), swin_bias.shape[2]), F32),
        ],
        compiler_params=params(),
        name="prepare",
    )(*operands)
    *swin, recon, bias, refine_qvt, refine_key, refine_projt, refine_grid = prepared

    def block_specs(i):
        arrays = (bias, *swin)
        return arrays, [
            pl.BlockSpec((None,) + a.shape[1:], lambda *_, n=a.ndim: (i,) + (0,) * (n - 1))
            for a in arrays
        ]

    def cost(windows):
        return pl.CostEstimate(
            flops=windows * 400_000_000, bytes_accessed=windows * 200_000, transcendentals=0
        )

    arrays, specs = block_specs(0)
    strips = height // WIN
    tokens = WIN * breadth
    side_rows = 2 * WIN * SHIFT
    labels_across = labels.T

    def block_one(ends):
        steps = 1 if ends else strips // 2 - 1
        first = (lambda i: 0) if ends else (lambda i: 2 * i + 1)
        second = (lambda i: strips - 1) if ends else (lambda i: 2 * i + 2)
        outs = [
            ((VAR_DEV, steps * 2 * WIN, breadth, lanes), BF16),
            ((VAR_DEV, steps * side_rows, lanes), BF16),
            ((VAR_DEV, steps * side_rows, lanes), BF16),
        ]
        out_specs = [
            pl.BlockSpec((VAR_DEV, 2 * WIN, breadth, lanes), lambda i: (0, i, 0, 0)),
            pl.BlockSpec((VAR_DEV, side_rows, lanes), lambda i: (0, i, 0)),
            pl.BlockSpec((VAR_DEV, side_rows, lanes), lambda i: (0, i, 0)),
        ]
        if ends:
            outs += [((VAR_DEV, SHIFT, breadth, lanes), BF16)] * 2
            out_specs += [
                pl.BlockSpec((VAR_DEV, SHIFT, breadth, lanes), lambda i: (0, 0, 0, 0))
            ] * 2
        return pl.pallas_call(
            functools.partial(first_kernel, heads, channels, ends),
            grid=(steps,),
            in_specs=[
                pl.BlockSpec((WIN, breadth, channels), lambda i: (first(i), 0, 0)),
                pl.BlockSpec((WIN, breadth, channels), lambda i: (second(i), 0, 0)),
                whole(labels_across),
                *specs,
            ],
            out_specs=out_specs,
            out_shape=[jax.ShapeDtypeStruct(*o) for o in outs],
            scratch_shapes=[
                pltpu.VMEM((2 * tokens, lanes), F32),
                pltpu.VMEM((2, side_rows, lanes), F32),
            ],
            compiler_params=params(),
            cost_estimate=cost(steps * breadth // WIN * 4),
            name="block_one_ends" if ends else "block_one_middle",
        )(features, features, labels_across, *arrays)

    y_ends, left_ends, right_ends, top_own, bottom_own = block_one(True)
    top, bottom = exchanged(bottom_own, top_own, "ty")
    y_middle, left_middle, right_middle = block_one(False)
    half = side_rows // 2
    strips_out = []
    for ends, middle, cut in (
        (right_ends, right_middle, slice(breadth - SHIFT, breadth)),
        (left_ends, left_middle, slice(0, SHIFT)),
    ):
        corners = [a[:, :, cut].reshape(VAR_DEV, SHIFT * SHIFT, lanes) for a in (top, bottom)]
        strips_out.append(
            jnp.concatenate(
                [corners[0], ends[:, :half], middle, ends[:, half:], corners[1]], axis=1
            )
        )
    sides = exchanged(*strips_out, "tx")

    arrays, specs = block_specs(1)
    inner_count = (strips - 1) * (breadth // WIN - 1)
    group = next(g for g in range(7, 0, -1) if inner_count % g == 0)
    inner, marks = pl.pallas_call(
        functools.partial(inner_kernel, heads, channels, group),
        grid=(inner_count // group,),
        in_specs=[whole(y_ends), whole(y_middle), *specs],
        out_specs=[
            pl.BlockSpec((group, VAR_DEV, CELLS, lanes), lambda i: (i, 0, 0, 0)),
            pl.BlockSpec((strips, tokens, LANES), lambda i: (0, 0, 0)),
        ],
        out_shape=[
            jax.ShapeDtypeStruct((inner_count, VAR_DEV, CELLS, lanes), BF16),
            jax.ShapeDtypeStruct((strips, tokens, LANES), BF16),
        ],
        scratch_shapes=[
            pltpu.VMEM((height, breadth, lanes), F32),
            pltpu.VMEM((inner_count, VAR_DEV, CELLS, lanes), F32),
        ],
        compiler_params=params(),
        cost_estimate=cost(inner_count * VAR_DEV),
        name="block_two_inner",
    )(y_ends, y_middle, *arrays)

    tall, wide = height + 2 * SHIFT, breadth + 2 * SHIFT
    slots = 2 * (tall + wide) // WIN - 4
    group = next(g for g in range(8, 0, -1) if slots % g == 0)
    operands = (y_ends, y_middle, top, bottom, *sides, inner)
    partial_shape = jax.ShapeDtypeStruct((strips, out_channels, tokens), BF16)
    partial = pl.pallas_call(
        functools.partial(outer_kernel, heads, channels, group),
        grid=(1,),
        in_specs=[*[whole(a) for a in operands], *specs, whole(recon)],
        out_specs=whole(partial_shape),
        out_shape=partial_shape,
        scratch_shapes=[
            pltpu.VMEM((WIN, wide, lanes), F32),
            pltpu.VMEM((height, 2 * WIN, lanes), F32),
            pltpu.VMEM((slots, VAR_DEV, CELLS, lanes), F32),
            pltpu.VMEM((slots, VAR_DEV, CELLS, lanes), BF16),
            pltpu.VMEM((tall + WIN, wide, lanes), F32),
        ],
        compiler_params=params(),
        name="block_two_border",
    )(*operands, *arrays, recon)

    sharers = lax.axis_size("var")
    strips = strips // sharers
    parts = lax.all_to_all(
        partial.reshape(sharers, strips, out_channels, tokens), "var", 0, 0
    )
    colours = out_channels // (SCALE * SCALE)
    final = (colours, strips * WIN * SCALE, breadth * SCALE)
    operands = (parts, marks, refine_grid, refine_qvt, refine_key, refine_projt)
    in_specs = [
        pl.BlockSpec(a.shape, lambda i, place, n=a.ndim: (0,) * n) for a in operands
    ]
    in_specs[1] = pl.BlockSpec((strips, tokens, LANES), lambda i, place: (place[0], 0, 0))
    strip = pl.pallas_call(
        functools.partial(refine_kernel, refine_heads, channels % LANES),
        grid_spec=pltpu.PrefetchScalarGridSpec(
            num_scalar_prefetch=1,
            grid=(1,),
            in_specs=in_specs,
            out_specs=pl.BlockSpec(final, lambda i, place: (0, 0, 0)),
            scratch_shapes=[pltpu.VMEM(final, F32)],
        ),
        out_shape=jax.ShapeDtypeStruct(final, BF16),
        compiler_params=params(),
        name="refinement",
    )(position[None], *operands)
    gathered = lax.all_gather(strip, "var", axis=0)
    picture = gathered.transpose(1, 0, 2, 3).reshape(colours, height * SCALE, breadth * SCALE)
    return picture.astype(F32)


def solution(mesh):
    placed = (P("ty", "tx", None), P("ty", "tx"), P(), P(), P(), P(), P(), P(), P(), P(), P())
    return jax.shard_map(
        local, mesh=mesh, in_specs=placed, out_specs=P(None, "ty", "tx"), check_vma=False
    )
```

```python
import functools

import jax
import jax.numpy as jnp
from jax import lax
from jax.experimental import pallas as pl
from jax.experimental.pallas import tpu as pltpu
from jax.sharding import PartitionSpec as P

WIN = 8
CELLS = WIN * WIN
SHIFT = 4
SCALE = 4
VAR_DEV = 2
LANES = 128
HEAD_ROWS = 32
CLASSES = 4
MARKS = CLASSES + 2
SIDE = 2 * WIN - 1

EPSILON = 1e-05
LOG2E = 1.4426950408889634
BIG = float(2.0**100)
ERF_TANH = (0.7975076, 0.0370060, -0.00035159)
REACH = 36.0

NN = (((1,), (0,)), ((), ()))
NT = (((1,), (1,)), ((), ()))
F32 = jnp.float32
BF16 = jnp.bfloat16


def dot(a, b, dims=NN):
    return lax.dot_general(a, b, dims, preferred_element_type=F32)


def iota(shape, dim):
    return lax.broadcasted_iota(jnp.int32, shape, dim)


def round_up(size, multiple):
    return -(-size // multiple) * multiple


def one_hot(condition):
    return jnp.where(condition, 1.0, 0.0).astype(BF16)


def exact(a, b, dims=NN):
    return dot(a, b, dims).astype(BF16)


def pad_matrix(rows, size):
    return one_hot(iota((rows, size), 0) == iota((rows, size), 1))


def head_matrix(rows, size, heads, width, first=0):
    row = iota((rows, size), 0)
    unit = row % HEAD_ROWS
    source = first + row // HEAD_ROWS * width + unit
    keep = (unit < width) & (row < heads * HEAD_ROWS)
    return one_hot(keep & (iota((rows, size), 1) == source))


def query_labels(rows, lanes, first_row, first_lane):
    row = iota((rows, lanes), 0) - first_row
    lane = iota((rows, lanes), 1) - first_lane
    is_class = (row >= 0) & (row < CLASSES)
    is_pad = row == CLASSES
    same = is_class & (row == lane)
    always = lane == CLASSES + 1
    return jnp.where(same, BIG, 0.0) - jnp.where(always & (is_class | is_pad), BIG, 0.0)


def key_labels(rows, lanes, first_row, first_lane):
    row = iota((rows, lanes), 0) - first_row
    lane = iota((rows, lanes), 1) - first_lane
    is_class = (lane >= 0) & (lane < CLASSES)
    is_pad = lane == CLASSES
    add = is_class & (row == lane) | is_pad & (row == CLASSES + 1)
    return jnp.where(add, 1.0, 0.0) - jnp.where(is_pad & (row == CLASSES), 1.0, 0.0)


def bias_rows(table, turn, flip_rows, flip_cols):
    shape = (1, WIN * LANES)
    lane = iota(shape, 1)
    row_step = lane % LANES // WIN - (WIN - 1)
    col_step = lane % WIN - lane // LANES
    row_step = jnp.where(flip_rows, -row_step, row_step)
    col_step = jnp.where(flip_cols, -col_step, col_step)
    lead = jnp.where(turn, col_step, row_step)
    trail = jnp.where(turn, row_step, col_step)
    index = (lead + WIN - 1) * SIDE + trail + WIN - 1
    pick = one_hot(iota((table.shape[1], WIN * LANES), 0) == index)
    rest = table * LOG2E
    parts = []
    for _ in range(3):
        parts.append(rest.astype(BF16))
        rest = rest - parts[-1].astype(F32)
    moved = dot(jnp.concatenate(parts, axis=0), pick)
    size = table.shape[0]
    return moved[:size] + moved[size : 2 * size] + moved[2 * size :]


def bias_grid(rows, rows_ref, store):
    heads = rows.shape[0]
    for key_col in range(WIN):
        rows_ref[0:heads, key_col, :] = rows[:, key_col * LANES : (key_col + 1) * LANES]
    half = iota((WIN, LANES), 1)
    for pair in range(heads // 2):
        even, odd = rows_ref[2 * pair], rows_ref[2 * pair + 1]
        for key_row in range(WIN):
            start = (WIN - 1 - key_row) * WIN
            left = pltpu.roll(even, (LANES - start) % LANES, 1)
            right = pltpu.roll(odd, (LANES - start + CELLS) % LANES, 1)
            store(key_row, pair, jnp.where(half < CELLS, left, right))


def prepare_kernel(
    heads,
    qkv_ref,
    proj_ref,
    up_ref,
    down_ref,
    swin_bias_ref,
    recon_ref,
    refine_qkv_ref,
    refine_proj_ref,
    refine_bias_ref,
    qvt_out,
    key_out,
    proj_out,
    up_out,
    down_out,
    recon_out,
    bias_out,
    refine_qvt_out,
    refine_key_out,
    refine_proj_out,
    refine_bias_out,
    rows_ref,
    tables_ref,
):
    blocks, channels, hidden = up_ref.shape
    width = channels // heads
    lanes = key_out.shape[1]
    head_rows = heads * HEAD_ROWS
    mark_rows = head_rows + 16
    taps, out, _ = recon_ref.shape
    refine_heads = refine_bias_ref.shape[0]
    refine_width = out // refine_heads
    refine_rows = refine_heads * HEAD_ROWS
    mark = channels % LANES
    pad = one_hot(iota((lanes, channels), 0) == iota((lanes, channels), 1))

    for i in range(blocks):
        tables_ref[i * heads : (i + 1) * heads] = swin_bias_ref[:, i]
    rows, moved = [], []
    kernel = recon_ref[...].reshape(taps * out, channels)
    for v in range(VAR_DEV):
        code = lax.axis_index("var") * VAR_DEV + v
        turn, flip_rows, flip_cols = code // 4 == 1, code // 2 % 2 == 1, code % 2 == 1
        rows.append(bias_rows(tables_ref[: blocks * heads], turn, flip_rows, flip_cols))
        shape = (3 * lanes, 1)
        row = iota(shape, 0)
        row_step = row // lanes - 1
        lane = row % lanes
        col_step = jnp.where(lane >= LANES, 1, jnp.where(lane >= out, 0, -1))
        channel = jnp.where(lane >= LANES, lane - LANES, jnp.where(lane >= out, lane - out, lane))
        row_step = jnp.where(flip_rows, -row_step, row_step)
        col_step = jnp.where(flip_cols, -col_step, col_step)
        tap = (jnp.where(turn, col_step, row_step) + 1) * 3
        tap = tap + jnp.where(turn, row_step, col_step) + 1
        sub_row = channel % (SCALE * SCALE) // SCALE
        sub_col = channel % SCALE
        sub_row = jnp.where(flip_rows, SCALE - 1 - sub_row, sub_row)
        sub_col = jnp.where(flip_cols, SCALE - 1 - sub_col, sub_col)
        source = channel // (SCALE * SCALE) * SCALE * SCALE
        source = source + jnp.where(turn, sub_col, sub_row) * SCALE
        source = tap * out + source + jnp.where(turn, sub_row, sub_col)
        source = jnp.where(channel < out, source, -1)
        moved.append(exact(one_hot(iota((3 * lanes, taps * out), 1) == source), kernel))
    never = lax.axis_index("var") < 0
    refine_table = bias_rows(refine_bias_ref[...], never, never, never)
    keys = [
        exact(qkv_ref[i], head_matrix(lanes, 3 * channels, heads, width, channels), NT)
        for i in range(blocks)
    ]
    weight = refine_qkv_ref[...]
    refine_queries = exact(
        head_matrix(refine_rows + 16, 3 * out, refine_heads, refine_width), weight, NT
    )
    refine_values = exact(
        head_matrix(refine_rows, 3 * out, refine_heads, refine_width, 2 * out), weight, NT
    )
    refine_keys = exact(head_matrix(LANES, 3 * out, refine_heads, refine_width, out), weight, NT)
    refine_proj = []
    for h in range(refine_heads):
        shape = (LANES, out)
        row = iota(shape, 0)
        pick = one_hot((row < refine_width) & (iota(shape, 1) == row + h * refine_width))
        refine_proj.append(exact(pick, refine_proj_ref[...]))

    queries = head_matrix(mark_rows, 3 * channels, heads, width)
    values = head_matrix(head_rows, 3 * channels, heads, width, 2 * channels)
    query_add = query_labels(mark_rows, lanes, head_rows, channels).astype(BF16)
    key_add = key_labels(lanes, lanes, channels, head_rows)
    shape = (2 * LANES, channels)
    row = iota(shape, 0)
    head, unit = row % LANES // HEAD_ROWS * 2 + row // LANES, row % HEAD_ROWS
    proj_rows = one_hot((head < heads) & (unit < width) & (iota(shape, 1) == head * width + unit))
    shape = (down_out.shape[1], hidden)
    down_rows = one_hot(iota(shape, 0) == iota(shape, 1))
    for i in range(blocks):
        for ref in (qvt_out, proj_out, up_out, down_out):
            ref[i] = jnp.zeros(ref.shape[1:], BF16)
        qvt_out[i, :mark_rows] = query_add
        qvt_out[i, :mark_rows, :channels] = exact(queries, qkv_ref[i], NT)
        qvt_out[i, mark_rows:, :channels] = exact(values, qkv_ref[i], NT)
        proj_out[i, :, :channels] = exact(proj_rows, proj_ref[i])
        up_out[i, :, :hidden] = exact(pad, up_ref[i])
        down_out[i, :, :channels] = exact(down_rows, down_ref[i], NT)

    for i in range(blocks):
        key_out[i] = (dot(pad, keys[i]) + key_add).astype(BF16)
    for v in range(VAR_DEV):
        recon_out[v] = exact(pad, moved[v], NT)
    out_pad = one_hot(iota((LANES, out), 0) == iota((LANES, out), 1))
    refine_qvt_out[: refine_rows + 16] = (
        dot(refine_queries, out_pad, NT)
        + query_labels(refine_rows + 16, LANES, refine_rows, mark)
    ).astype(BF16)
    refine_qvt_out[refine_rows + 16 :] = exact(refine_values, out_pad, NT)
    refine_key_out[...] = (
        dot(out_pad, refine_keys, NT) + key_labels(LANES, LANES, mark, refine_rows)
    ).astype(BF16)
    for h in range(refine_heads):
        square = dot(refine_proj[h], out_pad, NT)
        refine_proj_out[h * out : (h + 1) * out] = square.T[:out].astype(BF16)
    for v in range(VAR_DEV):
        for i in range(blocks):

            def store(key_row, pair, value):
                at = slice(key_row * WIN, (key_row + 1) * WIN)
                bias_out[i, v, at, pair * LANES : (pair + 1) * LANES] = value

            bias_grid(rows[v][i * heads : (i + 1) * heads], rows_ref, store)

    def store_refine(key_row, pair, value):
        refine_bias_out[key_row * WIN : (key_row + 1) * WIN] = value

    bias_grid(refine_table, rows_ref, store_refine)


def gelu(x):
    x = x.astype(BF16)
    square = jnp.minimum(x * x, BF16(REACH))
    first, second, third = (BF16(factor) for factor in ERF_TANH)
    series = (square * third + second) * square + first
    half = BF16(0.5) * x
    return half + half * jnp.tanh(x * series)


def normalize(x, channels):
    inside = iota((1, x.shape[1]), 1) < channels
    mean = jnp.sum(jnp.where(inside, x, 0.0), axis=1, keepdims=True) * (1.0 / channels)
    centred = jnp.where(inside, x - mean, 0.0)
    spread = jnp.sum(centred * centred, axis=1, keepdims=True) * (1.0 / channels)
    return jnp.where(inside, centred * lax.rsqrt(spread + EPSILON), x).astype(BF16)


def split_queries(queries, heads):
    pairs = heads // 2
    head_rows = heads * HEAD_ROWS
    left = iota((1, LANES), 1) < CELLS
    turned = pltpu.roll(queries, CELLS, 1).astype(BF16)
    queries = queries.astype(BF16)
    depth = round_up(queries.shape[0], LANES)
    zero = jnp.zeros((HEAD_ROWS, LANES), BF16)
    results = []
    for even, odd in ((queries, turned), (turned, queries)):
        marks = jnp.where(left, even[head_rows:], odd[head_rows:])
        columns = []
        for pair in range(pairs):
            at = pair * 2 * HEAD_ROWS
            rows = [zero] * heads
            rows[2 * pair] = jnp.where(left, even[at : at + HEAD_ROWS], zero)
            rows[2 * pair + 1] = jnp.where(left, zero, odd[at + HEAD_ROWS : at + 2 * HEAD_ROWS])
            rows.append(marks)
            rows.append(jnp.zeros((depth - queries.shape[0], LANES), BF16))
            columns.append(jnp.concatenate(rows, axis=0))
        results.append(jnp.concatenate(columns, axis=1) if pairs > 1 else columns[0])
    return results


def heads_of(n, scale, heads, width, w_qvt, w_key):
    mark_rows = heads * HEAD_ROWS + 16
    both = dot(w_qvt, n, NT)
    row = iota((mark_rows, 1), 0)
    queries = both[:mark_rows] * jnp.where(row < heads * HEAD_ROWS, scale, 1.0)
    values = both[mark_rows:]
    row = iota((heads * HEAD_ROWS, 1), 0) % HEAD_ROWS
    values = jnp.where(row == width, 1.0, values).astype(BF16)
    keys = dot(n, w_key).astype(BF16)
    scores = []
    for place in range(n.shape[0] // LANES):
        cut = slice(place * LANES, (place + 1) * LANES)
        for half, stationary in enumerate(split_queries(queries[:, cut], heads)):
            at = place * LANES + half * CELLS
            scores.append(dot(keys[at : at + CELLS], stationary))
    return scores, values


def soft(scores):
    largest = jnp.max(scores, axis=0, keepdims=True)
    return jnp.exp2(scores - largest).astype(BF16)


def mix_pair(values, first, second, heads, ones_row):
    zero = jnp.zeros((CELLS, LANES), BF16)
    lane = iota((HEAD_ROWS, 2 * LANES), 1) % LANES
    mixed = []
    for pair in range(heads // 2):
        cut = slice(pair * LANES, (pair + 1) * LANES)
        stationary = jnp.concatenate(
            [
                jnp.concatenate([first[:, cut], zero], axis=1),
                jnp.concatenate([zero, second[:, cut]], axis=1),
            ],
            axis=0,
        )
        result = dot(values[pair * CELLS : (pair + 1) * CELLS], stationary)
        joined = jnp.where(lane < CELLS, result[:HEAD_ROWS], result[HEAD_ROWS:])
        mixed.append(joined * pl.reciprocal(joined[ones_row : ones_row + 1]))
    return mixed


def swin_block(x, pairs, heads, channels, bias, w_qvt, w_key, w_proj, w_up, w_down):
    width = channels // heads
    n = normalize(x, channels)
    scale = width**-0.5 * LOG2E
    scores, values = heads_of(n, scale, heads, width, w_qvt[...], w_key[...])
    pad = jnp.zeros((LANES - heads // 2 * HEAD_ROWS, 2 * LANES), F32)
    weights = [
        (soft(scores[2 * place] + bias(a)), soft(scores[2 * place + 1] + bias(b)))
        for place, a, b in pairs
    ]
    blocks = []
    for (place, _, _), (first, second) in zip(pairs, weights):
        cut = slice(place * LANES, (place + 1) * LANES)
        mixed = mix_pair(values[:, cut], first, second, heads, width)
        blocks.append(jnp.concatenate(mixed + [pad], axis=0).astype(BF16))
    outputs = []
    for block in blocks:
        for half in range(2):
            turned = block[:, half * LANES : (half + 1) * LANES].T
            outputs.append(jnp.concatenate([turned[:CELLS], turned[CELLS:]], axis=1))
    outputs = jnp.concatenate(outputs, axis=0)
    places = [place for place, _, _ in pairs]
    if places != list(range(x.shape[0] // LANES)):
        x = jnp.concatenate([x[place * LANES : (place + 1) * LANES] for place in places], axis=0)
    h = (x + dot(outputs, w_proj[...])).astype(BF16).astype(F32)
    hidden = gelu(dot(normalize(h, channels), w_up[...]))
    y = h + dot(hidden, w_down[...])
    return [y[i * LANES : (i + 1) * LANES] for i in range(len(pairs))]


def windows_of(grid):
    lanes = grid.shape[2]
    return jnp.concatenate(
        [
            grid[:, w * WIN : (w + 1) * WIN].reshape(CELLS, lanes)
            for w in range(grid.shape[1] // WIN)
        ],
        axis=0,
    )


def first_kernel(heads, channels, strips, x_ref, labels_ref, bias_ref, *refs):
    ends = strips[0] == 0
    *weights, y_ref, left_ref, right_ref = refs[:8]
    held, side = refs[-2:]
    breadth = x_ref.shape[1]
    count = breadth // WIN
    tokens, lanes = held.shape
    part = tokens // len(strips)
    rows_total = labels_ref.shape[1]
    for k, strip in enumerate(strips):
        rows = x_ref[strip * WIN : (strip + 1) * WIN].astype(F32)
        held[k * part : (k + 1) * part, :channels] = windows_of(rows)
    token = iota((tokens, rows_total), 0)
    strip = token // part + strips[0]
    if ends:
        strip = jnp.where(token < part, strips[0], strips[1])
    at_row = strip * WIN + token % CELLS // WIN == iota((tokens, rows_total), 1)
    by_row = dot(one_hot(at_row), labels_ref[...].astype(F32).astype(BF16), NT)
    token = iota((tokens, breadth), 0)
    at_col = token % part // CELLS * WIN + token % WIN == iota((tokens, breadth), 1)
    label = dot(jnp.where(at_col, by_row, 0.0).astype(BF16), jnp.ones((breadth, LANES), BF16))
    lane = iota((tokens, LANES), 1) - channels % LANES
    marks = jnp.where(
        (label == (lane + 1).astype(F32)) & (lane < CLASSES)
        | (lane >= CLASSES) & (lane < MARKS),
        1.0,
        0.0,
    )
    tail = jnp.where(lane < 0, held[:, lanes - LANES :], marks)
    x = jnp.concatenate([held[:, : lanes - LANES], tail], axis=1)
    places = tokens // LANES
    pairs = [(place, v, v) for v in range(VAR_DEV) for place in range(places)]
    results = swin_block(x, pairs, heads, channels, lambda v: bias_ref[v], *weights)
    for v in range(VAR_DEV):
        for k in range(len(strips)):
            windows = []
            for w in range(count):
                group = k * count + w
                block = results[v * places + group // 2]
                at = group % 2 * CELLS
                windows.append(block[at : at + CELLS].reshape(WIN, WIN, lanes))
            y_ref[v, k * WIN : (k + 1) * WIN] = jnp.concatenate(windows, axis=1).astype(BF16)
            at = k * WIN * SHIFT
            for r in range(WIN):
                rows = slice(at + r * SHIFT, at + (r + 1) * SHIFT)
                side[0, rows] = windows[0][r, :SHIFT]
                side[1, rows] = windows[-1][r, SHIFT:]
        left_ref[v] = side[0].astype(BF16)
        right_ref[v] = side[1].astype(BF16)
    if ends:
        if len(refs) == 11:
            refs[8][...] = jnp.where(
                lax.axis_index("ty") == 0, y_ref[:, 2 * WIN - SHIFT :], y_ref[:, :SHIFT]
            )
        else:
            refs[8][...] = y_ref[:, :SHIFT]
            refs[9][...] = y_ref[:, 2 * WIN - SHIFT :]


def place_rows(store, ends_ref, middle_ref, v):
    store(0, ends_ref[v, :WIN])
    for r in range(0, middle_ref.shape[1], WIN):
        store(WIN + r, middle_ref[v, r : r + WIN])
    store(WIN + middle_ref.shape[1], ends_ref[v, WIN:])


def inner_kernel(
    heads, channels, group, ends_ref, middle_ref, bias_ref, *refs
):
    *weights, y_ref, marks_ref, held, x_held = refs
    height, breadth, lanes = held.shape
    count = breadth // WIN - 1

    @pl.when(pl.program_id(0) == 0)
    def _():
        for v in range(VAR_DEV):

            def store(first, rows):
                rows = rows.astype(F32)
                held[first : first + WIN] = rows
                if v == 0:
                    marks_ref[first // WIN] = windows_of(rows[:, :, lanes - LANES :]).astype(BF16)

            place_rows(store, ends_ref, middle_ref, v)
            for strip in range(height // WIN - 1):
                rows = slice(strip * WIN + SHIFT, (strip + 1) * WIN + SHIFT)
                for w in range(count):
                    at = SHIFT + w * WIN
                    x_held[strip * count + w, v] = held[rows, at : at + WIN].reshape(CELLS, lanes)

    base = pl.program_id(0) * group
    x = x_held[pl.ds(base, group)].reshape(group * VAR_DEV * CELLS, lanes)
    pairs = [(w, 0, 1) for w in range(group)]
    results = swin_block(x, pairs, heads, channels, lambda v: bias_ref[v], *weights)
    for w in range(group):
        y_ref[w] = results[w].astype(BF16).reshape(VAR_DEV, CELLS, lanes)


def outer_kernel(
    heads,
    channels,
    group,
    ends_ref,
    middle_ref,
    top_ref,
    bottom_ref,
    left_ref,
    right_ref,
    inner_ref,
    bias_ref,
    *refs,
):
    *weights, w_recon, out_ref, rows_held, sides_held, x_held, y_held, acc = refs
    lanes = middle_ref.shape[3]
    height, breadth = middle_ref.shape[1] + 2 * WIN, middle_ref.shape[2]
    tall, wide = height + 2 * SHIFT, breadth + 2 * SHIFT
    strips, count = tall // WIN, wide // WIN
    always = iota((1, lanes), 1) == channels + CLASSES + 1

    def marked(received):
        return jnp.where(always, 1.0, received.astype(F32))

    for v in range(VAR_DEV):
        for end in range(2):
            outside, inside = (0, SHIFT) if end == 0 else (SHIFT, 0)
            corner = 0 if end == 0 else (tall - SHIFT) * SHIFT
            received = top_ref if end == 0 else bottom_ref
            first = 0 if end == 0 else 2 * WIN - SHIFT
            across = slice(SHIFT, SHIFT + breadth)
            rows_held[outside : outside + SHIFT, across] = marked(received[v])
            rows_held[inside : inside + SHIFT, across] = ends_ref[
                v, first : first + SHIFT
            ].astype(F32)
            side_first = SHIFT * SHIFT if end == 0 else (tall - 2 * SHIFT) * SHIFT
            for ref, at in ((left_ref, 0), (right_ref, wide - SHIFT)):
                for rows, start in ((outside, corner), (inside, side_first)):
                    piece = marked(ref[v, start : start + SHIFT * SHIFT])
                    rows_held[rows : rows + SHIFT, at : at + SHIFT] = piece.reshape(
                        SHIFT, SHIFT, lanes
                    )
            for w in range(count):
                x_held[end * count + w, v] = rows_held[:, w * WIN : (w + 1) * WIN].reshape(
                    CELLS, lanes
                )

        def store(first, rows):
            sides_held[first : first + WIN, :WIN] = rows[:, :WIN].astype(F32)
            sides_held[first : first + WIN, WIN:] = rows[:, breadth - WIN :].astype(F32)

        place_rows(store, ends_ref, middle_ref, v)
        for strip in range(1, strips - 1):
            rows = slice(strip * WIN - SHIFT, (strip + 1) * WIN - SHIFT)
            cut = slice(strip * WIN * SHIFT, (strip + 1) * WIN * SHIFT)
            for end in range(2):
                ref = left_ref if end == 0 else right_ref
                piece = marked(ref[v, cut]).reshape(WIN, SHIFT, lanes)
                at = 0 if end == 0 else WIN + SHIFT
                own = sides_held[rows, at : at + SHIFT]
                both = [piece, own] if end == 0 else [own, piece]
                slot = 2 * count + 2 * (strip - 1) + end
                x_held[slot, v] = jnp.concatenate(both, axis=1).reshape(CELLS, lanes)

    slots = x_held.shape[0]

    def border(step, carry):
        x = x_held[pl.ds(step * group, group)].reshape(group * VAR_DEV * CELLS, lanes)
        pairs = [(w, 0, 1) for w in range(group)]
        results = swin_block(x, pairs, heads, channels, lambda v: bias_ref[v], *weights)
        at = channels + CLASSES
        for w in range(group):
            block = x[w * LANES : (w + 1) * LANES]
            y = results[w] * block[:, at : at + 1]
            y_held[step * group + w] = y.astype(BF16).reshape(VAR_DEV, CELLS, lanes)
        return carry

    lax.fori_loop(0, slots // group, border, 0)

    weights = w_recon[...].reshape(VAR_DEV * lanes, 3 * lanes)

    def scatter(strip, windows):
        tokens = [jnp.concatenate(windows(v), axis=0) for v in range(VAR_DEV)]
        total = dot(jnp.concatenate(tokens, axis=1), weights)
        total = total.reshape(count, WIN, WIN, 3 * lanes)
        for e in range(3):
            rows = slice(strip * WIN + 2 - e, (strip + 1) * WIN + 2 - e)
            for w in range(count):
                across = slice(w * WIN, (w + 1) * WIN)
                part = total[w, :, :, e * lanes : (e + 1) * lanes]
                acc[rows, across] = part if e == 0 else acc[rows, across] + part

    out_channels = out_ref.shape[1]

    def finish(strip):
        rows = slice(1 + SHIFT + strip * WIN, 1 + SHIFT + (strip + 1) * WIN)
        centre = acc[rows, SHIFT : SHIFT + breadth, :LANES]
        centre = pltpu.roll(centre.reshape(WIN * breadth, LANES), LANES - out_channels, 1)
        result = (
            acc[rows, SHIFT - 1 : SHIFT - 1 + breadth, :LANES]
            + centre.reshape(WIN, breadth, LANES)
            + acc[rows, SHIFT + 1 : SHIFT + 1 + breadth, LANES : 2 * LANES]
        )
        out_ref[strip] = windows_of(result).T[:out_channels].astype(BF16)

    scatter(0, lambda v: [y_held[w, v] for w in range(count)])
    for strip in range(1, strips):
        if strip == strips - 1:
            scatter(strip, lambda v: [y_held[count + w, v] for w in range(count)])
        else:
            slot = 2 * count + 2 * (strip - 1)
            first = (strip - 1) * (count - 2)
            scatter(
                strip,
                lambda v: [
                    y_held[slot, v],
                    *[inner_ref[first + w, v] for w in range(count - 2)],
                    y_held[slot + 1, v],
                ],
            )
        finish(strip - 1)


def refine_kernel(
    heads, first_mark, parts_ref, marks_ref, bias_ref, w_qvt, w_key, w_projt, out_ref, spread_ref
):
    sources, strips, channels, strip_tokens = parts_ref.shape
    breadth = strip_tokens // WIN
    width = channels // heads

    @pl.when(pl.program_id(0) == 0)
    def _():
        shape = spread_ref.shape
        cell = iota(shape, 1) // SCALE
        source = (cell % breadth // WIN) * CELLS + (cell // breadth) * WIN + cell % WIN
        spread_ref[...] = one_hot(iota(shape, 0) == source)

    z = jnp.concatenate(
        [
            sum(parts_ref[s, strip].astype(F32) for s in range(sources))
            for strip in range(strips)
        ],
        axis=1,
    ) * (1.0 / (sources * VAR_DEV))
    mean = jnp.sum(z, axis=0, keepdims=True) * (1.0 / channels)
    centred = z - mean
    spread = jnp.sum(centred * centred, axis=0, keepdims=True) * (1.0 / channels)
    normed = centred * lax.rsqrt(spread + EPSILON)
    tall = jnp.concatenate([normed, jnp.zeros((LANES - channels, normed.shape[1]), F32)], axis=0)
    marks = jnp.concatenate([marks_ref[s].astype(F32) for s in range(strips)], axis=0)
    lane = iota((1, LANES), 1)
    is_mark = (lane >= first_mark) & (lane < first_mark + MARKS)
    n = jnp.where(is_mark, marks, tall.T).astype(BF16)
    scores, values = heads_of(
        n, width**-0.5 * LOG2E, heads, width, w_qvt[...], w_key[...]
    )
    probabilities = [soft(s + bias_ref[...]) for s in scores]
    lane = iota((channels, LANES), 1)
    branches = []
    for pair in range(len(probabilities) // 2):
        mixed = mix_pair(
            values[:, pair * LANES : (pair + 1) * LANES],
            probabilities[2 * pair],
            probabilities[2 * pair + 1],
            heads,
            width,
        )[0].astype(BF16)
        both = dot(w_projt[...][:, :HEAD_ROWS], mixed)
        even, odd = both[:channels], both[channels:]
        halves = []
        for half in range(2):
            cut = slice(half * LANES, (half + 1) * LANES)
            halves.append(even[:, cut] + pltpu.roll(odd[:, cut], CELLS, 1))
        branches.append(jnp.where(lane < CELLS, halves[0], pltpu.roll(halves[1], CELLS, 1)))
    refined = (z + jnp.concatenate(branches, axis=1)).astype(BF16)
    stacked = jnp.concatenate(
        [refined[:, s * strip_tokens : (s + 1) * strip_tokens] for s in range(strips)], axis=0
    )
    wide = dot(stacked, spread_ref[...])
    own = iota(wide.shape, 1) % SCALE == iota(wide.shape, 0) % SCALE
    wide = jnp.where(own, wide, 0.0).astype(BF16)
    shape = (wide.shape[0] // SCALE, wide.shape[0])
    folded = dot(one_hot(iota(shape, 1) // SCALE == iota(shape, 0)), wide)
    colours = channels // (SCALE * SCALE)
    row_lanes = breadth * SCALE
    for s in range(strips):
        for c in range(colours):
            first = (s * colours + c) * SCALE
            for y in range(WIN):
                start = (s * WIN + y) * SCALE
                out_ref[c, start : start + SCALE] = folded[
                    first : first + SCALE, y * row_lanes : (y + 1) * row_lanes
                ]


def exchanged(last, first, axis):
    count = lax.axis_size(axis)
    up = [(i, i + 1) for i in range(count - 1)]
    down = [(i + 1, i) for i in range(count - 1)]
    return lax.ppermute(last, axis, up), lax.ppermute(first, axis, down)


def swapped(strip, axis):
    at_start = lax.axis_index(axis) == 0
    received = lax.ppermute(strip, axis, [(0, 1), (1, 0)])
    zero = jnp.zeros_like(received)
    return jnp.where(at_start, zero, received), jnp.where(at_start, received, zero)


def whole(a):
    return pl.BlockSpec(a.shape, lambda *i: (0,) * a.ndim)


def params():
    return pltpu.CompilerParams(
        dimension_semantics=("arbitrary",), vmem_limit_bytes=56 * 1024 * 1024
    )


def local(
    features,
    labels,
    qkv_weight,
    proj_weight,
    up_weight,
    down_weight,
    swin_bias,
    recon_weight,
    refine_qkv,
    refine_proj,
    refine_bias,
):
    height, breadth, channels = features.shape
    heads = swin_bias.shape[1]
    out_channels = recon_weight.shape[-1]
    refine_heads = refine_bias.shape[0]
    lanes = round_up(channels + MARKS, LANES)
    hidden = round_up(up_weight.shape[-1], LANES)
    operands = (
        qkv_weight,
        proj_weight,
        up_weight,
        jnp.swapaxes(down_weight, 1, 2),
        jnp.swapaxes(swin_bias, 0, 1),
        jnp.swapaxes(recon_weight, 1, 2),
        refine_qkv,
        refine_proj,
        refine_bias,
    )
    head_rows, refine_rows = heads * HEAD_ROWS, refine_heads * HEAD_ROWS
    shapes = [
        ((2, 2 * head_rows + 16, lanes), BF16),
        ((2, lanes, lanes), BF16),
        ((2, 2 * LANES, lanes), BF16),
        ((2, lanes, hidden), BF16),
        ((2, hidden, lanes), BF16),
        ((VAR_DEV, lanes, 3 * lanes), BF16),
        ((2, VAR_DEV, CELLS, heads * CELLS), F32),
        ((2 * refine_rows + 16, LANES), BF16),
        ((LANES, LANES), BF16),
        ((refine_heads * out_channels, LANES), BF16),
        ((CELLS, refine_heads * CELLS), F32),
    ]
    shapes = [jax.ShapeDtypeStruct(*s) for s in shapes]
    prepared = pl.pallas_call(
        functools.partial(prepare_kernel, heads),
        grid=(1,),
        in_specs=[whole(a) for a in operands],
        out_specs=[whole(s) for s in shapes],
        out_shape=shapes,
        scratch_shapes=[
            pltpu.VMEM((heads, WIN, LANES), F32),
            pltpu.VMEM((round_up(2 * heads, 8), swin_bias.shape[2]), F32),
        ],
        compiler_params=params(),
        name="prepare",
    )(*operands)
    *swin, recon, bias, refine_qvt, refine_key, refine_projt, refine_grid = prepared

    def block_specs(i):
        arrays = (bias, *swin)
        return arrays, [
            pl.BlockSpec((None,) + a.shape[1:], lambda *_, n=a.ndim: (i,) + (0,) * (n - 1))
            for a in arrays
        ]

    def cost(windows):
        return pl.CostEstimate(
            flops=windows * 400_000_000, bytes_accessed=windows * 200_000, transcendentals=0
        )

    arrays, specs = block_specs(0)
    strips = height // WIN
    tokens = WIN * breadth
    labels_across = labels.T

    pair_axis = lax.axis_size("ty") == 2

    def block_one(places, name):
        rows = len(places) * WIN
        outs = [
            ((VAR_DEV, rows, breadth, lanes), BF16),
            ((VAR_DEV, rows * SHIFT, lanes), BF16),
            ((VAR_DEV, rows * SHIFT, lanes), BF16),
        ]
        if places[0] == 0:
            outs += [((VAR_DEV, SHIFT, breadth, lanes), BF16)] * (1 if pair_axis else 2)
        outs = [jax.ShapeDtypeStruct(*o) for o in outs]
        return pl.pallas_call(
            functools.partial(first_kernel, heads, channels, places),
            grid=(1,),
            in_specs=[whole(features), whole(labels_across), *specs],
            out_specs=[whole(o) for o in outs],
            out_shape=outs,
            scratch_shapes=[
                pltpu.VMEM((len(places) * tokens, lanes), F32),
                pltpu.VMEM((2, rows * SHIFT, lanes), F32),
            ],
            compiler_params=params(),
            cost_estimate=cost(len(places) * breadth // WIN * VAR_DEV),
            name=name,
        )(features, labels_across, *arrays)

    y_ends, left_ends, right_ends, *own_ends = block_one((0, strips - 1), "block_one_ends")
    top, bottom = swapped(*own_ends, "ty") if pair_axis else exchanged(*own_ends[::-1], "ty")
    y_middle, left_middle, right_middle = block_one(tuple(range(1, strips - 1)), "block_one_middle")
    half = WIN * SHIFT
    strips_out = []
    for ends, middle, cut in (
        (right_ends, right_middle, slice(breadth - SHIFT, breadth)),
        (left_ends, left_middle, slice(0, SHIFT)),
    ):
        corners = [a[:, :, cut].reshape(VAR_DEV, SHIFT * SHIFT, lanes) for a in (top, bottom)]
        strips_out.append(
            jnp.concatenate(
                [corners[0], ends[:, :half], middle, ends[:, half:], corners[1]], axis=1
            )
        )
    sides = exchanged(*strips_out, "tx")

    arrays, specs = block_specs(1)
    inner_count = (strips - 1) * (breadth // WIN - 1)
    group = next(g for g in range(24, 0, -1) if inner_count % g == 0)
    inner, marks = pl.pallas_call(
        functools.partial(inner_kernel, heads, channels, group),
        grid=(inner_count // group,),
        in_specs=[whole(y_ends), whole(y_middle), *specs],
        out_specs=[
            pl.BlockSpec((group, VAR_DEV, CELLS, lanes), lambda i: (i, 0, 0, 0)),
            pl.BlockSpec((strips, tokens, LANES), lambda i: (0, 0, 0)),
        ],
        out_shape=[
            jax.ShapeDtypeStruct((inner_count, VAR_DEV, CELLS, lanes), BF16),
            jax.ShapeDtypeStruct((strips, tokens, LANES), BF16),
        ],
        scratch_shapes=[
            pltpu.VMEM((height, breadth, lanes), F32),
            pltpu.VMEM((inner_count, VAR_DEV, CELLS, lanes), F32),
        ],
        compiler_params=params(),
        cost_estimate=cost(inner_count * VAR_DEV),
        name="block_two_inner",
    )(y_ends, y_middle, *arrays)

    tall, wide = height + 2 * SHIFT, breadth + 2 * SHIFT
    slots = 2 * (tall + wide) // WIN - 4
    group = next(g for g in range(24, 0, -1) if slots % g == 0)
    operands = (y_ends, y_middle, top, bottom, *sides, inner)
    partial_shape = jax.ShapeDtypeStruct((strips, out_channels, tokens), BF16)
    partial = pl.pallas_call(
        functools.partial(outer_kernel, heads, channels, group),
        grid=(1,),
        in_specs=[*[whole(a) for a in operands], *specs, whole(recon)],
        out_specs=whole(partial_shape),
        out_shape=partial_shape,
        scratch_shapes=[
            pltpu.VMEM((WIN, wide, lanes), F32),
            pltpu.VMEM((height, 2 * WIN, lanes), F32),
            pltpu.VMEM((slots, VAR_DEV, CELLS, lanes), F32),
            pltpu.VMEM((slots, VAR_DEV, CELLS, lanes), BF16),
            pltpu.VMEM((tall + WIN, wide, lanes), F32),
        ],
        compiler_params=params(),
        name="block_two_border",
    )(*operands, *arrays, recon)

    parts = lax.all_gather(partial, "var", axis=0)
    colours = out_channels // (SCALE * SCALE)
    chunk = next(c for c in (8, 4, 2, 1) if strips % c == 0)
    operands = (parts, marks, refine_grid, refine_qvt, refine_key, refine_projt)
    in_specs = [whole(a) for a in operands]
    in_specs[0] = pl.BlockSpec(
        (parts.shape[0], chunk, out_channels, tokens), lambda i: (0, i, 0, 0)
    )
    in_specs[1] = pl.BlockSpec((chunk, tokens, LANES), lambda i: (i, 0, 0))
    return pl.pallas_call(
        functools.partial(refine_kernel, refine_heads, channels % LANES),
        grid=(strips // chunk,),
        in_specs=in_specs,
        out_specs=pl.BlockSpec(
            (colours, chunk * WIN * SCALE, breadth * SCALE), lambda i: (0, i, 0)
        ),
        out_shape=jax.ShapeDtypeStruct((colours, height * SCALE, breadth * SCALE), F32),
        scratch_shapes=[pltpu.VMEM((tokens, tokens * SCALE), BF16)],
        compiler_params=params(),
        name="refinement",
    )(*operands)


def solution(mesh):
    placed = (P("ty", "tx", None), P("ty", "tx"), P(), P(), P(), P(), P(), P(), P(), P(), P())
    return jax.shard_map(
        local, mesh=mesh, in_specs=placed, out_specs=P(None, "ty", "tx"), check_vma=False
    )
```

```python
import functools

import jax
import jax.numpy as jnp
from jax import lax
from jax.experimental import pallas as pl
from jax.experimental.pallas import tpu as pltpu
from jax.sharding import PartitionSpec as P

WIN = 8
CELLS = WIN * WIN
SHIFT = 4
SCALE = 4
VAR_DEV = 2
CODES = 8
LANES = 128
HEAD_ROWS = 32
CLASSES = 4
MARKS = CLASSES + 2
SIDE = 2 * WIN - 1

EPSILON = 1e-05
LOG2E = 1.4426950408889634
BIG = float(2.0**100)
ERF_TANH = (0.7975076, 0.0370060, -0.00035159)
REACH = 36.0

NN = (((1,), (0,)), ((), ()))
NT = (((1,), (1,)), ((), ()))
F32 = jnp.float32
BF16 = jnp.bfloat16


def dot(a, b, dims=NN):
    return lax.dot_general(a, b, dims, preferred_element_type=F32)


def iota(shape, dim):
    return lax.broadcasted_iota(jnp.int32, shape, dim)


def round_up(size, multiple):
    return -(-size // multiple) * multiple


def one_hot(condition):
    return jnp.where(condition, 1.0, 0.0).astype(BF16)


def exact(a, b, dims=NN):
    return dot(a, b, dims).astype(BF16)


def pad_matrix(rows, size):
    return one_hot(iota((rows, size), 0) == iota((rows, size), 1))


def head_matrix(rows, size, heads, width, first=0):
    row = iota((rows, size), 0)
    unit = row % HEAD_ROWS
    source = first + row // HEAD_ROWS * width + unit
    keep = (unit < width) & (row < heads * HEAD_ROWS)
    return one_hot(keep & (iota((rows, size), 1) == source))


def query_labels(rows, lanes, first_row, first_lane):
    row = iota((rows, lanes), 0) - first_row
    lane = iota((rows, lanes), 1) - first_lane
    is_class = (row >= 0) & (row < CLASSES)
    is_pad = row == CLASSES
    same = is_class & (row == lane)
    always = lane == CLASSES + 1
    return jnp.where(same, BIG, 0.0) - jnp.where(always & (is_class | is_pad), BIG, 0.0)


def key_labels(rows, lanes, first_row, first_lane):
    row = iota((rows, lanes), 0) - first_row
    lane = iota((rows, lanes), 1) - first_lane
    is_class = (lane >= 0) & (lane < CLASSES)
    is_pad = lane == CLASSES
    add = is_class & (row == lane) | is_pad & (row == CLASSES + 1)
    return jnp.where(add, 1.0, 0.0) - jnp.where(is_pad & (row == CLASSES), 1.0, 0.0)


def bias_rows(table, turn, flip_rows, flip_cols):
    shape = (1, WIN * LANES)
    lane = iota(shape, 1)
    row_step = lane % LANES // WIN - (WIN - 1)
    col_step = lane % WIN - lane // LANES
    row_step = jnp.where(flip_rows, -row_step, row_step)
    col_step = jnp.where(flip_cols, -col_step, col_step)
    lead = jnp.where(turn, col_step, row_step)
    trail = jnp.where(turn, row_step, col_step)
    index = (lead + WIN - 1) * SIDE + trail + WIN - 1
    pick = one_hot(iota((table.shape[1], WIN * LANES), 0) == index)
    rest = table * LOG2E
    parts = []
    for _ in range(3):
        parts.append(rest.astype(BF16))
        rest = rest - parts[-1].astype(F32)
    moved = dot(jnp.concatenate(parts, axis=0), pick)
    size = table.shape[0]
    return moved[:size] + moved[size : 2 * size] + moved[2 * size :]


def bias_grid(rows, rows_ref, store):
    heads = rows.shape[0]
    for key_col in range(WIN):
        rows_ref[0:heads, key_col, :] = rows[:, key_col * LANES : (key_col + 1) * LANES]
    half = iota((WIN, LANES), 1)
    for pair in range(heads // 2):
        even, odd = rows_ref[2 * pair], rows_ref[2 * pair + 1]
        for key_row in range(WIN):
            start = (WIN - 1 - key_row) * WIN
            left = pltpu.roll(even, (LANES - start) % LANES, 1)
            right = pltpu.roll(odd, (LANES - start + CELLS) % LANES, 1)
            store(key_row, pair, jnp.where(half < CELLS, left, right))


def prepare_kernel(
    heads,
    qkv_ref,
    proj_ref,
    up_ref,
    down_ref,
    swin_bias_ref,
    recon_ref,
    refine_qkv_ref,
    refine_proj_ref,
    refine_bias_ref,
    qvt_out,
    key_out,
    proj_out,
    up_out,
    down_out,
    recon_out,
    bias_out,
    refine_qvt_out,
    refine_key_out,
    refine_proj_out,
    refine_bias_out,
    rows_ref,
    tables_ref,
):
    blocks, channels, hidden = up_ref.shape
    width = channels // heads
    lanes = key_out.shape[1]
    head_rows = heads * HEAD_ROWS
    mark_rows = head_rows + 16
    taps, out, _ = recon_ref.shape
    refine_heads = refine_bias_ref.shape[0]
    refine_width = out // refine_heads
    refine_rows = refine_heads * HEAD_ROWS
    mark = channels % LANES
    pad = one_hot(iota((lanes, channels), 0) == iota((lanes, channels), 1))

    for i in range(blocks):
        tables_ref[i * heads : (i + 1) * heads] = swin_bias_ref[:, i]
    rows, moved = [], []
    kernel = recon_ref[...].reshape(taps * out, channels)
    for v in range(VAR_DEV):
        code = lax.axis_index("var") * VAR_DEV + v
        turn, flip_rows, flip_cols = code // 4 == 1, code // 2 % 2 == 1, code % 2 == 1
        rows.append(bias_rows(tables_ref[: blocks * heads], turn, flip_rows, flip_cols))
        shape = (3 * lanes, 1)
        row = iota(shape, 0)
        row_step = row // lanes - 1
        lane = row % lanes
        col_step = jnp.where(lane >= LANES, 1, jnp.where(lane >= out, 0, -1))
        channel = jnp.where(lane >= LANES, lane - LANES, jnp.where(lane >= out, lane - out, lane))
        row_step = jnp.where(flip_rows, -row_step, row_step)
        col_step = jnp.where(flip_cols, -col_step, col_step)
        tap = (jnp.where(turn, col_step, row_step) + 1) * 3
        tap = tap + jnp.where(turn, row_step, col_step) + 1
        sub_row = channel % (SCALE * SCALE) // SCALE
        sub_col = channel % SCALE
        sub_row = jnp.where(flip_rows, SCALE - 1 - sub_row, sub_row)
        sub_col = jnp.where(flip_cols, SCALE - 1 - sub_col, sub_col)
        source = channel // (SCALE * SCALE) * SCALE * SCALE
        source = source + jnp.where(turn, sub_col, sub_row) * SCALE
        source = tap * out + source + jnp.where(turn, sub_row, sub_col)
        source = jnp.where(channel < out, source, -1)
        moved.append(exact(one_hot(iota((3 * lanes, taps * out), 1) == source), kernel))
    never = lax.axis_index("var") < 0
    refine_table = bias_rows(refine_bias_ref[...], never, never, never)
    keys = [
        exact(qkv_ref[i], head_matrix(lanes, 3 * channels, heads, width, channels), NT)
        for i in range(blocks)
    ]
    weight = refine_qkv_ref[...]
    refine_queries = exact(
        head_matrix(refine_rows + 16, 3 * out, refine_heads, refine_width), weight, NT
    )
    refine_values = exact(
        head_matrix(refine_rows, 3 * out, refine_heads, refine_width, 2 * out), weight, NT
    )
    refine_keys = exact(head_matrix(LANES, 3 * out, refine_heads, refine_width, out), weight, NT)
    refine_proj = []
    for h in range(refine_heads):
        shape = (LANES, out)
        row = iota(shape, 0)
        pick = one_hot((row < refine_width) & (iota(shape, 1) == row + h * refine_width))
        refine_proj.append(exact(pick, refine_proj_ref[...]))

    queries = head_matrix(mark_rows, 3 * channels, heads, width)
    values = head_matrix(head_rows, 3 * channels, heads, width, 2 * channels)
    query_add = query_labels(mark_rows, lanes, head_rows, channels).astype(BF16)
    key_add = key_labels(lanes, lanes, channels, head_rows)
    shape = (2 * LANES, channels)
    row = iota(shape, 0)
    head, unit = row % LANES // HEAD_ROWS * 2 + row // LANES, row % HEAD_ROWS
    proj_rows = one_hot((head < heads) & (unit < width) & (iota(shape, 1) == head * width + unit))
    shape = (down_out.shape[1], hidden)
    down_rows = one_hot(iota(shape, 0) == iota(shape, 1))
    for i in range(blocks):
        for ref in (qvt_out, proj_out, up_out, down_out):
            ref[i] = jnp.zeros(ref.shape[1:], BF16)
        qvt_out[i, :mark_rows] = query_add
        qvt_out[i, :mark_rows, :channels] = exact(queries, qkv_ref[i], NT)
        qvt_out[i, mark_rows:, :channels] = exact(values, qkv_ref[i], NT)
        proj_out[i, :, :channels] = exact(proj_rows, proj_ref[i])
        up_out[i, :, :hidden] = exact(pad, up_ref[i])
        down_out[i, :, :channels] = exact(down_rows, down_ref[i], NT)

    for i in range(blocks):
        key_out[i] = (dot(pad, keys[i]) + key_add).astype(BF16)
    for v in range(VAR_DEV):
        recon_out[v] = exact(pad, moved[v], NT)
    out_pad = one_hot(iota((LANES, out), 0) == iota((LANES, out), 1))
    refine_qvt_out[: refine_rows + 16] = (
        dot(refine_queries, out_pad, NT)
        + query_labels(refine_rows + 16, LANES, refine_rows, mark)
    ).astype(BF16)
    refine_qvt_out[refine_rows + 16 :] = exact(refine_values, out_pad, NT)
    refine_key_out[...] = (
        dot(out_pad, refine_keys, NT) + key_labels(LANES, LANES, mark, refine_rows)
    ).astype(BF16)
    for h in range(refine_heads):
        square = dot(refine_proj[h], out_pad, NT)
        refine_proj_out[h * out : (h + 1) * out] = square.T[:out].astype(BF16)
    for v in range(VAR_DEV):
        for i in range(blocks):

            def store(key_row, pair, value):
                at = slice(key_row * WIN, (key_row + 1) * WIN)
                bias_out[i, v, at, pair * LANES : (pair + 1) * LANES] = value

            bias_grid(rows[v][i * heads : (i + 1) * heads], rows_ref, store)

    def store_refine(key_row, pair, value):
        refine_bias_out[key_row * WIN : (key_row + 1) * WIN] = value

    bias_grid(refine_table, rows_ref, store_refine)


def gelu(x):
    x = x.astype(BF16)
    square = jnp.minimum(x * x, BF16(REACH))
    first, second, third = (BF16(factor) for factor in ERF_TANH)
    series = (square * third + second) * square + first
    half = BF16(0.5) * x
    return half + half * jnp.tanh(x * series)


def normalize(x, channels):
    inside = iota((1, x.shape[1]), 1) < channels
    mean = jnp.sum(jnp.where(inside, x, 0.0), axis=1, keepdims=True) * (1.0 / channels)
    centred = jnp.where(inside, x - mean, 0.0)
    spread = jnp.sum(centred * centred, axis=1, keepdims=True) * (1.0 / channels)
    return jnp.where(inside, centred * lax.rsqrt(spread + EPSILON), x).astype(BF16)


def split_queries(queries, heads):
    pairs = heads // 2
    head_rows = heads * HEAD_ROWS
    left = iota((1, LANES), 1) < CELLS
    turned = pltpu.roll(queries, CELLS, 1).astype(BF16)
    queries = queries.astype(BF16)
    depth = round_up(queries.shape[0], LANES)
    zero = jnp.zeros((HEAD_ROWS, LANES), BF16)
    results = []
    for even, odd in ((queries, turned), (turned, queries)):
        marks = jnp.where(left, even[head_rows:], odd[head_rows:])
        columns = []
        for pair in range(pairs):
            at = pair * 2 * HEAD_ROWS
            rows = [zero] * heads
            rows[2 * pair] = jnp.where(left, even[at : at + HEAD_ROWS], zero)
            rows[2 * pair + 1] = jnp.where(left, zero, odd[at + HEAD_ROWS : at + 2 * HEAD_ROWS])
            rows.append(marks)
            rows.append(jnp.zeros((depth - queries.shape[0], LANES), BF16))
            columns.append(jnp.concatenate(rows, axis=0))
        results.append(jnp.concatenate(columns, axis=1) if pairs > 1 else columns[0])
    return results


def heads_of(n, scale, heads, width, w_qvt, w_key):
    mark_rows = heads * HEAD_ROWS + 16
    both = dot(w_qvt, n, NT)
    row = iota((mark_rows, 1), 0)
    queries = both[:mark_rows] * jnp.where(row < heads * HEAD_ROWS, scale, 1.0)
    values = both[mark_rows:]
    row = iota((heads * HEAD_ROWS, 1), 0) % HEAD_ROWS
    values = jnp.where(row == width, 1.0, values).astype(BF16)
    keys = dot(n, w_key).astype(BF16)
    scores = []
    for place in range(n.shape[0] // LANES):
        cut = slice(place * LANES, (place + 1) * LANES)
        for half, stationary in enumerate(split_queries(queries[:, cut], heads)):
            at = place * LANES + half * CELLS
            scores.append(dot(keys[at : at + CELLS], stationary))
    return scores, values


def soft(scores):
    largest = jnp.max(scores, axis=0, keepdims=True)
    return jnp.exp2(scores - largest).astype(BF16)


def mix_pair(values, first, second, heads, ones_row):
    zero = jnp.zeros((CELLS, LANES), BF16)
    lane = iota((HEAD_ROWS, 2 * LANES), 1) % LANES
    mixed = []
    for pair in range(heads // 2):
        cut = slice(pair * LANES, (pair + 1) * LANES)
        stationary = jnp.concatenate(
            [
                jnp.concatenate([first[:, cut], zero], axis=1),
                jnp.concatenate([zero, second[:, cut]], axis=1),
            ],
            axis=0,
        )
        result = dot(values[pair * CELLS : (pair + 1) * CELLS], stationary)
        joined = jnp.where(lane < CELLS, result[:HEAD_ROWS], result[HEAD_ROWS:])
        mixed.append(joined * pl.reciprocal(joined[ones_row : ones_row + 1]))
    return mixed


def swin_block(x, pairs, heads, channels, bias, w_qvt, w_key, w_proj, w_up, w_down):
    width = channels // heads
    n = normalize(x, channels)
    scale = width**-0.5 * LOG2E
    scores, values = heads_of(n, scale, heads, width, w_qvt[...], w_key[...])
    pad = jnp.zeros((LANES - heads // 2 * HEAD_ROWS, 2 * LANES), F32)
    weights = [
        (soft(scores[2 * place] + bias(a)), soft(scores[2 * place + 1] + bias(b)))
        for place, a, b in pairs
    ]
    blocks = []
    for (place, _, _), (first, second) in zip(pairs, weights):
        cut = slice(place * LANES, (place + 1) * LANES)
        mixed = mix_pair(values[:, cut], first, second, heads, width)
        blocks.append(jnp.concatenate(mixed + [pad], axis=0).astype(BF16))
    outputs = []
    for block in blocks:
        for half in range(2):
            turned = block[:, half * LANES : (half + 1) * LANES].T
            outputs.append(jnp.concatenate([turned[:CELLS], turned[CELLS:]], axis=1))
    outputs = jnp.concatenate(outputs, axis=0)
    places = [place for place, _, _ in pairs]
    if places != list(range(x.shape[0] // LANES)):
        x = jnp.concatenate([x[place * LANES : (place + 1) * LANES] for place in places], axis=0)
    h = (x + dot(outputs, w_proj[...])).astype(BF16).astype(F32)
    hidden = gelu(dot(normalize(h, channels), w_up[...]))
    y = h + dot(hidden, w_down[...])
    return [y[i * LANES : (i + 1) * LANES] for i in range(len(pairs))]


def windows_of(grid):
    lanes = grid.shape[2]
    return jnp.concatenate(
        [
            grid[:, w * WIN : (w + 1) * WIN].reshape(CELLS, lanes)
            for w in range(grid.shape[1] // WIN)
        ],
        axis=0,
    )


def first_kernel(heads, channels, strips, x_ref, labels_ref, bias_ref, *refs):
    ends = strips[0] == 0
    *weights, y_ref, side_a_ref, side_b_ref = refs[:8]
    held, side = refs[-2:]
    breadth = x_ref.shape[1]
    count = breadth // WIN
    tokens, lanes = held.shape
    part = tokens // len(strips)
    rows_total = labels_ref.shape[1]
    for k, strip in enumerate(strips):
        rows = x_ref[strip * WIN : (strip + 1) * WIN].astype(F32)
        held[k * part : (k + 1) * part, :channels] = windows_of(rows)
    token = iota((tokens, rows_total), 0)
    strip = token // part + strips[0]
    if ends:
        strip = jnp.where(token < part, strips[0], strips[1])
    at_row = strip * WIN + token % CELLS // WIN == iota((tokens, rows_total), 1)
    by_row = dot(one_hot(at_row), labels_ref[...].astype(F32).astype(BF16), NT)
    token = iota((tokens, breadth), 0)
    at_col = token % part // CELLS * WIN + token % WIN == iota((tokens, breadth), 1)
    label = dot(jnp.where(at_col, by_row, 0.0).astype(BF16), jnp.ones((breadth, LANES), BF16))
    lane = iota((tokens, LANES), 1) - channels % LANES
    marks = jnp.where(
        (label == (lane + 1).astype(F32)) & (lane < CLASSES)
        | (lane >= CLASSES) & (lane < MARKS),
        1.0,
        0.0,
    )
    tail = jnp.where(lane < 0, held[:, lanes - LANES :], marks)
    x = jnp.concatenate([held[:, : lanes - LANES], tail], axis=1)
    places = tokens // LANES
    pairs = [(place, v, v) for v in range(VAR_DEV) for place in range(places)]
    results = swin_block(x, pairs, heads, channels, lambda v: bias_ref[v], *weights)
    for v in range(VAR_DEV):
        for k in range(len(strips)):
            windows = []
            for w in range(count):
                group = k * count + w
                block = results[v * places + group // 2]
                at = group % 2 * CELLS
                windows.append(block[at : at + CELLS].reshape(WIN, WIN, lanes))
            y_ref[v, k * WIN : (k + 1) * WIN] = jnp.concatenate(windows, axis=1).astype(BF16)
            at = k * WIN * SHIFT
            for r in range(WIN):
                rows = slice(at + r * SHIFT, at + (r + 1) * SHIFT)
                side[0, rows] = windows[0][r, :SHIFT]
                side[1, rows] = windows[-1][r, SHIFT:]
        left, right = side[0].astype(BF16), side[1].astype(BF16)
        even = is_even("tx")
        side_a_ref[v] = jnp.where(even, right, left)
        side_b_ref[v] = jnp.where(even, left, right)
    if ends:
        top, bottom = y_ref[:, :SHIFT], y_ref[:, 2 * WIN - SHIFT :]
        even = is_even("ty")
        refs[8][...] = jnp.where(even, bottom, top)
        if len(refs) == 12:
            refs[9][...] = jnp.where(even, top, bottom)


def place_rows(store, ends_ref, middle_ref, v):
    store(0, ends_ref[v, :WIN])
    for r in range(0, middle_ref.shape[1], WIN):
        store(WIN + r, middle_ref[v, r : r + WIN])
    store(WIN + middle_ref.shape[1], ends_ref[v, WIN:])


def inner_kernel(
    heads, channels, group, ends_ref, middle_ref, bias_ref, *refs
):
    *weights, y_ref, marks_ref, held, x_held = refs
    height, breadth, lanes = held.shape
    count = breadth // WIN - 1

    @pl.when(pl.program_id(0) == 0)
    def _():
        for v in range(VAR_DEV):

            def store(first, rows):
                rows = rows.astype(F32)
                held[first : first + WIN] = rows
                if v == 0:
                    marks_ref[first // WIN] = windows_of(rows[:, :, lanes - LANES :]).astype(BF16)

            place_rows(store, ends_ref, middle_ref, v)
            for strip in range(height // WIN - 1):
                rows = slice(strip * WIN + SHIFT, (strip + 1) * WIN + SHIFT)
                for w in range(count):
                    at = SHIFT + w * WIN
                    x_held[strip * count + w, v] = held[rows, at : at + WIN].reshape(CELLS, lanes)

    base = pl.program_id(0) * group
    x = x_held[pl.ds(base, group)].reshape(group * VAR_DEV * CELLS, lanes)
    pairs = [(w, 0, 1) for w in range(group)]
    results = swin_block(x, pairs, heads, channels, lambda v: bias_ref[v], *weights)
    for w in range(group):
        y_ref[w] = results[w].astype(BF16).reshape(VAR_DEV, CELLS, lanes)


def received(refs, axis, after, place):
    value = refs[0][place].astype(F32)
    other = refs[1][place].astype(F32) if len(refs) > 1 else 0.0
    return jnp.where(is_even(axis) == after, value, other)


def edge_kernel(swaps, *refs):
    across, own, outs = refs[:swaps], refs[swaps : swaps + 4], refs[swaps + 4 :]
    breadth = across[0].shape[2]
    half = WIN * SHIFT
    corner = SHIFT * SHIFT
    for first in range(2):
        ends, middle = own[2 * first : 2 * first + 2]
        out = outs[first]
        at_right = is_even("tx") == (first == 0)
        last = out.shape[1] - corner
        for v in range(VAR_DEV):
            for start, after in ((0, False), (last, True)):
                rows = received(across, "ty", after, v)
                cells = jnp.where(at_right, rows[:, breadth - SHIFT :], rows[:, :SHIFT])
                cells = jnp.concatenate([cells[r] for r in range(SHIFT)], axis=0)
                out[v, start : start + corner] = cells.astype(BF16)
            out[v, corner : corner + half] = ends[v, :half]
            out[v, corner + half : last - half] = middle[v]
            out[v, last - half : last] = ends[v, half:]


def outer_kernel(
    heads,
    channels,
    group,
    swaps,
    ends_ref,
    middle_ref,
    *refs,
):
    across, sides, (inner_ref, bias_ref) = refs[:swaps], refs[swaps : swaps + 2], refs[swaps + 2 : swaps + 4]
    refs = refs[swaps + 4 :]
    *weights, w_recon, keep_ref, give_ref, rows_held, sides_held, x_held, y_held, acc = refs
    lanes = middle_ref.shape[3]
    height, breadth = middle_ref.shape[1] + 2 * WIN, middle_ref.shape[2]
    tall, wide = height + 2 * SHIFT, breadth + 2 * SHIFT
    strips, count = tall // WIN, wide // WIN
    always = iota((1, lanes), 1) == channels + CLASSES + 1

    def marked(refs, axis, after, place):
        return jnp.where(always, 1.0, received(refs, axis, after, place))

    for v in range(VAR_DEV):
        for end in range(2):
            outside, inside = (0, SHIFT) if end == 0 else (SHIFT, 0)
            corner = 0 if end == 0 else (tall - SHIFT) * SHIFT
            first = 0 if end == 0 else 2 * WIN - SHIFT
            between = slice(SHIFT, SHIFT + breadth)
            rows_held[outside : outside + SHIFT, between] = marked(
                across, "ty", end == 1, v
            )
            rows_held[inside : inside + SHIFT, between] = ends_ref[
                v, first : first + SHIFT
            ].astype(F32)
            side_first = SHIFT * SHIFT if end == 0 else (tall - 2 * SHIFT) * SHIFT
            for side, at in ((0, 0), (1, wide - SHIFT)):
                for rows, start in ((outside, corner), (inside, side_first)):
                    cut = (v, slice(start, start + SHIFT * SHIFT))
                    piece = marked(sides, "tx", side == 1, cut)
                    rows_held[rows : rows + SHIFT, at : at + SHIFT] = piece.reshape(
                        SHIFT, SHIFT, lanes
                    )
            for w in range(count):
                x_held[end * count + w, v] = rows_held[:, w * WIN : (w + 1) * WIN].reshape(
                    CELLS, lanes
                )

        def store(first, rows):
            sides_held[first : first + WIN, :WIN] = rows[:, :WIN].astype(F32)
            sides_held[first : first + WIN, WIN:] = rows[:, breadth - WIN :].astype(F32)

        place_rows(store, ends_ref, middle_ref, v)
        for strip in range(1, strips - 1):
            rows = slice(strip * WIN - SHIFT, (strip + 1) * WIN - SHIFT)
            cut = slice(strip * WIN * SHIFT, (strip + 1) * WIN * SHIFT)
            for end in range(2):
                piece = marked(sides, "tx", end == 1, (v, cut))
                piece = piece.reshape(WIN, SHIFT, lanes)
                at = 0 if end == 0 else WIN + SHIFT
                own = sides_held[rows, at : at + SHIFT]
                both = [piece, own] if end == 0 else [own, piece]
                slot = 2 * count + 2 * (strip - 1) + end
                x_held[slot, v] = jnp.concatenate(both, axis=1).reshape(CELLS, lanes)

    slots = x_held.shape[0]

    def border(step, carry):
        x = x_held[pl.ds(step * group, group)].reshape(group * VAR_DEV * CELLS, lanes)
        pairs = [(w, 0, 1) for w in range(group)]
        results = swin_block(x, pairs, heads, channels, lambda v: bias_ref[v], *weights)
        at = channels + CLASSES
        for w in range(group):
            block = x[w * LANES : (w + 1) * LANES]
            y = results[w] * block[:, at : at + 1]
            y_held[step * group + w] = y.astype(BF16).reshape(VAR_DEV, CELLS, lanes)
        return carry

    lax.fori_loop(0, slots // group, border, 0)

    weights = w_recon[...].reshape(VAR_DEV * lanes, 3 * lanes)

    def scatter(strip, windows):
        tokens = [jnp.concatenate(windows(v), axis=0) for v in range(VAR_DEV)]
        total = dot(jnp.concatenate(tokens, axis=1), weights)
        total = total.reshape(count, WIN, WIN, 3 * lanes)
        for e in range(3):
            rows = slice(strip * WIN + 2 - e, (strip + 1) * WIN + 2 - e)
            for w in range(count):
                across = slice(w * WIN, (w + 1) * WIN)
                part = total[w, :, :, e * lanes : (e + 1) * lanes]
                acc[rows, across] = part if e == 0 else acc[rows, across] + part

    out_channels = keep_ref.shape[1]

    def finish(strip):
        rows = slice(1 + SHIFT + strip * WIN, 1 + SHIFT + (strip + 1) * WIN)
        centre = acc[rows, SHIFT : SHIFT + breadth, :LANES]
        centre = pltpu.roll(centre.reshape(WIN * breadth, LANES), LANES - out_channels, 1)
        result = (
            acc[rows, SHIFT - 1 : SHIFT - 1 + breadth, :LANES]
            + centre.reshape(WIN, breadth, LANES)
            + acc[rows, SHIFT + 1 : SHIFT + 1 + breadth, LANES : 2 * LANES]
        )
        return windows_of(result).T[:out_channels].astype(BF16)

    results = []
    scatter(0, lambda v: [y_held[w, v] for w in range(count)])
    for strip in range(1, strips):
        if strip == strips - 1:
            scatter(strip, lambda v: [y_held[count + w, v] for w in range(count)])
        else:
            slot = 2 * count + 2 * (strip - 1)
            first = (strip - 1) * (count - 2)
            scatter(
                strip,
                lambda v: [
                    y_held[slot, v],
                    *[inner_ref[first + w, v] for w in range(count - 2)],
                    y_held[slot + 1, v],
                ],
            )
        results.append(finish(strip - 1))
    half = len(results) // 2
    even = is_even("var")
    for strip in range(half):
        keep_ref[strip] = jnp.where(even, results[strip], results[strip + half])
        give_ref[strip] = jnp.where(even, results[strip + half], results[strip])


def refine_kernel(
    heads, first_mark, mine_ref, other_ref, marks_ref, bias_ref, w_qvt, w_key, w_projt, out_ref, final
):
    strips, channels, strip_tokens = mine_ref.shape
    breadth = strip_tokens // WIN
    width = channels // heads
    z = jnp.concatenate(
        [mine_ref[s].astype(F32) + other_ref[s].astype(F32) for s in range(strips)], axis=1
    ) * (1.0 / CODES)
    mean = jnp.sum(z, axis=0, keepdims=True) * (1.0 / channels)
    centred = z - mean
    spread = jnp.sum(centred * centred, axis=0, keepdims=True) * (1.0 / channels)
    normed = centred * lax.rsqrt(spread + EPSILON)
    tall = jnp.concatenate([normed, jnp.zeros((LANES - channels, normed.shape[1]), F32)], axis=0)
    first = lax.axis_index("var") % 2 * strips
    marks = jnp.concatenate([marks_ref[first + s].astype(F32) for s in range(strips)], axis=0)
    lane = iota((1, LANES), 1)
    is_mark = (lane >= first_mark) & (lane < first_mark + MARKS)
    n = jnp.where(is_mark, marks, tall.T).astype(BF16)
    scores, values = heads_of(
        n, width**-0.5 * LOG2E, heads, width, w_qvt[...], w_key[...]
    )
    probabilities = [soft(s + bias_ref[...]) for s in scores]
    lane = iota((channels, LANES), 1)
    branches = []
    for pair in range(len(probabilities) // 2):
        mixed = mix_pair(
            values[:, pair * LANES : (pair + 1) * LANES],
            probabilities[2 * pair],
            probabilities[2 * pair + 1],
            heads,
            width,
        )[0].astype(BF16)
        both = dot(w_projt[...][:, :HEAD_ROWS], mixed)
        even, odd = both[:channels], both[channels:]
        halves = []
        for half in range(2):
            cut = slice(half * LANES, (half + 1) * LANES)
            halves.append(even[:, cut] + pltpu.roll(odd[:, cut], CELLS, 1))
        branches.append(jnp.where(lane < CELLS, halves[0], pltpu.roll(halves[1], CELLS, 1)))
    refined = (z + jnp.concatenate(branches, axis=1)).astype(BF16)
    stacked = jnp.concatenate(
        [refined[:, s * strip_tokens : (s + 1) * strip_tokens] for s in range(strips)], axis=0
    )
    shape = (strip_tokens, WIN * breadth * SCALE)
    cell = iota(shape, 1) // SCALE
    source = (cell % breadth // WIN) * CELLS + (cell // breadth) * WIN + cell % WIN
    wide = dot(stacked, one_hot(iota(shape, 0) == source))
    own = iota(wide.shape, 1) % SCALE == iota(wide.shape, 0) % SCALE
    wide = jnp.where(own, wide, 0.0).astype(BF16)
    shape = (wide.shape[0] // SCALE, wide.shape[0])
    folded = dot(one_hot(iota(shape, 1) // SCALE == iota(shape, 0)), wide)
    colours = channels // (SCALE * SCALE)
    row_lanes = breadth * SCALE
    for s in range(strips):
        for c in range(colours):
            first = (s * colours + c) * SCALE
            for y in range(WIN):
                start = (s * WIN + y) * SCALE
                final[c, start : start + SCALE] = folded[
                    first : first + SCALE, y * row_lanes : (y + 1) * row_lanes
                ]
    out_ref[...] = final[...].astype(BF16)


def is_even(axis):
    return lax.axis_index(axis) % 2 == 0


def swap_pairs(strip, axis, first):
    count = lax.axis_size(axis)
    pairs = [(i, i + 1) for i in range(first, count - 1, 2)]
    return lax.ppermute(strip, axis, pairs + [(j, i) for i, j in pairs])


def whole_swap(a, bit):
    count = lax.axis_size("var")
    return lax.ppermute(a, "var", [(i, i ^ bit) for i in range(count)])


def whole(a):
    return pl.BlockSpec(a.shape, lambda *i: (0,) * a.ndim)


def params(mebibytes):
    return pltpu.CompilerParams(
        dimension_semantics=("arbitrary",), vmem_limit_bytes=mebibytes * 1024 * 1024
    )


def local(
    features,
    labels,
    qkv_weight,
    proj_weight,
    up_weight,
    down_weight,
    swin_bias,
    recon_weight,
    refine_qkv,
    refine_proj,
    refine_bias,
):
    height, breadth, channels = features.shape
    heads = swin_bias.shape[1]
    out_channels = recon_weight.shape[-1]
    refine_heads = refine_bias.shape[0]
    lanes = round_up(channels + MARKS, LANES)
    hidden = round_up(up_weight.shape[-1], LANES)
    operands = (
        qkv_weight,
        proj_weight,
        up_weight,
        jnp.swapaxes(down_weight, 1, 2),
        jnp.swapaxes(swin_bias, 0, 1),
        jnp.swapaxes(recon_weight, 1, 2),
        refine_qkv,
        refine_proj,
        refine_bias,
    )
    head_rows, refine_rows = heads * HEAD_ROWS, refine_heads * HEAD_ROWS
    shapes = [
        ((2, 2 * head_rows + 16, lanes), BF16),
        ((2, lanes, lanes), BF16),
        ((2, 2 * LANES, lanes), BF16),
        ((2, lanes, hidden), BF16),
        ((2, hidden, lanes), BF16),
        ((VAR_DEV, lanes, 3 * lanes), BF16),
        ((2, VAR_DEV, CELLS, heads * CELLS), F32),
        ((2 * refine_rows + 16, LANES), BF16),
        ((LANES, LANES), BF16),
        ((refine_heads * out_channels, LANES), BF16),
        ((CELLS, refine_heads * CELLS), F32),
    ]
    shapes = [jax.ShapeDtypeStruct(*s) for s in shapes]
    prepared = pl.pallas_call(
        functools.partial(prepare_kernel, heads),
        grid=(1,),
        in_specs=[whole(a) for a in operands],
        out_specs=[whole(s) for s in shapes],
        out_shape=shapes,
        scratch_shapes=[
            pltpu.VMEM((heads, WIN, LANES), F32),
            pltpu.VMEM((round_up(2 * heads, 8), swin_bias.shape[2]), F32),
        ],
        compiler_params=params(10),
        name="prepare",
    )(*operands)
    *swin, recon, bias, refine_qvt, refine_key, refine_projt, refine_grid = prepared

    def block_specs(i):
        arrays = (bias, *swin)
        return arrays, [
            pl.BlockSpec((None,) + a.shape[1:], lambda *_, n=a.ndim: (i,) + (0,) * (n - 1))
            for a in arrays
        ]

    def cost(windows):
        return pl.CostEstimate(
            flops=windows * 400_000_000, bytes_accessed=windows * 200_000, transcendentals=0
        )

    arrays, specs = block_specs(0)
    strips = height // WIN
    tokens = WIN * breadth
    labels_across = labels.T

    pair_axis = lax.axis_size("ty") == 2

    def block_one(places, name):
        rows = len(places) * WIN
        outs = [
            ((VAR_DEV, rows, breadth, lanes), BF16),
            ((VAR_DEV, rows * SHIFT, lanes), BF16),
            ((VAR_DEV, rows * SHIFT, lanes), BF16),
        ]
        if places[0] == 0:
            outs += [((VAR_DEV, SHIFT, breadth, lanes), BF16)] * (1 if pair_axis else 2)
        outs = [jax.ShapeDtypeStruct(*o) for o in outs]
        return pl.pallas_call(
            functools.partial(first_kernel, heads, channels, places),
            grid=(1,),
            in_specs=[whole(features), whole(labels_across), *specs],
            out_specs=[whole(o) for o in outs],
            out_shape=outs,
            scratch_shapes=[
                pltpu.VMEM((len(places) * tokens, lanes), F32),
                pltpu.VMEM((2, rows * SHIFT, lanes), F32),
            ],
            compiler_params=params(12 if places[0] == 0 else 18),
            cost_estimate=cost(len(places) * breadth // WIN * VAR_DEV),
            name=name,
        )(features, labels_across, *arrays)

    y_ends, a_ends, b_ends, *own_ends = block_one((0, strips - 1), "block_one_ends")
    across = [swap_pairs(own, "ty", first) for first, own in enumerate(own_ends)]
    y_middle, a_middle, b_middle = block_one(tuple(range(1, strips - 1)), "block_one_middle")
    operands = (*across, a_ends, a_middle, b_ends, b_middle)
    strip_shape = jax.ShapeDtypeStruct((VAR_DEV, (height + 2 * SHIFT) * SHIFT, lanes), BF16)
    strips_out = pl.pallas_call(
        functools.partial(edge_kernel, len(across)),
        grid=(1,),
        in_specs=[whole(a) for a in operands],
        out_specs=[whole(strip_shape)] * 2,
        out_shape=[strip_shape] * 2,
        compiler_params=params(6),
        name="edges",
    )(*operands)
    sides = [swap_pairs(strip, "tx", first) for first, strip in enumerate(strips_out)]

    arrays, specs = block_specs(1)
    inner_count = (strips - 1) * (breadth // WIN - 1)
    group = next(g for g in range(24, 0, -1) if inner_count % g == 0)
    inner, marks = pl.pallas_call(
        functools.partial(inner_kernel, heads, channels, group),
        grid=(inner_count // group,),
        in_specs=[whole(y_ends), whole(y_middle), *specs],
        out_specs=[
            pl.BlockSpec((group, VAR_DEV, CELLS, lanes), lambda i: (i, 0, 0, 0)),
            pl.BlockSpec((strips, tokens, LANES), lambda i: (0, 0, 0)),
        ],
        out_shape=[
            jax.ShapeDtypeStruct((inner_count, VAR_DEV, CELLS, lanes), BF16),
            jax.ShapeDtypeStruct((strips, tokens, LANES), BF16),
        ],
        scratch_shapes=[
            pltpu.VMEM((height, breadth, lanes), F32),
            pltpu.VMEM((inner_count, VAR_DEV, CELLS, lanes), F32),
        ],
        compiler_params=params(20),
        cost_estimate=cost(inner_count * VAR_DEV),
        name="block_two_inner",
    )(y_ends, y_middle, *arrays)

    tall, wide = height + 2 * SHIFT, breadth + 2 * SHIFT
    slots = 2 * (tall + wide) // WIN - 4
    group = next(g for g in range(24, 0, -1) if slots % g == 0)
    operands = (y_ends, y_middle, *across, *sides, inner)
    half_shape = jax.ShapeDtypeStruct((strips // 2, out_channels, tokens), BF16)
    keep, give = pl.pallas_call(
        functools.partial(outer_kernel, heads, channels, group, len(across)),
        grid=(1,),
        in_specs=[*[whole(a) for a in operands], *specs, whole(recon)],
        out_specs=[whole(half_shape)] * 2,
        out_shape=[half_shape] * 2,
        scratch_shapes=[
            pltpu.VMEM((WIN, wide, lanes), F32),
            pltpu.VMEM((height, 2 * WIN, lanes), F32),
            pltpu.VMEM((slots, VAR_DEV, CELLS, lanes), F32),
            pltpu.VMEM((slots, VAR_DEV, CELLS, lanes), BF16),
            pltpu.VMEM((tall + WIN, wide, lanes), F32),
        ],
        compiler_params=params(26),
        name="block_two_border",
    )(*operands, *arrays, recon)

    mine = (keep.astype(F32) + whole_swap(give, 1).astype(F32)).astype(BF16)
    other = whole_swap(mine, 2)
    colours = out_channels // (SCALE * SCALE)
    operands = (mine, other, marks, refine_grid, refine_qvt, refine_key, refine_projt)
    out_shape = (colours, height * SCALE // 2, breadth * SCALE)
    refined = pl.pallas_call(
        functools.partial(refine_kernel, refine_heads, channels % LANES),
        grid=(1,),
        in_specs=[whole(a) for a in operands],
        out_specs=pl.BlockSpec(out_shape, lambda i: (0, 0, 0)),
        out_shape=jax.ShapeDtypeStruct(out_shape, BF16),
        scratch_shapes=[pltpu.VMEM(out_shape, F32)],
        compiler_params=params(8),
        name="refinement",
    )(*operands)
    received = whole_swap(refined, 1)
    even = is_even("var")
    halves = jnp.where(even, refined, received), jnp.where(even, received, refined)
    return jnp.concatenate(halves, axis=1).astype(F32)


def solution(mesh):
    placed = (P("ty", "tx", None), P("ty", "tx"), P(), P(), P(), P(), P(), P(), P(), P(), P())
    return jax.shard_map(
        local, mesh=mesh, in_specs=placed, out_specs=P(None, "ty", "tx"), check_vma=False
    )
```

```python
import functools

import jax
import jax.numpy as jnp
from jax import lax
from jax.experimental import pallas as pl
from jax.experimental.pallas import tpu as pltpu
from jax.sharding import PartitionSpec as P

WIN = 8
CELLS = WIN * WIN
SHIFT = 4
SCALE = 4
VAR_DEV = 2
CODES = 8
LANES = 128
HEAD_ROWS = 32
CLASSES = 4
MARKS = CLASSES + 2
CONSTANT = -2.0
SIDE = 2 * WIN - 1

EPSILON = 1e-05
LOG2E = 1.4426950408889634
BIG = float(2.0**100)
ERF_TANH = (0.7975076, 0.0370060, -0.00035159)
REACH = 36.0

NN = (((1,), (0,)), ((), ()))
NT = (((1,), (1,)), ((), ()))
F32 = jnp.float32
BF16 = jnp.bfloat16


def dot(a, b, dims=NN):
    return lax.dot_general(a, b, dims, preferred_element_type=F32)


def iota(shape, dim):
    return lax.broadcasted_iota(jnp.int32, shape, dim)


def round_up(size, multiple):
    return -(-size // multiple) * multiple


def one_hot(condition):
    return jnp.where(condition, 1.0, 0.0).astype(BF16)


def exact(a, b, dims=NN):
    return dot(a, b, dims).astype(BF16)


def pick_rows(source, size):
    return one_hot(iota((1, size), 1) == source)


def pick_columns(source, size):
    return one_hot(iota((size, 1), 0) == source)


def head_source(index, heads, width, first=0):
    unit = index % HEAD_ROWS
    keep = (unit < width) & (index < heads * HEAD_ROWS)
    return jnp.where(keep, first + index // HEAD_ROWS * width + unit, -1)


def query_value_source(heads, width, channels):
    row = iota((2 * heads * HEAD_ROWS + 16, 1), 0)
    values = row - heads * HEAD_ROWS - 16
    return jnp.where(
        values < 0,
        head_source(row, heads, width),
        head_source(jnp.maximum(values, 0), heads, width, 2 * channels),
    )


def query_value_marks(heads, width, lanes, first_lane):
    row = iota((2 * heads * HEAD_ROWS + 16, 1), 0)
    lane = iota((1, lanes), 1) - first_lane
    mark = row - heads * HEAD_ROWS
    is_class = (mark >= 0) & (mark < CLASSES)
    differ = jnp.where(is_class | (mark == CLASSES), -BIG / CONSTANT, 0.0)
    unit = (mark - 16) % HEAD_ROWS
    ones = jnp.where((mark >= 16) & (unit == width), 1.0 / CONSTANT, 0.0)
    same = jnp.where(is_class & (mark == lane), BIG, 0.0)
    return same + jnp.where(lane == CLASSES + 1, differ + ones, 0.0)


def key_marks(rows, lanes, first_row, first_lane):
    row = iota((rows, 1), 0) - first_row
    lane = iota((1, lanes), 1) - first_lane
    is_class = (lane >= 0) & (lane < CLASSES)
    same = jnp.where(is_class & (row == lane), 1.0, 0.0)
    pad = jnp.where(row == CLASSES, -1.0, jnp.where(row == CLASSES + 1, 1.0 / CONSTANT, 0.0))
    return same + jnp.where(lane == CLASSES, pad, 0.0)


def bias_rows(table, turn, flip_rows, flip_cols):
    shape = (1, WIN * LANES)
    lane = iota(shape, 1)
    row_step = lane % LANES // WIN - (WIN - 1)
    col_step = lane % WIN - lane // LANES
    row_step = jnp.where(flip_rows, -row_step, row_step)
    col_step = jnp.where(flip_cols, -col_step, col_step)
    lead = jnp.where(turn, col_step, row_step)
    trail = jnp.where(turn, row_step, col_step)
    index = (lead + WIN - 1) * SIDE + trail + WIN - 1
    pick = one_hot(iota((table.shape[1], WIN * LANES), 0) == index)
    rest = table * LOG2E
    parts = []
    for _ in range(3):
        parts.append(rest.astype(BF16))
        rest = rest - parts[-1].astype(F32)
    moved = dot(jnp.concatenate(parts, axis=0), pick)
    size = table.shape[0]
    return moved[:size] + moved[size : 2 * size] + moved[2 * size :]


def bias_grid(rows, rows_ref, store):
    heads = rows.shape[0]
    for key_col in range(WIN):
        rows_ref[0:heads, key_col, :] = rows[:, key_col * LANES : (key_col + 1) * LANES]
    half = iota((WIN, LANES), 1)
    for pair in range(heads // 2):
        even, odd = rows_ref[2 * pair], rows_ref[2 * pair + 1]
        for key_row in range(WIN):
            start = (WIN - 1 - key_row) * WIN
            left = pltpu.roll(even, (LANES - start) % LANES, 1)
            right = pltpu.roll(odd, (LANES - start + CELLS) % LANES, 1)
            store(key_row, pair, jnp.where(half < CELLS, left, right))


def prepare_kernel(
    heads,
    features_ref,
    labels_ref,
    *refs,
):
    sources, outs, scratch = refs[:9], refs[9:22], refs[22:]
    held, (rows_ref, tables_ref, semaphores) = scratch[:9], scratch[9:]
    (
        qvt_out,
        key_out,
        proj_out,
        up_out,
        down_out,
        recon_out,
        bias_out,
        refine_qvt_out,
        refine_key_out,
        refine_proj_out,
        refine_bias_out,
        features_out,
        labels_out,
    ) = outs
    arrivals = [
        pltpu.make_async_copy(source, target, semaphores.at[i])
        for i, (source, target) in enumerate(
            zip(
                (*sources, features_ref, labels_ref), (*held, features_out, labels_out)
            )
        )
    ]
    for arrival in arrivals:
        arrival.start()
    for arrival in arrivals[:9]:
        arrival.wait()
    (
        qkv_ref,
        proj_ref,
        up_ref,
        down_ref,
        swin_bias_ref,
        recon_ref,
        refine_qkv_ref,
        refine_proj_ref,
        refine_bias_ref,
    ) = held
    channels, blocks, hidden = up_ref.shape
    width = channels // heads
    lanes = key_out.shape[1]
    head_rows = heads * HEAD_ROWS
    taps, out, _ = recon_ref.shape
    refine_heads = refine_bias_ref.shape[0]
    refine_width = out // refine_heads
    refine_rows = refine_heads * HEAD_ROWS
    mark = channels % LANES
    both = blocks * channels
    qkv, proj, up, down = (
        ref[...].reshape(both, ref.shape[2]) for ref in (qkv_ref, proj_ref, up_ref, down_ref)
    )

    def block_source(index, i):
        return jnp.where(index < channels, index * blocks + i, -1)

    moved = exact(pick_rows(query_value_source(heads, width, channels), 3 * channels), qkv, NT)
    keys = exact(
        qkv, pick_columns(head_source(iota((1, lanes), 1), heads, width, channels), 3 * channels)
    )
    turned = exact(pick_rows(iota((down_out.shape[1], 1), 0), hidden), down, NT)
    pad = pick_rows(iota((lanes, 1), 0), channels)
    kernel = exact(pad, recon_ref[...].reshape(taps * out, channels), NT)
    for i in range(blocks):
        tables_ref[i * heads : (i + 1) * heads] = swin_bias_ref[:, i]
    rows = []
    for v in range(VAR_DEV):
        code = lax.axis_index("var") * VAR_DEV + v
        turn, flip_rows, flip_cols = code // 4 == 1, code // 2 % 2 == 1, code % 2 == 1
        rows.append(bias_rows(tables_ref[: blocks * heads], turn, flip_rows, flip_cols))
    never = lax.axis_index("var") < 0
    refine_table = bias_rows(refine_bias_ref[...], never, never, never)
    weight = refine_qkv_ref[...]
    source = query_value_source(refine_heads, refine_width, out)
    refine_moved = exact(pick_rows(source, 3 * out), weight, NT)
    source = head_source(iota((1, LANES), 1), refine_heads, refine_width, out)
    refine_keys = exact(weight, pick_columns(source, 3 * out))
    refine_proj = []
    for h in range(refine_heads):
        row = iota((LANES, 1), 0)
        source = jnp.where(row < refine_width, row + h * refine_width, -1)
        refine_proj.append(exact(pick_rows(source, out), refine_proj_ref[...]))

    row = iota((2 * LANES, 1), 0)
    head, unit = row % LANES // HEAD_ROWS * 2 + row // LANES, row % HEAD_ROWS
    proj_source = jnp.where((head < heads) & (unit < width), head * width + unit, channels)
    for i in range(blocks):
        for ref in (proj_out, up_out):
            ref[i] = jnp.zeros(ref.shape[1:], BF16)
        proj_out[i, :, :channels] = exact(pick_rows(block_source(proj_source, i), both), proj)
        up_out[i, :, :hidden] = exact(pick_rows(block_source(iota((lanes, 1), 0), i), both), up)
    for v in range(VAR_DEV):
        code = lax.axis_index("var") * VAR_DEV + v
        turn, flip_rows, flip_cols = code // 4 == 1, code // 2 % 2 == 1, code % 2 == 1
        lane = iota((1, 3 * lanes), 1)
        row_step = lane // lanes - 1
        lane = lane % lanes
        col_step = jnp.where(lane >= LANES, 1, jnp.where(lane >= out, 0, -1))
        channel = jnp.where(lane >= LANES, lane - LANES, jnp.where(lane >= out, lane - out, lane))
        row_step = jnp.where(flip_rows, -row_step, row_step)
        col_step = jnp.where(flip_cols, -col_step, col_step)
        tap = (jnp.where(turn, col_step, row_step) + 1) * 3
        tap = tap + jnp.where(turn, row_step, col_step) + 1
        sub_row = channel % (SCALE * SCALE) // SCALE
        sub_col = channel % SCALE
        sub_row = jnp.where(flip_rows, SCALE - 1 - sub_row, sub_row)
        sub_col = jnp.where(flip_cols, SCALE - 1 - sub_col, sub_col)
        source = channel // (SCALE * SCALE) * SCALE * SCALE
        source = source + jnp.where(turn, sub_col, sub_row) * SCALE
        source = tap * out + source + jnp.where(turn, sub_row, sub_col)
        source = jnp.where(channel < out, source, -1)
        recon_out[v] = exact(kernel, pick_columns(source, taps * out))

    row = iota((2 * head_rows + 16, 1), 0)
    scale = jnp.where(row < head_rows, width**-0.5 * LOG2E, 1.0)
    query_add = query_value_marks(heads, width, lanes, channels)
    key_add = key_marks(lanes, lanes, channels, head_rows)
    for i in range(blocks):
        columns = pick_columns(block_source(iota((1, lanes), 1), i), both)
        qvt_out[i] = (dot(moved, columns) * scale + query_add).astype(BF16)
        down_out[i] = (dot(turned, columns) * 0.5).astype(BF16)
        key_out[i] = (
            dot(pick_rows(block_source(iota((lanes, 1), 0), i), both), keys) + key_add
        ).astype(BF16)
    row = iota((2 * refine_rows + 16, 1), 0)
    scale = jnp.where(row < refine_rows, refine_width**-0.5 * LOG2E, 1.0)
    out_pad = pick_rows(iota((LANES, 1), 0), out)
    refine_qvt_out[...] = (
        dot(refine_moved, out_pad, NT) * scale
        + query_value_marks(refine_heads, refine_width, LANES, mark)
    ).astype(BF16)
    refine_key_out[...] = (
        dot(out_pad, refine_keys) + key_marks(LANES, LANES, mark, refine_rows)
    ).astype(BF16)
    for h in range(refine_heads):
        square = dot(refine_proj[h], out_pad, NT)
        refine_proj_out[h * out : (h + 1) * out] = square.T[:out].astype(BF16)
    for v in range(VAR_DEV):
        for i in range(blocks):

            def store(key_row, pair, value):
                at = slice(key_row * WIN, (key_row + 1) * WIN)
                bias_out[i, v, at, pair * LANES : (pair + 1) * LANES] = value

            bias_grid(rows[v][i * heads : (i + 1) * heads], rows_ref, store)

    def store_refine(key_row, pair, value):
        refine_bias_out[key_row * WIN : (key_row + 1) * WIN] = value

    bias_grid(refine_table, rows_ref, store_refine)
    for arrival in arrivals[9:]:
        arrival.wait()


def twice_gelu(x):
    x = x.astype(BF16)
    square = jnp.minimum(x * x, BF16(REACH))
    first, second, third = (BF16(factor) for factor in ERF_TANH)
    series = (square * third + second) * square + first
    return x + x * jnp.tanh(x * series)


def normalize(x, channels, keep_marks):
    tiles = [x[:, i : i + LANES] for i in range(0, x.shape[1], LANES)]
    inside = iota((1, LANES), 1) < channels - (len(tiles) - 1) * LANES
    mean = jnp.sum(sum(tiles[1:], tiles[0]), axis=1, keepdims=True) * (1.0 / channels)
    centred = [tile - mean for tile in tiles]
    centred[-1] = jnp.where(inside, centred[-1], 0.0)
    squares = [tile * tile for tile in centred]
    spread = jnp.sum(sum(squares[1:], squares[0]), axis=1, keepdims=True) * (1.0 / channels)
    scale = lax.rsqrt(spread + EPSILON)
    result = [tile * scale for tile in centred]
    if keep_marks:
        result[-1] = jnp.where(inside, result[-1], tiles[-1])
    return jnp.concatenate(result, axis=1).astype(BF16)


def split_queries(queries, heads):
    pairs = heads // 2
    head_rows = heads * HEAD_ROWS
    left = iota((1, LANES), 1) < CELLS
    turned = pltpu.roll(queries, CELLS, 1).astype(BF16)
    queries = queries.astype(BF16)
    depth = round_up(queries.shape[0], LANES)
    zero = jnp.zeros((HEAD_ROWS, LANES), BF16)
    results = []
    for even, odd in ((queries, turned), (turned, queries)):
        marks = jnp.where(left, even[head_rows:], odd[head_rows:])
        columns = []
        for pair in range(pairs):
            at = pair * 2 * HEAD_ROWS
            rows = [zero] * heads
            rows[2 * pair] = jnp.where(left, even[at : at + HEAD_ROWS], zero)
            rows[2 * pair + 1] = jnp.where(left, zero, odd[at + HEAD_ROWS : at + 2 * HEAD_ROWS])
            rows.append(marks)
            rows.append(jnp.zeros((depth - queries.shape[0], LANES), BF16))
            columns.append(jnp.concatenate(rows, axis=0))
        results.append(jnp.concatenate(columns, axis=1) if pairs > 1 else columns[0])
    return results


def heads_of(n, heads, w_qvt, w_key):
    mark_rows = heads * HEAD_ROWS + 16
    both = dot(w_qvt, n, NT)
    queries = both[:mark_rows]
    values = both[mark_rows:].astype(BF16)
    keys = dot(n, w_key).astype(BF16)
    scores = []
    for place in range(n.shape[0] // LANES):
        cut = slice(place * LANES, (place + 1) * LANES)
        for half, stationary in enumerate(split_queries(queries[:, cut], heads)):
            at = place * LANES + half * CELLS
            scores.append(dot(keys[at : at + CELLS], stationary))
    return scores, values


def soft(scores):
    largest = jnp.max(scores, axis=0, keepdims=True)
    return jnp.exp2(scores - largest).astype(BF16)


def mix_pair(values, first, second, heads, ones_row):
    zero = jnp.zeros((CELLS, LANES), BF16)
    lane = iota((HEAD_ROWS, 2 * LANES), 1) % LANES
    mixed = []
    for pair in range(heads // 2):
        cut = slice(pair * LANES, (pair + 1) * LANES)
        stationary = jnp.concatenate(
            [
                jnp.concatenate([first[:, cut], zero], axis=1),
                jnp.concatenate([zero, second[:, cut]], axis=1),
            ],
            axis=0,
        )
        result = dot(values[pair * CELLS : (pair + 1) * CELLS], stationary)
        joined = jnp.where(lane < CELLS, result[:HEAD_ROWS], result[HEAD_ROWS:])
        mixed.append(joined * pl.reciprocal(joined[ones_row : ones_row + 1]))
    return mixed


def swin_block(x, pairs, heads, channels, bias, w_qvt, w_key, w_proj, w_up, w_down):
    width = channels // heads
    n = normalize(x, channels, True)
    scores, values = heads_of(n, heads, w_qvt[...], w_key[...])
    pad = jnp.zeros((LANES - heads // 2 * HEAD_ROWS, 2 * LANES), F32)
    weights = [
        (soft(scores[2 * place] + bias(a)), soft(scores[2 * place + 1] + bias(b)))
        for place, a, b in pairs
    ]
    blocks = []
    for (place, _, _), (first, second) in zip(pairs, weights):
        cut = slice(place * LANES, (place + 1) * LANES)
        mixed = mix_pair(values[:, cut], first, second, heads, width)
        blocks.append(jnp.concatenate(mixed + [pad], axis=0).astype(BF16))
    outputs = []
    for block in blocks:
        for half in range(2):
            turned = block[:, half * LANES : (half + 1) * LANES].T
            outputs.append(jnp.concatenate([turned[:CELLS], turned[CELLS:]], axis=1))
    outputs = jnp.concatenate(outputs, axis=0)
    places = [place for place, _, _ in pairs]
    if places != list(range(x.shape[0] // LANES)):
        x = jnp.concatenate([x[place * LANES : (place + 1) * LANES] for place in places], axis=0)
    h = (x + dot(outputs, w_proj[...])).astype(BF16).astype(F32)
    hidden = twice_gelu(dot(normalize(h, channels, False), w_up[...]))
    y = h + dot(hidden, w_down[...])
    return [y[i * LANES : (i + 1) * LANES] for i in range(len(pairs))]


def windows_of(grid):
    lanes = grid.shape[2]
    return jnp.concatenate(
        [
            grid[:, w * WIN : (w + 1) * WIN].reshape(CELLS, lanes)
            for w in range(grid.shape[1] // WIN)
        ],
        axis=0,
    )


def first_kernel(heads, channels, strips, x_ref, labels_ref, bias_ref, *refs):
    ends = strips[0] == 0
    *weights, y_ref, side_a_ref, side_b_ref = refs[:8]
    held, side = refs[-2:]
    breadth = x_ref.shape[1]
    count = breadth // WIN
    tokens, lanes = held.shape
    part = tokens // len(strips)
    rows_total = labels_ref.shape[1]
    for k, strip in enumerate(strips):
        rows = x_ref[strip * WIN : (strip + 1) * WIN].astype(F32)
        held[k * part : (k + 1) * part, :channels] = windows_of(rows)
    labels = labels_ref[...].astype(F32).astype(BF16)
    row_gap = iota((CELLS, rows_total), 1) - iota((CELLS, rows_total), 0) // WIN
    col_gap = iota((CELLS, breadth), 1) - iota((CELLS, breadth), 0) % WIN
    by_row = [dot(one_hot(row_gap == strip * WIN), labels, NT) for strip in strips]
    cells = [jnp.where(col_gap == w * WIN, rows, 0.0) for rows in by_row for w in range(count)]
    label = dot(
        jnp.concatenate(cells, axis=0).astype(BF16), jnp.ones((breadth, LANES), BF16)
    )
    lane = iota((1, LANES), 1) - channels % LANES
    wanted = jnp.where((lane >= 0) & (lane < CLASSES), lane + 1, -1).astype(F32)
    fixed = jnp.where(lane == CLASSES, 1.0, jnp.where(lane == CLASSES + 1, CONSTANT, 0.0))
    tail = jnp.where(lane < 0, held[:, lanes - LANES :], jnp.where(label == wanted, 1.0, fixed))
    x = jnp.concatenate([held[:, : lanes - LANES], tail], axis=1)
    places = tokens // LANES
    pairs = [(place, v, v) for v in range(VAR_DEV) for place in range(places)]
    results = swin_block(x, pairs, heads, channels, lambda v: bias_ref[v], *weights)
    for v in range(VAR_DEV):
        for k in range(len(strips)):
            windows = []
            for w in range(count):
                group = k * count + w
                block = results[v * places + group // 2]
                at = group % 2 * CELLS
                windows.append(block[at : at + CELLS].reshape(WIN, WIN, lanes))
            y_ref[v, k * WIN : (k + 1) * WIN] = jnp.concatenate(windows, axis=1).astype(BF16)
            at = k * WIN * SHIFT
            for r in range(WIN):
                rows = slice(at + r * SHIFT, at + (r + 1) * SHIFT)
                side[0, rows] = windows[0][r, :SHIFT]
                side[1, rows] = windows[-1][r, SHIFT:]
        left, right = side[0].astype(BF16), side[1].astype(BF16)
        even = is_even("tx")
        side_a_ref[v] = jnp.where(even, right, left)
        side_b_ref[v] = jnp.where(even, left, right)
    if ends:
        top, bottom = y_ref[:, :SHIFT], y_ref[:, 2 * WIN - SHIFT :]
        even = is_even("ty")
        refs[8][...] = jnp.where(even, bottom, top)
        if len(refs) == 12:
            refs[9][...] = jnp.where(even, top, bottom)


def place_rows(store, ends_ref, middle_ref, v):
    store(0, ends_ref[v, :WIN])
    for r in range(0, middle_ref.shape[1], WIN):
        store(WIN + r, middle_ref[v, r : r + WIN])
    store(WIN + middle_ref.shape[1], ends_ref[v, WIN:])


def inner_kernel(
    heads, channels, group, ends_ref, middle_ref, bias_ref, *refs
):
    *weights, y_ref, marks_ref, held, x_held = refs
    height, breadth, lanes = held.shape
    count = breadth // WIN - 1

    @pl.when(pl.program_id(0) == 0)
    def _():
        for v in range(VAR_DEV):

            def store(first, rows):
                rows = rows.astype(F32)
                held[first : first + WIN] = rows
                if v == 0:
                    marks_ref[first // WIN] = windows_of(rows[:, :, lanes - LANES :]).astype(BF16)

            place_rows(store, ends_ref, middle_ref, v)
            for strip in range(height // WIN - 1):
                rows = slice(strip * WIN + SHIFT, (strip + 1) * WIN + SHIFT)
                for w in range(count):
                    at = SHIFT + w * WIN
                    x_held[strip * count + w, v] = held[rows, at : at + WIN].reshape(CELLS, lanes)

    base = pl.program_id(0) * group
    x = x_held[pl.ds(base, group)].reshape(group * VAR_DEV * CELLS, lanes)
    pairs = [(w, 0, 1) for w in range(group)]
    results = swin_block(x, pairs, heads, channels, lambda v: bias_ref[v], *weights)
    for w in range(group):
        y_ref[w] = results[w].astype(BF16).reshape(VAR_DEV, CELLS, lanes)


def received(refs, axis, after, place):
    value = refs[0][place].astype(F32)
    other = refs[1][place].astype(F32) if len(refs) > 1 else 0.0
    return jnp.where(is_even(axis) == after, value, other)


def edge_kernel(swaps, *refs):
    across, own, outs = refs[:swaps], refs[swaps : swaps + 4], refs[swaps + 4 :]
    breadth = across[0].shape[2]
    half = WIN * SHIFT
    corner = SHIFT * SHIFT
    for first in range(2):
        ends, middle = own[2 * first : 2 * first + 2]
        out = outs[first]
        at_right = is_even("tx") == (first == 0)
        last = out.shape[1] - corner
        for v in range(VAR_DEV):
            for start, after in ((0, False), (last, True)):
                rows = received(across, "ty", after, v)
                cells = jnp.where(at_right, rows[:, breadth - SHIFT :], rows[:, :SHIFT])
                cells = jnp.concatenate([cells[r] for r in range(SHIFT)], axis=0)
                out[v, start : start + corner] = cells.astype(BF16)
            out[v, corner : corner + half] = ends[v, :half]
            out[v, corner + half : last - half] = middle[v]
            out[v, last - half : last] = ends[v, half:]


def outer_kernel(
    heads,
    channels,
    group,
    swaps,
    ends_ref,
    middle_ref,
    *refs,
):
    across, sides, (inner_ref, bias_ref) = refs[:swaps], refs[swaps : swaps + 2], refs[swaps + 2 : swaps + 4]
    refs = refs[swaps + 4 :]
    *weights, w_recon, keep_ref, give_ref, rows_held, sides_held, x_held, y_held, acc = refs
    lanes = middle_ref.shape[3]
    height, breadth = middle_ref.shape[1] + 2 * WIN, middle_ref.shape[2]
    tall, wide = height + 2 * SHIFT, breadth + 2 * SHIFT
    strips, count = tall // WIN, wide // WIN
    always = iota((1, lanes), 1) == channels + CLASSES + 1

    def marked(refs, axis, after, place):
        return jnp.where(always, CONSTANT, received(refs, axis, after, place))

    for v in range(VAR_DEV):
        for end in range(2):
            outside, inside = (0, SHIFT) if end == 0 else (SHIFT, 0)
            corner = 0 if end == 0 else (tall - SHIFT) * SHIFT
            first = 0 if end == 0 else 2 * WIN - SHIFT
            between = slice(SHIFT, SHIFT + breadth)
            rows_held[outside : outside + SHIFT, between] = marked(
                across, "ty", end == 1, v
            )
            rows_held[inside : inside + SHIFT, between] = ends_ref[
                v, first : first + SHIFT
            ].astype(F32)
            side_first = SHIFT * SHIFT if end == 0 else (tall - 2 * SHIFT) * SHIFT
            for side, at in ((0, 0), (1, wide - SHIFT)):
                for rows, start in ((outside, corner), (inside, side_first)):
                    cut = (v, slice(start, start + SHIFT * SHIFT))
                    piece = marked(sides, "tx", side == 1, cut)
                    rows_held[rows : rows + SHIFT, at : at + SHIFT] = piece.reshape(
                        SHIFT, SHIFT, lanes
                    )
            for w in range(count):
                x_held[end * count + w, v] = rows_held[:, w * WIN : (w + 1) * WIN].reshape(
                    CELLS, lanes
                )

        def store(first, rows):
            sides_held[first : first + WIN, :WIN] = rows[:, :WIN].astype(F32)
            sides_held[first : first + WIN, WIN:] = rows[:, breadth - WIN :].astype(F32)

        place_rows(store, ends_ref, middle_ref, v)
        for strip in range(1, strips - 1):
            rows = slice(strip * WIN - SHIFT, (strip + 1) * WIN - SHIFT)
            cut = slice(strip * WIN * SHIFT, (strip + 1) * WIN * SHIFT)
            for end in range(2):
                piece = marked(sides, "tx", end == 1, (v, cut))
                piece = piece.reshape(WIN, SHIFT, lanes)
                at = 0 if end == 0 else WIN + SHIFT
                own = sides_held[rows, at : at + SHIFT]
                both = [piece, own] if end == 0 else [own, piece]
                slot = 2 * count + 2 * (strip - 1) + end
                x_held[slot, v] = jnp.concatenate(both, axis=1).reshape(CELLS, lanes)

    slots = x_held.shape[0]

    def border(step, carry):
        x = x_held[pl.ds(step * group, group)].reshape(group * VAR_DEV * CELLS, lanes)
        pairs = [(w, 0, 1) for w in range(group)]
        results = swin_block(x, pairs, heads, channels, lambda v: bias_ref[v], *weights)
        at = channels + CLASSES
        for w in range(group):
            block = x[w * LANES : (w + 1) * LANES]
            y = results[w] * block[:, at : at + 1]
            y_held[step * group + w] = y.astype(BF16).reshape(VAR_DEV, CELLS, lanes)
        return carry

    lax.fori_loop(0, slots // group, border, 0)

    weights = w_recon[...].reshape(VAR_DEV * lanes, 3 * lanes)

    def scatter(strip, windows):
        tokens = [jnp.concatenate(windows(v), axis=0) for v in range(VAR_DEV)]
        total = dot(jnp.concatenate(tokens, axis=1), weights)
        total = total.reshape(count, WIN, WIN, 3 * lanes)
        for e in range(3):
            rows = slice(strip * WIN + 2 - e, (strip + 1) * WIN + 2 - e)
            for w in range(count):
                across = slice(w * WIN, (w + 1) * WIN)
                part = total[w, :, :, e * lanes : (e + 1) * lanes]
                acc[rows, across] = part if e == 0 else acc[rows, across] + part

    out_channels = keep_ref.shape[1]

    def finish(strip):
        rows = slice(1 + SHIFT + strip * WIN, 1 + SHIFT + (strip + 1) * WIN)
        centre = acc[rows, SHIFT : SHIFT + breadth, :LANES]
        centre = pltpu.roll(centre.reshape(WIN * breadth, LANES), LANES - out_channels, 1)
        result = (
            acc[rows, SHIFT - 1 : SHIFT - 1 + breadth, :LANES]
            + centre.reshape(WIN, breadth, LANES)
            + acc[rows, SHIFT + 1 : SHIFT + 1 + breadth, LANES : 2 * LANES]
        )
        return windows_of(result).T[:out_channels].astype(BF16)

    results = []
    scatter(0, lambda v: [y_held[w, v] for w in range(count)])
    for strip in range(1, strips):
        if strip == strips - 1:
            scatter(strip, lambda v: [y_held[count + w, v] for w in range(count)])
        else:
            slot = 2 * count + 2 * (strip - 1)
            first = (strip - 1) * (count - 2)
            scatter(
                strip,
                lambda v: [
                    y_held[slot, v],
                    *[inner_ref[first + w, v] for w in range(count - 2)],
                    y_held[slot + 1, v],
                ],
            )
        results.append(finish(strip - 1))
    half = len(results) // 2
    even = is_even("var")
    for strip in range(half):
        keep_ref[strip] = jnp.where(even, results[strip], results[strip + half])
        give_ref[strip] = jnp.where(even, results[strip + half], results[strip])


def refine_kernel(
    heads, first_mark, mine_ref, other_ref, marks_ref, bias_ref, w_qvt, w_key, w_projt, out_ref, final
):
    strips, channels, strip_tokens = mine_ref.shape
    breadth = strip_tokens // WIN
    width = channels // heads
    z = jnp.concatenate(
        [mine_ref[s].astype(F32) + other_ref[s].astype(F32) for s in range(strips)], axis=1
    ) * (1.0 / CODES)
    mean = jnp.sum(z, axis=0, keepdims=True) * (1.0 / channels)
    centred = z - mean
    spread = jnp.sum(centred * centred, axis=0, keepdims=True) * (1.0 / channels)
    normed = centred * lax.rsqrt(spread + EPSILON)
    tall = jnp.concatenate([normed, jnp.zeros((LANES - channels, normed.shape[1]), F32)], axis=0)
    first = lax.axis_index("var") % 2 * strips
    marks = jnp.concatenate([marks_ref[first + s].astype(F32) for s in range(strips)], axis=0)
    lane = iota((1, LANES), 1)
    is_mark = (lane >= first_mark) & (lane < first_mark + MARKS)
    n = jnp.where(is_mark, marks, tall.T).astype(BF16)
    scores, values = heads_of(n, heads, w_qvt[...], w_key[...])
    probabilities = [soft(s + bias_ref[...]) for s in scores]
    lane = iota((channels, LANES), 1)
    branches = []
    for pair in range(len(probabilities) // 2):
        mixed = mix_pair(
            values[:, pair * LANES : (pair + 1) * LANES],
            probabilities[2 * pair],
            probabilities[2 * pair + 1],
            heads,
            width,
        )[0].astype(BF16)
        both = dot(w_projt[...][:, :HEAD_ROWS], mixed)
        even, odd = both[:channels], both[channels:]
        halves = []
        for half in range(2):
            cut = slice(half * LANES, (half + 1) * LANES)
            halves.append(even[:, cut] + pltpu.roll(odd[:, cut], CELLS, 1))
        branches.append(jnp.where(lane < CELLS, halves[0], pltpu.roll(halves[1], CELLS, 1)))
    refined = (z + jnp.concatenate(branches, axis=1)).astype(BF16)
    stacked = jnp.concatenate(
        [refined[:, s * strip_tokens : (s + 1) * strip_tokens] for s in range(strips)], axis=0
    )
    shape = (strip_tokens, WIN * breadth * SCALE)
    cell = iota(shape, 1) // SCALE
    source = (cell % breadth // WIN) * CELLS + (cell // breadth) * WIN + cell % WIN
    wide = dot(stacked, one_hot(iota(shape, 0) == source))
    own = iota(wide.shape, 1) % SCALE == iota(wide.shape, 0) % SCALE
    wide = jnp.where(own, wide, 0.0).astype(BF16)
    shape = (wide.shape[0] // SCALE, wide.shape[0])
    folded = dot(one_hot(iota(shape, 1) // SCALE == iota(shape, 0)), wide)
    colours = channels // (SCALE * SCALE)
    row_lanes = breadth * SCALE
    for s in range(strips):
        for c in range(colours):
            first = (s * colours + c) * SCALE
            for y in range(WIN):
                start = (s * WIN + y) * SCALE
                final[c, start : start + SCALE] = folded[
                    first : first + SCALE, y * row_lanes : (y + 1) * row_lanes
                ]
    out_ref[...] = final[...].astype(BF16)


def is_even(axis):
    return lax.axis_index(axis) % 2 == 0


def swap_pairs(strip, axis, first):
    count = lax.axis_size(axis)
    pairs = [(i, i + 1) for i in range(first, count - 1, 2)]
    return lax.ppermute(strip, axis, pairs + [(j, i) for i, j in pairs])


def whole_swap(a, bit):
    count = lax.axis_size("var")
    return lax.ppermute(a, "var", [(i, i ^ bit) for i in range(count)])


def whole(a):
    return pl.BlockSpec(a.shape, lambda *i: (0,) * a.ndim)


def params(mebibytes):
    return pltpu.CompilerParams(
        dimension_semantics=("arbitrary",), vmem_limit_bytes=mebibytes * 1024 * 1024
    )


def local(
    features,
    labels,
    qkv_weight,
    proj_weight,
    up_weight,
    down_weight,
    swin_bias,
    recon_weight,
    refine_qkv,
    refine_proj,
    refine_bias,
):
    height, breadth, channels = features.shape
    heads = swin_bias.shape[1]
    out_channels = recon_weight.shape[-1]
    refine_heads = refine_bias.shape[0]
    lanes = round_up(channels + MARKS, LANES)
    hidden = round_up(up_weight.shape[-1], LANES)
    operands = (
        features,
        labels.T,
        jnp.swapaxes(qkv_weight, 0, 1),
        jnp.swapaxes(proj_weight, 0, 1),
        jnp.swapaxes(up_weight, 0, 1),
        down_weight.transpose(2, 0, 1),
        jnp.swapaxes(swin_bias, 0, 1),
        jnp.swapaxes(recon_weight, 1, 2),
        refine_qkv,
        refine_proj,
        refine_bias,
    )
    head_rows, refine_rows = heads * HEAD_ROWS, refine_heads * HEAD_ROWS
    shapes = [
        ((2, 2 * head_rows + 16, lanes), BF16),
        ((2, lanes, lanes), BF16),
        ((2, 2 * LANES, lanes), BF16),
        ((2, lanes, hidden), BF16),
        ((2, hidden, lanes), BF16),
        ((VAR_DEV, lanes, 3 * lanes), BF16),
        ((2, VAR_DEV, CELLS, heads * CELLS), F32),
        ((2 * refine_rows + 16, LANES), BF16),
        ((LANES, LANES), BF16),
        ((refine_heads * out_channels, LANES), BF16),
        ((CELLS, refine_heads * CELLS), F32),
        (features.shape, BF16),
        (operands[1].shape, jnp.int32),
    ]
    shapes = [jax.ShapeDtypeStruct(*s) for s in shapes]
    prepared = pl.pallas_call(
        functools.partial(prepare_kernel, heads),
        grid=(1,),
        in_specs=[pl.BlockSpec(memory_space=pltpu.HBM)] * len(operands),
        out_specs=[whole(s) for s in shapes],
        out_shape=shapes,
        scratch_shapes=[
            *[pltpu.VMEM(a.shape, a.dtype) for a in operands[2:]],
            pltpu.VMEM((heads, WIN, LANES), F32),
            pltpu.VMEM((round_up(2 * heads, 8), swin_bias.shape[2]), F32),
            pltpu.SemaphoreType.DMA((len(operands),)),
        ],
        compiler_params=params(12),
        name="prepare",
    )(*[pltpu.with_memory_space_constraint(a, pltpu.HBM) for a in operands])
    *swin, recon, bias, refine_qvt, refine_key, refine_projt, refine_grid = prepared[:-2]
    features, labels_across = prepared[-2:]

    def block_specs(i):
        arrays = (bias, *swin)
        return arrays, [
            pl.BlockSpec((None,) + a.shape[1:], lambda *_, n=a.ndim: (i,) + (0,) * (n - 1))
            for a in arrays
        ]

    def cost(windows):
        return pl.CostEstimate(
            flops=windows * 400_000_000, bytes_accessed=windows * 200_000, transcendentals=0
        )

    arrays, specs = block_specs(0)
    strips = height // WIN
    tokens = WIN * breadth

    pair_axis = lax.axis_size("ty") == 2

    def block_one(places, name):
        rows = len(places) * WIN
        outs = [
            ((VAR_DEV, rows, breadth, lanes), BF16),
            ((VAR_DEV, rows * SHIFT, lanes), BF16),
            ((VAR_DEV, rows * SHIFT, lanes), BF16),
        ]
        if places[0] == 0:
            outs += [((VAR_DEV, SHIFT, breadth, lanes), BF16)] * (1 if pair_axis else 2)
        outs = [jax.ShapeDtypeStruct(*o) for o in outs]
        return pl.pallas_call(
            functools.partial(first_kernel, heads, channels, places),
            grid=(1,),
            in_specs=[whole(features), whole(labels_across), *specs],
            out_specs=[whole(o) for o in outs],
            out_shape=outs,
            scratch_shapes=[
                pltpu.VMEM((len(places) * tokens, lanes), F32),
                pltpu.VMEM((2, rows * SHIFT, lanes), F32),
            ],
            compiler_params=params(12 if places[0] == 0 else 18),
            cost_estimate=cost(len(places) * breadth // WIN * VAR_DEV),
            name=name,
        )(features, labels_across, *arrays)

    y_ends, a_ends, b_ends, *own_ends = block_one((0, strips - 1), "block_one_ends")
    across = [swap_pairs(own, "ty", first) for first, own in enumerate(own_ends)]
    y_middle, a_middle, b_middle = block_one(tuple(range(1, strips - 1)), "block_one_middle")
    operands = (*across, a_ends, a_middle, b_ends, b_middle)
    strip_shape = jax.ShapeDtypeStruct((VAR_DEV, (height + 2 * SHIFT) * SHIFT, lanes), BF16)
    strips_out = pl.pallas_call(
        functools.partial(edge_kernel, len(across)),
        grid=(1,),
        in_specs=[whole(a) for a in operands],
        out_specs=[whole(strip_shape)] * 2,
        out_shape=[strip_shape] * 2,
        compiler_params=params(6),
        name="edges",
    )(*operands)
    sides = [swap_pairs(strip, "tx", first) for first, strip in enumerate(strips_out)]

    arrays, specs = block_specs(1)
    inner_count = (strips - 1) * (breadth // WIN - 1)
    group = next(g for g in range(24, 0, -1) if inner_count % g == 0)
    inner, marks = pl.pallas_call(
        functools.partial(inner_kernel, heads, channels, group),
        grid=(inner_count // group,),
        in_specs=[whole(y_ends), whole(y_middle), *specs],
        out_specs=[
            pl.BlockSpec((group, VAR_DEV, CELLS, lanes), lambda i: (i, 0, 0, 0)),
            pl.BlockSpec((strips, tokens, LANES), lambda i: (0, 0, 0)),
        ],
        out_shape=[
            jax.ShapeDtypeStruct((inner_count, VAR_DEV, CELLS, lanes), BF16),
            jax.ShapeDtypeStruct((strips, tokens, LANES), BF16),
        ],
        scratch_shapes=[
            pltpu.VMEM((height, breadth, lanes), F32),
            pltpu.VMEM((inner_count, VAR_DEV, CELLS, lanes), F32),
        ],
        compiler_params=params(20),
        cost_estimate=cost(inner_count * VAR_DEV),
        name="block_two_inner",
    )(y_ends, y_middle, *arrays)

    tall, wide = height + 2 * SHIFT, breadth + 2 * SHIFT
    slots = 2 * (tall + wide) // WIN - 4
    group = next(g for g in range(24, 0, -1) if slots % g == 0)
    operands = (y_ends, y_middle, *across, *sides, inner)
    half_shape = jax.ShapeDtypeStruct((strips // 2, out_channels, tokens), BF16)
    keep, give = pl.pallas_call(
        functools.partial(outer_kernel, heads, channels, group, len(across)),
        grid=(1,),
        in_specs=[*[whole(a) for a in operands], *specs, whole(recon)],
        out_specs=[whole(half_shape)] * 2,
        out_shape=[half_shape] * 2,
        scratch_shapes=[
            pltpu.VMEM((WIN, wide, lanes), F32),
            pltpu.VMEM((height, 2 * WIN, lanes), F32),
            pltpu.VMEM((slots, VAR_DEV, CELLS, lanes), F32),
            pltpu.VMEM((slots, VAR_DEV, CELLS, lanes), BF16),
            pltpu.VMEM((tall + WIN, wide, lanes), F32),
        ],
        compiler_params=params(26),
        name="block_two_border",
    )(*operands, *arrays, recon)

    mine = (keep.astype(F32) + whole_swap(give, 1).astype(F32)).astype(BF16)
    other = whole_swap(mine, 2)
    colours = out_channels // (SCALE * SCALE)
    operands = (mine, other, marks, refine_grid, refine_qvt, refine_key, refine_projt)
    out_shape = (colours, height * SCALE // 2, breadth * SCALE)
    refined = pl.pallas_call(
        functools.partial(refine_kernel, refine_heads, channels % LANES),
        grid=(1,),
        in_specs=[whole(a) for a in operands],
        out_specs=pl.BlockSpec(out_shape, lambda i: (0, 0, 0)),
        out_shape=jax.ShapeDtypeStruct(out_shape, BF16),
        scratch_shapes=[pltpu.VMEM(out_shape, F32)],
        compiler_params=params(8),
        name="refinement",
    )(*operands)
    received = whole_swap(refined, 1)
    even = is_even("var")
    halves = jnp.where(even, refined, received), jnp.where(even, received, refined)
    return jnp.concatenate(halves, axis=1).astype(F32)


def solution(mesh):
    placed = (P("ty", "tx", None), P("ty", "tx"), P(), P(), P(), P(), P(), P(), P(), P(), P())
    return jax.shard_map(
        local, mesh=mesh, in_specs=placed, out_specs=P(None, "ty", "tx"), check_vma=False
    )
```

```python
import functools

import jax
import jax.numpy as jnp
from jax import lax
from jax.experimental import pallas as pl
from jax.experimental.pallas import tpu as pltpu
from jax.sharding import PartitionSpec as P

WIN = 8
CELLS = WIN * WIN
SHIFT = 4
SCALE = 4
VAR_DEV = 2
CODES = 8
LANES = 128
HEAD_ROWS = 32
CLASSES = 4
MARKS = CLASSES + 2
CONSTANT = -2.0
SIDE = 2 * WIN - 1

EPSILON = 1e-05
LOG2E = 1.4426950408889634
BIG = float(2.0**100)
ERF_TANH = (0.7975076, 0.0370060, -0.00035159)
REACH = 36.0

NN = (((1,), (0,)), ((), ()))
NT = (((1,), (1,)), ((), ()))
F32 = jnp.float32
BF16 = jnp.bfloat16


def dot(a, b, dims=NN):
    return lax.dot_general(a, b, dims, preferred_element_type=F32)


def iota(shape, dim):
    return lax.broadcasted_iota(jnp.int32, shape, dim)


def round_up(size, multiple):
    return -(-size // multiple) * multiple


def one_hot(condition):
    return jnp.where(condition, 1.0, 0.0).astype(BF16)


def exact(a, b, dims=NN):
    return dot(a, b, dims).astype(BF16)


def pick_rows(source, size):
    return one_hot(iota((1, size), 1) == source)


def pick_columns(source, size):
    return one_hot(iota((size, 1), 0) == source)


def head_source(index, heads, width, first=0):
    unit = index % HEAD_ROWS
    keep = (unit < width) & (index < heads * HEAD_ROWS)
    return jnp.where(keep, first + index // HEAD_ROWS * width + unit, -1)


def query_value_source(heads, width, channels):
    row = iota((2 * heads * HEAD_ROWS + 16, 1), 0)
    values = row - heads * HEAD_ROWS - 16
    return jnp.where(
        values < 0,
        head_source(row, heads, width),
        head_source(jnp.maximum(values, 0), heads, width, 2 * channels),
    )


def query_value_marks(heads, width, lanes, first_lane):
    row = iota((2 * heads * HEAD_ROWS + 16, 1), 0)
    lane = iota((1, lanes), 1) - first_lane
    mark = row - heads * HEAD_ROWS
    is_class = (mark >= 0) & (mark < CLASSES)
    differ = jnp.where(is_class | (mark == CLASSES), -BIG / CONSTANT, 0.0)
    unit = (mark - 16) % HEAD_ROWS
    ones = jnp.where((mark >= 16) & (unit == width), 1.0 / CONSTANT, 0.0)
    same = jnp.where(is_class & (mark == lane), BIG, 0.0)
    return same + jnp.where(lane == CLASSES + 1, differ + ones, 0.0)


def key_marks(rows, lanes, first_row, first_lane):
    row = iota((rows, 1), 0) - first_row
    lane = iota((1, lanes), 1) - first_lane
    is_class = (lane >= 0) & (lane < CLASSES)
    same = jnp.where(is_class & (row == lane), 1.0, 0.0)
    pad = jnp.where(row == CLASSES, -1.0, jnp.where(row == CLASSES + 1, 1.0 / CONSTANT, 0.0))
    return same + jnp.where(lane == CLASSES, pad, 0.0)


def bias_rows(table, turn, flip_rows, flip_cols):
    shape = (1, WIN * LANES)
    lane = iota(shape, 1)
    row_step = lane % LANES // WIN - (WIN - 1)
    col_step = lane % WIN - lane // LANES
    row_step = jnp.where(flip_rows, -row_step, row_step)
    col_step = jnp.where(flip_cols, -col_step, col_step)
    lead = jnp.where(turn, col_step, row_step)
    trail = jnp.where(turn, row_step, col_step)
    index = (lead + WIN - 1) * SIDE + trail + WIN - 1
    pick = one_hot(iota((table.shape[1], WIN * LANES), 0) == index)
    rest = table * LOG2E
    parts = []
    for _ in range(3):
        parts.append(rest.astype(BF16))
        rest = rest - parts[-1].astype(F32)
    moved = dot(jnp.concatenate(parts, axis=0), pick)
    size = table.shape[0]
    return moved[:size] + moved[size : 2 * size] + moved[2 * size :]


def bias_grid(rows, rows_ref, store):
    heads = rows.shape[0]
    for key_col in range(WIN):
        rows_ref[0:heads, key_col, :] = rows[:, key_col * LANES : (key_col + 1) * LANES]
    half = iota((WIN, LANES), 1)
    for pair in range(heads // 2):
        even, odd = rows_ref[2 * pair], rows_ref[2 * pair + 1]
        for key_row in range(WIN):
            start = (WIN - 1 - key_row) * WIN
            left = pltpu.roll(even, (LANES - start) % LANES, 1)
            right = pltpu.roll(odd, (LANES - start + CELLS) % LANES, 1)
            store(key_row, pair, jnp.where(half < CELLS, left, right))


def prepare_kernel(
    heads,
    features_ref,
    labels_ref,
    *refs,
):
    sources, outs, scratch = refs[:9], refs[9:22], refs[22:]
    held, (rows_ref, tables_ref, semaphores) = scratch[:9], scratch[9:]
    (
        qvt_out,
        key_out,
        proj_out,
        up_out,
        down_out,
        recon_out,
        bias_out,
        refine_qvt_out,
        refine_key_out,
        refine_proj_out,
        refine_bias_out,
        features_out,
        labels_out,
    ) = outs
    arrivals = [
        pltpu.make_async_copy(source, target, semaphores.at[i])
        for i, (source, target) in enumerate(
            zip(
                (*sources, features_ref, labels_ref), (*held, features_out, labels_out)
            )
        )
    ]
    for arrival in arrivals:
        arrival.start()
    (
        qkv_ref,
        proj_ref,
        up_ref,
        down_ref,
        swin_bias_ref,
        recon_ref,
        refine_qkv_ref,
        refine_proj_ref,
        refine_bias_ref,
    ) = held
    channels, blocks, hidden = up_ref.shape
    width = channels // heads
    lanes = key_out.shape[1]
    head_rows = heads * HEAD_ROWS
    taps, out, _ = recon_ref.shape
    refine_heads = refine_bias_ref.shape[0]
    refine_width = out // refine_heads
    refine_rows = refine_heads * HEAD_ROWS
    mark = channels % LANES
    both = blocks * channels

    for arrival in (arrivals[4], arrivals[8]):
        arrival.wait()
    for i in range(blocks):
        tables_ref[i * heads : (i + 1) * heads] = swin_bias_ref[:, i]
    rows = []
    for v in range(VAR_DEV):
        code = lax.axis_index("var") * VAR_DEV + v
        turn, flip_rows, flip_cols = code // 4 == 1, code // 2 % 2 == 1, code % 2 == 1
        rows.append(bias_rows(tables_ref[: blocks * heads], turn, flip_rows, flip_cols))
    never = lax.axis_index("var") < 0
    refine_table = bias_rows(refine_bias_ref[...], never, never, never)
    for arrival in (*arrivals[:4], *arrivals[5:8]):
        arrival.wait()
    qkv, proj, up, down = (
        ref[...].reshape(both, ref.shape[2]) for ref in (qkv_ref, proj_ref, up_ref, down_ref)
    )

    def block_source(index, i):
        return jnp.where(index < channels, index * blocks + i, -1)

    moved = exact(pick_rows(query_value_source(heads, width, channels), 3 * channels), qkv, NT)
    keys = exact(
        qkv, pick_columns(head_source(iota((1, lanes), 1), heads, width, channels), 3 * channels)
    )
    turned = exact(pick_rows(iota((down_out.shape[1], 1), 0), hidden), down, NT)
    pad = pick_rows(iota((lanes, 1), 0), channels)
    kernel = exact(pad, recon_ref[...].reshape(taps * out, channels), NT)
    weight = refine_qkv_ref[...]
    source = query_value_source(refine_heads, refine_width, out)
    refine_moved = exact(pick_rows(source, 3 * out), weight, NT)
    source = head_source(iota((1, LANES), 1), refine_heads, refine_width, out)
    refine_keys = exact(weight, pick_columns(source, 3 * out))
    refine_proj = []
    for h in range(refine_heads):
        row = iota((LANES, 1), 0)
        source = jnp.where(row < refine_width, row + h * refine_width, -1)
        refine_proj.append(exact(pick_rows(source, out), refine_proj_ref[...]))

    row = iota((2 * LANES, 1), 0)
    head, unit = row % LANES // HEAD_ROWS * 2 + row // LANES, row % HEAD_ROWS
    proj_source = jnp.where((head < heads) & (unit < width), head * width + unit, channels)
    for i in range(blocks):
        for ref in (proj_out, up_out):
            ref[i] = jnp.zeros(ref.shape[1:], BF16)
        proj_out[i, :, :channels] = exact(pick_rows(block_source(proj_source, i), both), proj)
        up_out[i, :, :hidden] = exact(pick_rows(block_source(iota((lanes, 1), 0), i), both), up)
    for v in range(VAR_DEV):
        code = lax.axis_index("var") * VAR_DEV + v
        turn, flip_rows, flip_cols = code // 4 == 1, code // 2 % 2 == 1, code % 2 == 1
        lane = iota((1, 3 * lanes), 1)
        row_step = lane // lanes - 1
        lane = lane % lanes
        col_step = jnp.where(lane >= LANES, 1, jnp.where(lane >= out, 0, -1))
        channel = jnp.where(lane >= LANES, lane - LANES, jnp.where(lane >= out, lane - out, lane))
        row_step = jnp.where(flip_rows, -row_step, row_step)
        col_step = jnp.where(flip_cols, -col_step, col_step)
        tap = (jnp.where(turn, col_step, row_step) + 1) * 3
        tap = tap + jnp.where(turn, row_step, col_step) + 1
        sub_row = channel % (SCALE * SCALE) // SCALE
        sub_col = channel % SCALE
        sub_row = jnp.where(flip_rows, SCALE - 1 - sub_row, sub_row)
        sub_col = jnp.where(flip_cols, SCALE - 1 - sub_col, sub_col)
        source = channel // (SCALE * SCALE) * SCALE * SCALE
        source = source + jnp.where(turn, sub_col, sub_row) * SCALE
        source = tap * out + source + jnp.where(turn, sub_row, sub_col)
        source = jnp.where(channel < out, source, -1)
        recon_out[v] = exact(kernel, pick_columns(source, taps * out))

    row = iota((2 * head_rows + 16, 1), 0)
    scale = jnp.where(row < head_rows, width**-0.5 * LOG2E, 1.0)
    query_add = query_value_marks(heads, width, lanes, channels)
    key_add = key_marks(lanes, lanes, channels, head_rows)
    for i in range(blocks):
        columns = pick_columns(block_source(iota((1, lanes), 1), i), both)
        qvt_out[i] = (dot(moved, columns) * scale + query_add).astype(BF16)
        down_out[i] = (dot(turned, columns) * 0.5).astype(BF16)
        key_out[i] = (
            dot(pick_rows(block_source(iota((lanes, 1), 0), i), both), keys) + key_add
        ).astype(BF16)
    row = iota((2 * refine_rows + 16, 1), 0)
    scale = jnp.where(row < refine_rows, refine_width**-0.5 * LOG2E, 1.0)
    out_pad = pick_rows(iota((LANES, 1), 0), out)
    refine_qvt_out[...] = (
        dot(refine_moved, out_pad, NT) * scale
        + query_value_marks(refine_heads, refine_width, LANES, mark)
    ).astype(BF16)
    refine_key_out[...] = (
        dot(out_pad, refine_keys) + key_marks(LANES, LANES, mark, refine_rows)
    ).astype(BF16)
    for h in range(refine_heads):
        square = dot(refine_proj[h], out_pad, NT)
        refine_proj_out[h * out : (h + 1) * out] = square.T[:out].astype(BF16)
    for v in range(VAR_DEV):
        for i in range(blocks):

            def store(key_row, pair, value):
                at = slice(key_row * WIN, (key_row + 1) * WIN)
                bias_out[i, v, at, pair * LANES : (pair + 1) * LANES] = value

            bias_grid(rows[v][i * heads : (i + 1) * heads], rows_ref, store)

    def store_refine(key_row, pair, value):
        refine_bias_out[key_row * WIN : (key_row + 1) * WIN] = value

    bias_grid(refine_table, rows_ref, store_refine)
    for arrival in arrivals[9:]:
        arrival.wait()


def twice_gelu(x):
    x = x.astype(BF16)
    square = jnp.minimum(x * x, BF16(REACH))
    first, second, third = (BF16(factor) for factor in ERF_TANH)
    series = (square * third + second) * square + first
    return x + x * jnp.tanh(x * series)


def normalize(x, channels, keep_marks):
    tiles = [x[:, i : i + LANES] for i in range(0, x.shape[1], LANES)]
    inside = iota((1, LANES), 1) < channels - (len(tiles) - 1) * LANES
    mean = jnp.sum(sum(tiles[1:], tiles[0]), axis=1, keepdims=True) * (1.0 / channels)
    centred = [tile - mean for tile in tiles]
    centred[-1] = jnp.where(inside, centred[-1], 0.0)
    squares = [tile * tile for tile in centred]
    spread = jnp.sum(sum(squares[1:], squares[0]), axis=1, keepdims=True) * (1.0 / channels)
    scale = lax.rsqrt(spread + EPSILON)
    result = [tile * scale for tile in centred]
    if keep_marks:
        result[-1] = jnp.where(inside, result[-1], tiles[-1])
    return jnp.concatenate(result, axis=1).astype(BF16)


def split_queries(queries, heads):
    pairs = heads // 2
    head_rows = heads * HEAD_ROWS
    left = iota((1, LANES), 1) < CELLS
    turned = pltpu.roll(queries, CELLS, 1).astype(BF16)
    queries = queries.astype(BF16)
    depth = round_up(queries.shape[0], LANES)
    zero = jnp.zeros((HEAD_ROWS, LANES), BF16)
    results = []
    for even, odd in ((queries, turned), (turned, queries)):
        marks = jnp.where(left, even[head_rows:], odd[head_rows:])
        columns = []
        for pair in range(pairs):
            at = pair * 2 * HEAD_ROWS
            rows = [zero] * heads
            rows[2 * pair] = jnp.where(left, even[at : at + HEAD_ROWS], zero)
            rows[2 * pair + 1] = jnp.where(left, zero, odd[at + HEAD_ROWS : at + 2 * HEAD_ROWS])
            rows.append(marks)
            rows.append(jnp.zeros((depth - queries.shape[0], LANES), BF16))
            columns.append(jnp.concatenate(rows, axis=0))
        results.append(jnp.concatenate(columns, axis=1) if pairs > 1 else columns[0])
    return results


def heads_of(n, heads, w_qvt, w_key):
    mark_rows = heads * HEAD_ROWS + 16
    both = dot(w_qvt, n, NT)
    queries = both[:mark_rows]
    values = both[mark_rows:].astype(BF16)
    keys = dot(n, w_key).astype(BF16)
    scores = []
    for place in range(n.shape[0] // LANES):
        cut = slice(place * LANES, (place + 1) * LANES)
        for half, stationary in enumerate(split_queries(queries[:, cut], heads)):
            at = place * LANES + half * CELLS
            scores.append(dot(keys[at : at + CELLS], stationary))
    return scores, values


def soft(scores):
    largest = jnp.max(scores, axis=0, keepdims=True)
    return jnp.exp2(scores - largest).astype(BF16)


def mix_pair(values, first, second, heads, ones_row):
    zero = jnp.zeros((CELLS, LANES), BF16)
    lane = iota((HEAD_ROWS, 2 * LANES), 1) % LANES
    mixed = []
    for pair in range(heads // 2):
        cut = slice(pair * LANES, (pair + 1) * LANES)
        stationary = jnp.concatenate(
            [
                jnp.concatenate([first[:, cut], zero], axis=1),
                jnp.concatenate([zero, second[:, cut]], axis=1),
            ],
            axis=0,
        )
        result = dot(values[pair * CELLS : (pair + 1) * CELLS], stationary)
        joined = jnp.where(lane < CELLS, result[:HEAD_ROWS], result[HEAD_ROWS:])
        mixed.append(joined * pl.reciprocal(joined[ones_row : ones_row + 1]))
    return mixed


def swin_unit(x, pairs, results, heads, channels, bias, w_qvt, w_key, w_proj, w_up, w_down):
    width = channels // heads
    mark_rows = heads * HEAD_ROWS + 16
    n = normalize(x, channels, True)
    yield
    both = dot(w_qvt[...], n, NT)
    queries = both[:mark_rows]
    values = both[mark_rows:].astype(BF16)
    keys = dot(n, w_key[...]).astype(BF16)
    yield
    scores = []
    for place in range(x.shape[0] // LANES):
        cut = slice(place * LANES, (place + 1) * LANES)
        for half, stationary in enumerate(split_queries(queries[:, cut], heads)):
            at = place * LANES + half * CELLS
            scores.append(dot(keys[at : at + CELLS], stationary))
    yield
    weights = [
        (soft(scores[2 * place] + bias(a)), soft(scores[2 * place + 1] + bias(b)))
        for place, a, b in pairs
    ]
    yield
    pad = jnp.zeros((LANES - heads // 2 * HEAD_ROWS, 2 * LANES), F32)
    blocks = []
    for (place, _, _), (first, second) in zip(pairs, weights):
        cut = slice(place * LANES, (place + 1) * LANES)
        mixed = mix_pair(values[:, cut], first, second, heads, width)
        blocks.append(jnp.concatenate(mixed + [pad], axis=0).astype(BF16))
    yield
    outputs = []
    for block in blocks:
        for half in range(2):
            turned = block[:, half * LANES : (half + 1) * LANES].T
            outputs.append(jnp.concatenate([turned[:CELLS], turned[CELLS:]], axis=1))
    outputs = jnp.concatenate(outputs, axis=0)
    yield
    x = jnp.concatenate([x[place * LANES : (place + 1) * LANES] for place, _, _ in pairs], axis=0)
    h = x + dot(outputs, w_proj[...])
    yield
    n = normalize(h, channels, False)
    yield
    hidden = dot(n, w_up[...])
    yield
    hidden = twice_gelu(hidden)
    yield
    y = h + dot(hidden, w_down[...])
    results.extend(y[i * LANES : (i + 1) * LANES] for i in range(len(pairs)))


def swin_block(x, pairs, unit, *args):
    places = x.shape[0] // LANES
    units = []
    for low in range(0, places, unit):
        high = min(low + unit, places)
        picked = [i for i, pair in enumerate(pairs) if low <= pair[0] < high]
        moved = [(pairs[i][0] - low, *pairs[i][1:]) for i in picked]
        found = []
        units.append((picked, found, swin_unit(x[low * LANES : high * LANES], moved, found, *args)))
    running = dict(enumerate(units))
    tick = 0
    while running:
        for number in sorted(running):
            if tick >= number and next(running[number][2], StopIteration) is StopIteration:
                del running[number]
        tick += 1
    results = [None] * len(pairs)
    for picked, found, _ in units:
        for i, result in zip(picked, found):
            results[i] = result
    return results


def windows_of(grid):
    lanes = grid.shape[2]
    return jnp.concatenate(
        [
            grid[:, w * WIN : (w + 1) * WIN].reshape(CELLS, lanes)
            for w in range(grid.shape[1] // WIN)
        ],
        axis=0,
    )


def first_kernel(heads, channels, strips, x_ref, labels_ref, bias_ref, *refs):
    ends = strips[0] == 0
    *weights, y_ref, side_a_ref, side_b_ref = refs[:8]
    held, side = refs[-2:]
    breadth = x_ref.shape[1]
    count = breadth // WIN
    tokens, lanes = held.shape
    part = tokens // len(strips)
    rows_total = labels_ref.shape[1]
    for k, strip in enumerate(strips):
        rows = x_ref[strip * WIN : (strip + 1) * WIN].astype(F32)
        held[k * part : (k + 1) * part, :channels] = windows_of(rows)
    labels = labels_ref[...].astype(F32).astype(BF16)
    row_gap = iota((CELLS, rows_total), 1) - iota((CELLS, rows_total), 0) // WIN
    col_gap = iota((CELLS, breadth), 1) - iota((CELLS, breadth), 0) % WIN
    by_row = [dot(one_hot(row_gap == strip * WIN), labels, NT) for strip in strips]
    cells = [jnp.where(col_gap == w * WIN, rows, 0.0) for rows in by_row for w in range(count)]
    label = dot(
        jnp.concatenate(cells, axis=0).astype(BF16), jnp.ones((breadth, LANES), BF16)
    )
    lane = iota((1, LANES), 1) - channels % LANES
    wanted = jnp.where((lane >= 0) & (lane < CLASSES), lane + 1, -1).astype(F32)
    fixed = jnp.where(lane == CLASSES, 1.0, jnp.where(lane == CLASSES + 1, CONSTANT, 0.0))
    tail = jnp.where(lane < 0, held[:, lanes - LANES :], jnp.where(label == wanted, 1.0, fixed))
    x = jnp.concatenate([held[:, : lanes - LANES], tail], axis=1)
    places = tokens // LANES
    pairs = [(place, v, v) for v in range(VAR_DEV) for place in range(places)]
    results = swin_block(x, pairs, x.shape[0], heads, channels, lambda v: bias_ref[v], *weights)
    for v in range(VAR_DEV):
        for k in range(len(strips)):
            windows = []
            for w in range(count):
                group = k * count + w
                block = results[v * places + group // 2]
                at = group % 2 * CELLS
                windows.append(block[at : at + CELLS].reshape(WIN, WIN, lanes))
            y_ref[v, k * WIN : (k + 1) * WIN] = jnp.concatenate(windows, axis=1)
            at = k * WIN * SHIFT
            for r in range(WIN):
                rows = slice(at + r * SHIFT, at + (r + 1) * SHIFT)
                side[0, rows] = windows[0][r, :SHIFT]
                side[1, rows] = windows[-1][r, SHIFT:]
        left, right = side[0].astype(BF16), side[1].astype(BF16)
        even = is_even("tx")
        side_a_ref[v] = jnp.where(even, right, left)
        side_b_ref[v] = jnp.where(even, left, right)
    if ends:
        top, bottom = y_ref[:, :SHIFT].astype(BF16), y_ref[:, 2 * WIN - SHIFT :].astype(BF16)
        even = is_even("ty")
        refs[8][...] = jnp.where(even, bottom, top)
        if len(refs) == 12:
            refs[9][...] = jnp.where(even, top, bottom)


def tile_rows(ends_ref, middle_ref, v, first, count, columns):
    height = middle_ref.shape[1] + 2 * WIN
    pieces = []
    while count > 0:
        if first < WIN:
            ref, at, limit = ends_ref, first, WIN - first
        elif first < height - WIN:
            ref, at, limit = middle_ref, first - WIN, height - WIN - first
        else:
            ref, at, limit = ends_ref, first - height + 2 * WIN, height - first
        taken = min(count, limit)
        pieces.append(ref[v, at : at + taken, columns])
        first, count = first + taken, count - taken
    return pieces[0] if len(pieces) == 1 else jnp.concatenate(pieces, axis=0)


def inner_kernel(heads, channels, ends_ref, middle_ref, bias_ref, *refs):
    *weights, y_ref, marks_ref = refs
    breadth, lanes = middle_ref.shape[2:]
    strips = middle_ref.shape[1] // WIN + 2
    count = breadth // WIN - 1
    for strip in range(strips):
        rows = tile_rows(ends_ref, middle_ref, 0, strip * WIN, WIN, slice(None))
        marks_ref[strip] = windows_of(rows[:, :, lanes - LANES :]).astype(BF16)
    x = jnp.concatenate(
        [
            tile_rows(
                ends_ref,
                middle_ref,
                v,
                strip * WIN + SHIFT,
                WIN,
                slice(SHIFT + w * WIN, SHIFT + (w + 1) * WIN),
            ).reshape(CELLS, lanes)
            for strip in range(strips - 1)
            for w in range(count)
            for v in range(VAR_DEV)
        ],
        axis=0,
    )
    pairs = [(w, 0, 1) for w in range((strips - 1) * count)]
    results = swin_block(x, pairs, 4, heads, channels, lambda v: bias_ref[v], *weights)
    for w, result in enumerate(results):
        y_ref[w] = result.astype(BF16).reshape(VAR_DEV, CELLS, lanes)


def received(refs, axis, after, place):
    value = refs[0][place].astype(F32)
    other = refs[1][place].astype(F32) if len(refs) > 1 else 0.0
    return jnp.where(is_even(axis) == after, value, other)


def edge_kernel(swaps, *refs):
    across, own, outs = refs[:swaps], refs[swaps : swaps + 4], refs[swaps + 4 :]
    breadth = across[0].shape[2]
    half = WIN * SHIFT
    corner = SHIFT * SHIFT
    for first in range(2):
        ends, middle = own[2 * first : 2 * first + 2]
        out = outs[first]
        at_right = is_even("tx") == (first == 0)
        last = out.shape[1] - corner
        for v in range(VAR_DEV):
            for start, after in ((0, False), (last, True)):
                rows = received(across, "ty", after, v)
                cells = jnp.where(at_right, rows[:, breadth - SHIFT :], rows[:, :SHIFT])
                cells = jnp.concatenate([cells[r] for r in range(SHIFT)], axis=0)
                out[v, start : start + corner] = cells.astype(BF16)
            out[v, corner : corner + half] = ends[v, :half]
            out[v, corner + half : last - half] = middle[v]
            out[v, last - half : last] = ends[v, half:]


def outer_kernel(
    heads,
    channels,
    swaps,
    ends_ref,
    middle_ref,
    *refs,
):
    across, sides, (inner_ref, bias_ref) = refs[:swaps], refs[swaps : swaps + 2], refs[swaps + 2 : swaps + 4]
    refs = refs[swaps + 4 :]
    *weights, w_recon, keep_ref, give_ref, rows_held, x_held, y_held, acc = refs
    lanes = middle_ref.shape[3]
    height, breadth = middle_ref.shape[1] + 2 * WIN, middle_ref.shape[2]
    tall, wide = height + 2 * SHIFT, breadth + 2 * SHIFT
    strips, count = tall // WIN, wide // WIN
    always = iota((1, lanes), 1) == channels + CLASSES + 1

    def marked(refs, axis, after, place):
        return jnp.where(always, CONSTANT, received(refs, axis, after, place))

    for v in range(VAR_DEV):
        for end in range(2):
            outside, inside = (0, SHIFT) if end == 0 else (SHIFT, 0)
            corner = 0 if end == 0 else (tall - SHIFT) * SHIFT
            first = 0 if end == 0 else 2 * WIN - SHIFT
            between = slice(SHIFT, SHIFT + breadth)
            rows_held[outside : outside + SHIFT, between] = marked(
                across, "ty", end == 1, v
            )
            rows_held[inside : inside + SHIFT, between] = ends_ref[v, first : first + SHIFT]
            side_first = SHIFT * SHIFT if end == 0 else (tall - 2 * SHIFT) * SHIFT
            for side, at in ((0, 0), (1, wide - SHIFT)):
                for rows, start in ((outside, corner), (inside, side_first)):
                    cut = (v, slice(start, start + SHIFT * SHIFT))
                    piece = marked(sides, "tx", side == 1, cut)
                    rows_held[rows : rows + SHIFT, at : at + SHIFT] = piece.reshape(
                        SHIFT, SHIFT, lanes
                    )
            for w in range(count):
                x_held[end * count + w, v] = rows_held[:, w * WIN : (w + 1) * WIN].reshape(
                    CELLS, lanes
                )
        for strip in range(1, strips - 1):
            cut = slice(strip * WIN * SHIFT, (strip + 1) * WIN * SHIFT)
            for end in range(2):
                piece = marked(sides, "tx", end == 1, (v, cut))
                piece = piece.reshape(WIN, SHIFT, lanes)
                at = 0 if end == 0 else breadth - SHIFT
                near = slice(at, at + SHIFT)
                own = tile_rows(ends_ref, middle_ref, v, strip * WIN - SHIFT, WIN, near)
                both = [piece, own] if end == 0 else [own, piece]
                slot = 2 * count + 2 * (strip - 1) + end
                x_held[slot, v] = jnp.concatenate(both, axis=1).reshape(CELLS, lanes)

    slots = x_held.shape[0]
    x = x_held[...].reshape(slots * VAR_DEV * CELLS, lanes)
    pairs = [(w, 0, 1) for w in range(slots)]
    results = swin_block(x, pairs, 6, heads, channels, lambda v: bias_ref[v], *weights)
    at = channels + CLASSES
    for w in range(slots):
        valid = x[w * LANES : (w + 1) * LANES, at : at + 1]
        y_held[w] = (results[w] * valid).astype(BF16).reshape(VAR_DEV, CELLS, lanes)

    weights = w_recon[...].reshape(VAR_DEV * lanes, 3 * lanes)

    def scatter(strip, windows):
        tokens = [jnp.concatenate(windows(v), axis=0) for v in range(VAR_DEV)]
        total = dot(jnp.concatenate(tokens, axis=1), weights)
        total = total.reshape(count, WIN, WIN, 3 * lanes)
        for e in range(3):
            rows = slice(strip * WIN + 2 - e, (strip + 1) * WIN + 2 - e)
            for w in range(count):
                across = slice(w * WIN, (w + 1) * WIN)
                part = total[w, :, :, e * lanes : (e + 1) * lanes]
                acc[rows, across] = part if e == 0 else acc[rows, across] + part

    out_channels = keep_ref.shape[1]

    def finish(strip):
        rows = slice(1 + SHIFT + strip * WIN, 1 + SHIFT + (strip + 1) * WIN)
        centre = acc[rows, SHIFT : SHIFT + breadth, :LANES]
        centre = pltpu.roll(centre.reshape(WIN * breadth, LANES), LANES - out_channels, 1)
        result = (
            acc[rows, SHIFT - 1 : SHIFT - 1 + breadth, :LANES]
            + centre.reshape(WIN, breadth, LANES)
            + acc[rows, SHIFT + 1 : SHIFT + 1 + breadth, LANES : 2 * LANES]
        )
        return windows_of(result).T[:out_channels].astype(BF16)

    results = []
    scatter(0, lambda v: [y_held[w, v] for w in range(count)])
    for strip in range(1, strips):
        if strip == strips - 1:
            scatter(strip, lambda v: [y_held[count + w, v] for w in range(count)])
        else:
            slot = 2 * count + 2 * (strip - 1)
            first = (strip - 1) * (count - 2)
            scatter(
                strip,
                lambda v: [
                    y_held[slot, v],
                    *[inner_ref[first + w, v] for w in range(count - 2)],
                    y_held[slot + 1, v],
                ],
            )
        results.append(finish(strip - 1))
    half = len(results) // 2
    even = is_even("var")
    for strip in range(half):
        keep_ref[strip] = jnp.where(even, results[strip], results[strip + half])
        give_ref[strip] = jnp.where(even, results[strip + half], results[strip])


def refine_kernel(
    heads, first_mark, mine_ref, other_ref, marks_ref, bias_ref, w_qvt, w_key, w_projt, out_ref, final
):
    strips, channels, strip_tokens = mine_ref.shape
    breadth = strip_tokens // WIN
    width = channels // heads
    z = jnp.concatenate(
        [mine_ref[s].astype(F32) + other_ref[s].astype(F32) for s in range(strips)], axis=1
    ) * (1.0 / CODES)
    mean = jnp.sum(z, axis=0, keepdims=True) * (1.0 / channels)
    centred = z - mean
    spread = jnp.sum(centred * centred, axis=0, keepdims=True) * (1.0 / channels)
    normed = centred * lax.rsqrt(spread + EPSILON)
    tall = jnp.concatenate([normed, jnp.zeros((LANES - channels, normed.shape[1]), F32)], axis=0)
    first = lax.axis_index("var") % 2 * strips
    marks = jnp.concatenate([marks_ref[first + s].astype(F32) for s in range(strips)], axis=0)
    lane = iota((1, LANES), 1)
    is_mark = (lane >= first_mark) & (lane < first_mark + MARKS)
    n = jnp.where(is_mark, marks, tall.T).astype(BF16)
    scores, values = heads_of(n, heads, w_qvt[...], w_key[...])
    probabilities = [soft(s + bias_ref[...]) for s in scores]
    lane = iota((channels, LANES), 1)
    branches = []
    for pair in range(len(probabilities) // 2):
        mixed = mix_pair(
            values[:, pair * LANES : (pair + 1) * LANES],
            probabilities[2 * pair],
            probabilities[2 * pair + 1],
            heads,
            width,
        )[0].astype(BF16)
        both = dot(w_projt[...][:, :HEAD_ROWS], mixed)
        even, odd = both[:channels], both[channels:]
        halves = []
        for half in range(2):
            cut = slice(half * LANES, (half + 1) * LANES)
            halves.append(even[:, cut] + pltpu.roll(odd[:, cut], CELLS, 1))
        branches.append(jnp.where(lane < CELLS, halves[0], pltpu.roll(halves[1], CELLS, 1)))
    refined = (z + jnp.concatenate(branches, axis=1)).astype(BF16)
    stacked = jnp.concatenate(
        [refined[:, s * strip_tokens : (s + 1) * strip_tokens] for s in range(strips)], axis=0
    )
    shape = (strip_tokens, WIN * breadth * SCALE)
    cell = iota(shape, 1) // SCALE
    source = (cell % breadth // WIN) * CELLS + (cell // breadth) * WIN + cell % WIN
    wide = dot(stacked, one_hot(iota(shape, 0) == source))
    own = iota(wide.shape, 1) % SCALE == iota(wide.shape, 0) % SCALE
    wide = jnp.where(own, wide, 0.0).astype(BF16)
    shape = (wide.shape[0] // SCALE, wide.shape[0])
    folded = dot(one_hot(iota(shape, 1) // SCALE == iota(shape, 0)), wide)
    colours = channels // (SCALE * SCALE)
    row_lanes = breadth * SCALE
    for s in range(strips):
        for c in range(colours):
            first = (s * colours + c) * SCALE
            for y in range(WIN):
                start = (s * WIN + y) * SCALE
                final[c, start : start + SCALE] = folded[
                    first : first + SCALE, y * row_lanes : (y + 1) * row_lanes
                ]
    out_ref[...] = final[...].astype(BF16)


def is_even(axis):
    return lax.axis_index(axis) % 2 == 0


def swap_pairs(strip, axis, first):
    count = lax.axis_size(axis)
    pairs = [(i, i + 1) for i in range(first, count - 1, 2)]
    return lax.ppermute(strip, axis, pairs + [(j, i) for i, j in pairs])


def whole_swap(a, bit):
    count = lax.axis_size("var")
    return lax.ppermute(a, "var", [(i, i ^ bit) for i in range(count)])


def whole(a):
    return pl.BlockSpec(a.shape, lambda *i: (0,) * a.ndim)


def params(mebibytes):
    return pltpu.CompilerParams(
        dimension_semantics=("arbitrary",), vmem_limit_bytes=mebibytes * 1024 * 1024
    )


def local(
    features,
    labels,
    qkv_weight,
    proj_weight,
    up_weight,
    down_weight,
    swin_bias,
    recon_weight,
    refine_qkv,
    refine_proj,
    refine_bias,
):
    height, breadth, channels = features.shape
    heads = swin_bias.shape[1]
    out_channels = recon_weight.shape[-1]
    refine_heads = refine_bias.shape[0]
    lanes = round_up(channels + MARKS, LANES)
    hidden = round_up(up_weight.shape[-1], LANES)
    operands = (
        features,
        labels.T,
        jnp.swapaxes(qkv_weight, 0, 1),
        jnp.swapaxes(proj_weight, 0, 1),
        jnp.swapaxes(up_weight, 0, 1),
        down_weight.transpose(2, 0, 1),
        jnp.swapaxes(swin_bias, 0, 1),
        jnp.swapaxes(recon_weight, 1, 2),
        refine_qkv,
        refine_proj,
        refine_bias,
    )
    head_rows, refine_rows = heads * HEAD_ROWS, refine_heads * HEAD_ROWS
    shapes = [
        ((2, 2 * head_rows + 16, lanes), BF16),
        ((2, lanes, lanes), BF16),
        ((2, 2 * LANES, lanes), BF16),
        ((2, lanes, hidden), BF16),
        ((2, hidden, lanes), BF16),
        ((VAR_DEV, lanes, 3 * lanes), BF16),
        ((2, VAR_DEV, CELLS, heads * CELLS), F32),
        ((2 * refine_rows + 16, LANES), BF16),
        ((LANES, LANES), BF16),
        ((refine_heads * out_channels, LANES), BF16),
        ((CELLS, refine_heads * CELLS), F32),
        (features.shape, BF16),
        (operands[1].shape, jnp.int32),
    ]
    shapes = [jax.ShapeDtypeStruct(*s) for s in shapes]
    prepared = pl.pallas_call(
        functools.partial(prepare_kernel, heads),
        grid=(1,),
        in_specs=[pl.BlockSpec(memory_space=pltpu.HBM)] * len(operands),
        out_specs=[whole(s) for s in shapes],
        out_shape=shapes,
        scratch_shapes=[
            *[pltpu.VMEM(a.shape, a.dtype) for a in operands[2:]],
            pltpu.VMEM((heads, WIN, LANES), F32),
            pltpu.VMEM((round_up(2 * heads, 8), swin_bias.shape[2]), F32),
            pltpu.SemaphoreType.DMA((len(operands),)),
        ],
        compiler_params=params(12),
        name="prepare",
    )(*[pltpu.with_memory_space_constraint(a, pltpu.HBM) for a in operands])
    *swin, recon, bias, refine_qvt, refine_key, refine_projt, refine_grid = prepared[:-2]
    features, labels_across = prepared[-2:]

    def block_specs(i):
        arrays = (bias, *swin)
        return arrays, [
            pl.BlockSpec((None,) + a.shape[1:], lambda *_, n=a.ndim: (i,) + (0,) * (n - 1))
            for a in arrays
        ]

    def cost(windows):
        return pl.CostEstimate(
            flops=windows * 400_000_000, bytes_accessed=windows * 200_000, transcendentals=0
        )

    arrays, specs = block_specs(0)
    strips = height // WIN
    tokens = WIN * breadth

    pair_axis = lax.axis_size("ty") == 2

    def block_one(places, name):
        rows = len(places) * WIN
        outs = [
            ((VAR_DEV, rows, breadth, lanes), F32),
            ((VAR_DEV, rows * SHIFT, lanes), BF16),
            ((VAR_DEV, rows * SHIFT, lanes), BF16),
        ]
        if places[0] == 0:
            outs += [((VAR_DEV, SHIFT, breadth, lanes), BF16)] * (1 if pair_axis else 2)
        outs = [jax.ShapeDtypeStruct(*o) for o in outs]
        return pl.pallas_call(
            functools.partial(first_kernel, heads, channels, places),
            grid=(1,),
            in_specs=[whole(features), whole(labels_across), *specs],
            out_specs=[whole(o) for o in outs],
            out_shape=outs,
            scratch_shapes=[
                pltpu.VMEM((len(places) * tokens, lanes), F32),
                pltpu.VMEM((2, rows * SHIFT, lanes), F32),
            ],
            compiler_params=params(12 if places[0] == 0 else 18),
            cost_estimate=cost(len(places) * breadth // WIN * VAR_DEV),
            name=name,
        )(features, labels_across, *arrays)

    y_ends, a_ends, b_ends, *own_ends = block_one((0, strips - 1), "block_one_ends")
    across = [swap_pairs(own, "ty", first) for first, own in enumerate(own_ends)]
    y_middle, a_middle, b_middle = block_one(tuple(range(1, strips - 1)), "block_one_middle")
    operands = (*across, a_ends, a_middle, b_ends, b_middle)
    strip_shape = jax.ShapeDtypeStruct((VAR_DEV, (height + 2 * SHIFT) * SHIFT, lanes), BF16)
    strips_out = pl.pallas_call(
        functools.partial(edge_kernel, len(across)),
        grid=(1,),
        in_specs=[whole(a) for a in operands],
        out_specs=[whole(strip_shape)] * 2,
        out_shape=[strip_shape] * 2,
        compiler_params=params(6),
        name="edges",
    )(*operands)
    sides = [swap_pairs(strip, "tx", first) for first, strip in enumerate(strips_out)]

    arrays, specs = block_specs(1)
    inner_count = (strips - 1) * (breadth // WIN - 1)
    outs = [
        jax.ShapeDtypeStruct((inner_count, VAR_DEV, CELLS, lanes), BF16),
        jax.ShapeDtypeStruct((strips, tokens, LANES), BF16),
    ]
    inner, marks = pl.pallas_call(
        functools.partial(inner_kernel, heads, channels),
        grid=(1,),
        in_specs=[whole(y_ends), whole(y_middle), *specs],
        out_specs=[whole(o) for o in outs],
        out_shape=outs,
        compiler_params=params(20),
        cost_estimate=cost(inner_count * VAR_DEV),
        name="block_two_inner",
    )(y_ends, y_middle, *arrays)

    tall, wide = height + 2 * SHIFT, breadth + 2 * SHIFT
    slots = 2 * (tall + wide) // WIN - 4
    operands = (y_ends, y_middle, *across, *sides, inner)
    half_shape = jax.ShapeDtypeStruct((strips // 2, out_channels, tokens), BF16)
    keep, give = pl.pallas_call(
        functools.partial(outer_kernel, heads, channels, len(across)),
        grid=(1,),
        in_specs=[*[whole(a) for a in operands], *specs, whole(recon)],
        out_specs=[whole(half_shape)] * 2,
        out_shape=[half_shape] * 2,
        scratch_shapes=[
            pltpu.VMEM((WIN, wide, lanes), F32),
            pltpu.VMEM((slots, VAR_DEV, CELLS, lanes), F32),
            pltpu.VMEM((slots, VAR_DEV, CELLS, lanes), BF16),
            pltpu.VMEM((tall + WIN, wide, lanes), F32),
        ],
        compiler_params=params(26),
        name="block_two_border",
    )(*operands, *arrays, recon)

    mine = (keep.astype(F32) + whole_swap(give, 1).astype(F32)).astype(BF16)
    other = whole_swap(mine, 2)
    colours = out_channels // (SCALE * SCALE)
    operands = (mine, other, marks, refine_grid, refine_qvt, refine_key, refine_projt)
    out_shape = (colours, height * SCALE // 2, breadth * SCALE)
    refined = pl.pallas_call(
        functools.partial(refine_kernel, refine_heads, channels % LANES),
        grid=(1,),
        in_specs=[whole(a) for a in operands],
        out_specs=pl.BlockSpec(out_shape, lambda i: (0, 0, 0)),
        out_shape=jax.ShapeDtypeStruct(out_shape, BF16),
        scratch_shapes=[pltpu.VMEM(out_shape, F32)],
        compiler_params=params(8),
        name="refinement",
    )(*operands)
    received = whole_swap(refined, 1)
    even = is_even("var")
    halves = jnp.where(even, refined, received), jnp.where(even, received, refined)
    return jnp.concatenate(halves, axis=1).astype(F32)


def solution(mesh):
    placed = (P("ty", "tx", None), P("ty", "tx"), P(), P(), P(), P(), P(), P(), P(), P(), P())
    return jax.shard_map(
        local, mesh=mesh, in_specs=placed, out_specs=P(None, "ty", "tx"), check_vma=False
    )
```

```python
import functools

import jax
import jax.numpy as jnp
from jax import lax
from jax.experimental import pallas as pl
from jax.experimental.pallas import tpu as pltpu
from jax.sharding import PartitionSpec as P

WIN = 8
CELLS = WIN * WIN
SHIFT = 4
SCALE = 4
VAR_DEV = 2
CODES = 8
LANES = 128
HEAD_ROWS = 32
CLASSES = 4
MARKS = CLASSES + 2
CONSTANT = -2.0
SIDE = 2 * WIN - 1

EPSILON = 1e-05
LOG2E = 1.4426950408889634
BIG = float(2.0**100)
ERF_TANH = (0.7975076, 0.0370060, -0.00035159)
REACH = 36.0

NN = (((1,), (0,)), ((), ()))
NT = (((1,), (1,)), ((), ()))
F32 = jnp.float32
BF16 = jnp.bfloat16


def dot(a, b, dims=NN):
    return lax.dot_general(a, b, dims, preferred_element_type=F32)


def iota(shape, dim):
    return lax.broadcasted_iota(jnp.int32, shape, dim)


def round_up(size, multiple):
    return -(-size // multiple) * multiple


def one_hot(condition):
    return jnp.where(condition, 1.0, 0.0).astype(BF16)


def exact(a, b, dims=NN):
    return dot(a, b, dims).astype(BF16)


def pick_rows(source, size):
    return one_hot(iota((1, size), 1) == source)


def pick_columns(source, size):
    return one_hot(iota((size, 1), 0) == source)


def head_source(index, heads, width, first=0):
    unit = index % HEAD_ROWS
    keep = (unit < width) & (index < heads * HEAD_ROWS)
    return jnp.where(keep, first + index // HEAD_ROWS * width + unit, -1)


def query_value_source(heads, width, channels):
    row = iota((2 * heads * HEAD_ROWS + 16, 1), 0)
    values = row - heads * HEAD_ROWS - 16
    return jnp.where(
        values < 0,
        head_source(row, heads, width),
        head_source(jnp.maximum(values, 0), heads, width, 2 * channels),
    )


def query_value_marks(heads, width, lanes, first_lane):
    row = iota((2 * heads * HEAD_ROWS + 16, 1), 0)
    lane = iota((1, lanes), 1) - first_lane
    mark = row - heads * HEAD_ROWS
    is_class = (mark >= 0) & (mark < CLASSES)
    differ = jnp.where(is_class | (mark == CLASSES), -BIG / CONSTANT, 0.0)
    unit = (mark - 16) % HEAD_ROWS
    ones = jnp.where((mark >= 16) & (unit == width), 1.0 / CONSTANT, 0.0)
    same = jnp.where(is_class & (mark == lane), BIG, 0.0)
    return same + jnp.where(lane == CLASSES + 1, differ + ones, 0.0)


def key_marks(rows, lanes, first_row, first_lane):
    row = iota((rows, 1), 0) - first_row
    lane = iota((1, lanes), 1) - first_lane
    is_class = (lane >= 0) & (lane < CLASSES)
    same = jnp.where(is_class & (row == lane), 1.0, 0.0)
    pad = jnp.where(row == CLASSES, -1.0, jnp.where(row == CLASSES + 1, 1.0 / CONSTANT, 0.0))
    return same + jnp.where(lane == CLASSES, pad, 0.0)


def bias_rows(table, turn, flip_rows, flip_cols):
    shape = (1, WIN * LANES)
    lane = iota(shape, 1)
    row_step = lane % LANES // WIN - (WIN - 1)
    col_step = lane % WIN - lane // LANES
    row_step = jnp.where(flip_rows, -row_step, row_step)
    col_step = jnp.where(flip_cols, -col_step, col_step)
    lead = jnp.where(turn, col_step, row_step)
    trail = jnp.where(turn, row_step, col_step)
    index = (lead + WIN - 1) * SIDE + trail + WIN - 1
    pick = one_hot(iota((table.shape[1], WIN * LANES), 0) == index)
    rest = table * LOG2E
    parts = []
    for _ in range(3):
        parts.append(rest.astype(BF16))
        rest = rest - parts[-1].astype(F32)
    moved = dot(jnp.concatenate(parts, axis=0), pick)
    size = table.shape[0]
    return moved[:size] + moved[size : 2 * size] + moved[2 * size :]


def bias_grid(rows, rows_ref, store):
    heads = rows.shape[0]
    for key_col in range(WIN):
        rows_ref[0:heads, key_col, :] = rows[:, key_col * LANES : (key_col + 1) * LANES]
    half = iota((WIN, LANES), 1)
    for pair in range(heads // 2):
        even, odd = rows_ref[2 * pair], rows_ref[2 * pair + 1]
        for key_row in range(WIN):
            start = (WIN - 1 - key_row) * WIN
            left = pltpu.roll(even, (LANES - start) % LANES, 1)
            right = pltpu.roll(odd, (LANES - start + CELLS) % LANES, 1)
            store(key_row, pair, jnp.where(half < CELLS, left, right))


def prepare_kernel(
    heads,
    features_ref,
    labels_ref,
    *refs,
):
    sources, outs, scratch = refs[:6], refs[6:15], refs[15:]
    held, spreads, (rows_ref, tables_ref, semaphores) = scratch[:6], scratch[6:10], scratch[10:]
    (
        qvt_out,
        key_out,
        proj_out,
        up_out,
        down_out,
        recon_out,
        bias_out,
        features_out,
        labels_out,
    ) = outs
    arrivals = [
        pltpu.make_async_copy(source, target, semaphores.at[i])
        for i, (source, target) in enumerate(
            zip(
                (*sources, features_ref, labels_ref), (*held, features_out, labels_out)
            )
        )
    ]
    for arrival in arrivals:
        arrival.start()
    (
        qkv_ref,
        proj_ref,
        up_ref,
        down_ref,
        swin_bias_ref,
        recon_ref,
    ) = held
    channels, blocks, hidden = up_ref.shape
    width = channels // heads
    lanes = key_out.shape[1]
    head_rows = heads * HEAD_ROWS
    taps, out, _ = recon_ref.shape
    both = blocks * channels

    arrivals[4].wait()
    for i in range(blocks):
        tables_ref[i * heads : (i + 1) * heads] = swin_bias_ref[:, i]
    rows = []
    for v in range(VAR_DEV):
        code = lax.axis_index("var") * VAR_DEV + v
        turn, flip_rows, flip_cols = code // 4 == 1, code // 2 % 2 == 1, code % 2 == 1
        rows.append(bias_rows(tables_ref[: blocks * heads], turn, flip_rows, flip_cols))
    row = iota((2 * LANES, 1), 0)
    head, unit = row % LANES // HEAD_ROWS * 2 + row // LANES, row % HEAD_ROWS
    proj_source = jnp.where((head < heads) & (unit < width), head * width + unit, -1)
    query_values = pick_rows(query_value_source(heads, width, channels), 3 * channels)
    keys = pick_columns(head_source(iota((1, lanes), 1), heads, width, channels), 3 * channels)
    hidden_rows = pick_rows(iota((down_out.shape[1], 1), 0), hidden)
    proj_rows = pick_rows(proj_source, lanes)
    for arrival in (*arrivals[:4], arrivals[5]):
        arrival.wait()

    def block_rows(ref, spread_ref):
        size = ref.shape[2]
        rows = ref[...].reshape(both, size).astype(F32)
        pieces = [[] for _ in range(blocks)]
        for at in range(0, size, LANES):
            used = min(LANES, size - at)
            place = at // LANES
            spread_ref[place, :both, :used] = rows[:, at : at + used]
            spread_ref[place, both:] = jnp.zeros((blocks * lanes - both, LANES), F32)
            for i in range(blocks):
                piece = spread_ref[place, pl.ds(i, lanes, stride=blocks), :]
                pieces[i].append(piece[:, :used].astype(BF16))
        return [jnp.concatenate(piece, axis=1) for piece in pieces]

    qkv, proj, up, down = (
        block_rows(ref, spread)
        for ref, spread in zip((qkv_ref, proj_ref, up_ref, down_ref), spreads)
    )

    pad = pick_rows(iota((lanes, 1), 0), channels)
    kernel = exact(pad, recon_ref[...].reshape(taps * out, channels), NT)
    row = iota((2 * head_rows + 16, 1), 0)
    scale = jnp.where(row < head_rows, width**-0.5 * LOG2E, 1.0)
    query_add = query_value_marks(heads, width, lanes, channels)
    key_add = key_marks(lanes, lanes, channels, head_rows)
    for i in range(blocks):
        qvt_out[i] = (dot(query_values, qkv[i], NT) * scale + query_add).astype(BF16)
        key_out[i] = (dot(qkv[i], keys) + key_add).astype(BF16)
        proj_out[i] = jnp.zeros(proj_out.shape[1:], BF16)
        proj_out[i, :, :channels] = exact(proj_rows, proj[i])
        up_out[i] = jnp.zeros(up_out.shape[1:], BF16)
        up_out[i, :, :hidden] = up[i]
        down_out[i] = (dot(hidden_rows, down[i], NT) * 0.5).astype(BF16)
    for v in range(VAR_DEV):
        code = lax.axis_index("var") * VAR_DEV + v
        turn, flip_rows, flip_cols = code // 4 == 1, code // 2 % 2 == 1, code % 2 == 1
        lane = iota((1, 4 * LANES), 1)
        tile, lane = lane // LANES, lane % LANES
        part = jnp.where(lane >= 2 * out, 2, jnp.where(lane >= out, 1, 0))
        is_last = tile == 3
        is_left = (tile == 0) & (part == 2)
        row_step = jnp.where(is_last, part, jnp.where(is_left, 2, tile)) - 1
        col_step = jnp.where(is_last | is_left, 2, part) - 1
        channel = lane - part * out + jnp.where(is_left, LANES - 2 * out, 0)
        used = (channel < out) & (is_last | is_left | (part < 2))
        row_step = jnp.where(flip_rows, -row_step, row_step)
        col_step = jnp.where(flip_cols, -col_step, col_step)
        tap = (jnp.where(turn, col_step, row_step) + 1) * 3
        tap = tap + jnp.where(turn, row_step, col_step) + 1
        sub_row = channel % (SCALE * SCALE) // SCALE
        sub_col = channel % SCALE
        sub_row = jnp.where(flip_rows, SCALE - 1 - sub_row, sub_row)
        sub_col = jnp.where(flip_cols, SCALE - 1 - sub_col, sub_col)
        source = channel // (SCALE * SCALE) * SCALE * SCALE
        source = source + jnp.where(turn, sub_col, sub_row) * SCALE
        source = tap * out + source + jnp.where(turn, sub_row, sub_col)
        source = jnp.where(used, source, -1)
        recon_out[v] = exact(kernel, pick_columns(source, taps * out))

    for v in range(VAR_DEV):
        for i in range(blocks):

            def store(key_row, pair, value):
                at = slice(key_row * WIN, (key_row + 1) * WIN)
                bias_out[i, v, at, pair * LANES : (pair + 1) * LANES] = value

            bias_grid(rows[v][i * heads : (i + 1) * heads], rows_ref, store)

    for arrival in arrivals[6:]:
        arrival.wait()


def prepare_refine_kernel(
    mark, after_ref, qkv_source, proj_source, bias_source, *refs
):
    refine_qvt_out, refine_key_out, refine_proj_out, refine_bias_out = refs[:4]
    refine_qkv_ref, refine_proj_ref, refine_bias_ref, rows_ref, semaphores = refs[4:]
    arrivals = [
        pltpu.make_async_copy(source, target, semaphores.at[i])
        for i, (source, target) in enumerate(
            zip((qkv_source, proj_source, bias_source), refs[4:7])
        )
    ]
    for arrival in arrivals:
        arrival.start()
    for arrival in arrivals:
        arrival.wait()
    out = refine_proj_ref.shape[0]
    refine_heads = refine_bias_ref.shape[0]
    refine_width = out // refine_heads
    refine_rows = refine_heads * HEAD_ROWS
    never = lax.axis_index("var") < 0
    refine_table = bias_rows(refine_bias_ref[...], never, never, never)
    weight = refine_qkv_ref[...]
    source = query_value_source(refine_heads, refine_width, out)
    refine_moved = exact(pick_rows(source, 3 * out), weight, NT)
    source = head_source(iota((1, LANES), 1), refine_heads, refine_width, out)
    refine_keys = exact(weight, pick_columns(source, 3 * out))
    refine_proj = []
    for h in range(refine_heads):
        row = iota((LANES, 1), 0)
        source = jnp.where(row < refine_width, row + h * refine_width, -1)
        refine_proj.append(exact(pick_rows(source, out), refine_proj_ref[...]))

    row = iota((2 * refine_rows + 16, 1), 0)
    scale = jnp.where(row < refine_rows, refine_width**-0.5 * LOG2E, 1.0)
    out_pad = pick_rows(iota((LANES, 1), 0), out)
    refine_qvt_out[...] = (
        dot(refine_moved, out_pad, NT) * scale
        + query_value_marks(refine_heads, refine_width, LANES, mark)
    ).astype(BF16)
    refine_key_out[...] = (
        dot(out_pad, refine_keys) + key_marks(LANES, LANES, mark, refine_rows)
    ).astype(BF16)
    for h in range(refine_heads):
        square = dot(refine_proj[h], out_pad, NT)
        refine_proj_out[h * out : (h + 1) * out] = square.T[:out].astype(BF16)
    def store_refine(key_row, pair, value):
        refine_bias_out[key_row * WIN : (key_row + 1) * WIN] = value

    bias_grid(refine_table, rows_ref, store_refine)


def twice_gelu(x):
    x = x.astype(BF16)
    square = jnp.minimum(x * x, BF16(REACH))
    first, second, third = (BF16(factor) for factor in ERF_TANH)
    series = (square * third + second) * square + first
    return x + x * jnp.tanh(x * series)


def normalize(x, channels, keep_marks):
    tiles = [x[:, i : i + LANES] for i in range(0, x.shape[1], LANES)]
    inside = iota((1, LANES), 1) < channels - (len(tiles) - 1) * LANES
    mean = jnp.sum(sum(tiles[1:], tiles[0]), axis=1, keepdims=True) * (1.0 / channels)
    centred = [tile - mean for tile in tiles]
    centred[-1] = jnp.where(inside, centred[-1], 0.0)
    squares = [tile * tile for tile in centred]
    spread = jnp.sum(sum(squares[1:], squares[0]), axis=1, keepdims=True) * (1.0 / channels)
    scale = lax.rsqrt(spread + EPSILON)
    result = [tile * scale for tile in centred]
    if keep_marks:
        result[-1] = jnp.where(inside, result[-1], tiles[-1])
    return jnp.concatenate(result, axis=1).astype(BF16)


def split_queries(queries, heads):
    pairs = heads // 2
    head_rows = heads * HEAD_ROWS
    left = iota((1, LANES), 1) < CELLS
    turned = pltpu.roll(queries, CELLS, 1).astype(BF16)
    queries = queries.astype(BF16)
    depth = round_up(queries.shape[0], LANES)
    zero = jnp.zeros((HEAD_ROWS, LANES), BF16)
    results = []
    for even, odd in ((queries, turned), (turned, queries)):
        marks = jnp.where(left, even[head_rows:], odd[head_rows:])
        columns = []
        for pair in range(pairs):
            at = pair * 2 * HEAD_ROWS
            rows = [zero] * heads
            rows[2 * pair] = jnp.where(left, even[at : at + HEAD_ROWS], zero)
            rows[2 * pair + 1] = jnp.where(left, zero, odd[at + HEAD_ROWS : at + 2 * HEAD_ROWS])
            rows.append(marks)
            rows.append(jnp.zeros((depth - queries.shape[0], LANES), BF16))
            columns.append(jnp.concatenate(rows, axis=0))
        results.append(jnp.concatenate(columns, axis=1) if pairs > 1 else columns[0])
    return results


def heads_of(n, heads, w_qvt, w_key):
    mark_rows = heads * HEAD_ROWS + 16
    both = dot(w_qvt, n, NT)
    queries = both[:mark_rows]
    values = both[mark_rows:].astype(BF16)
    keys = dot(n, w_key).astype(BF16)
    scores = []
    for place in range(n.shape[0] // LANES):
        cut = slice(place * LANES, (place + 1) * LANES)
        for half, stationary in enumerate(split_queries(queries[:, cut], heads)):
            at = place * LANES + half * CELLS
            scores.append(dot(keys[at : at + CELLS], stationary))
    return scores, values


def soft(scores):
    largest = jnp.max(scores, axis=0, keepdims=True)
    return jnp.exp2(scores - largest).astype(BF16)


def mix_pair(values, first, second, heads, ones_row):
    zero = jnp.zeros((CELLS, LANES), BF16)
    lane = iota((HEAD_ROWS, 2 * LANES), 1) % LANES
    mixed = []
    for pair in range(heads // 2):
        cut = slice(pair * LANES, (pair + 1) * LANES)
        stationary = jnp.concatenate(
            [
                jnp.concatenate([first[:, cut], zero], axis=1),
                jnp.concatenate([zero, second[:, cut]], axis=1),
            ],
            axis=0,
        )
        result = dot(values[pair * CELLS : (pair + 1) * CELLS], stationary)
        joined = jnp.where(lane < CELLS, result[:HEAD_ROWS], result[HEAD_ROWS:])
        mixed.append(joined * pl.reciprocal(joined[ones_row : ones_row + 1]))
    return mixed


def swin_unit(x, pairs, results, heads, channels, bias, w_qvt, w_key, w_proj, w_up, w_down):
    width = channels // heads
    mark_rows = heads * HEAD_ROWS + 16
    n = normalize(x, channels, True)
    yield
    both = dot(w_qvt[...], n, NT)
    queries = both[:mark_rows]
    values = both[mark_rows:].astype(BF16)
    keys = dot(n, w_key[...]).astype(BF16)
    yield
    scores = []
    for place in range(x.shape[0] // LANES):
        cut = slice(place * LANES, (place + 1) * LANES)
        for half, stationary in enumerate(split_queries(queries[:, cut], heads)):
            at = place * LANES + half * CELLS
            scores.append(dot(keys[at : at + CELLS], stationary))
    yield
    weights = [
        (soft(scores[2 * place] + bias(a)), soft(scores[2 * place + 1] + bias(b)))
        for place, a, b in pairs
    ]
    yield
    pad = jnp.zeros((LANES - heads // 2 * HEAD_ROWS, 2 * LANES), F32)
    blocks = []
    for (place, _, _), (first, second) in zip(pairs, weights):
        cut = slice(place * LANES, (place + 1) * LANES)
        mixed = mix_pair(values[:, cut], first, second, heads, width)
        blocks.append(jnp.concatenate(mixed + [pad], axis=0).astype(BF16))
    yield
    outputs = []
    for block in blocks:
        for half in range(2):
            turned = block[:, half * LANES : (half + 1) * LANES].T
            outputs.append(jnp.concatenate([turned[:CELLS], turned[CELLS:]], axis=1))
    outputs = jnp.concatenate(outputs, axis=0)
    yield
    x = jnp.concatenate([x[place * LANES : (place + 1) * LANES] for place, _, _ in pairs], axis=0)
    h = x + dot(outputs, w_proj[...])
    yield
    n = normalize(h, channels, False)
    yield
    hidden = dot(n, w_up[...])
    yield
    hidden = twice_gelu(hidden)
    yield
    y = h + dot(hidden, w_down[...])
    results.extend(y[i * LANES : (i + 1) * LANES] for i in range(len(pairs)))


def swin_block(x, pairs, unit, lag, *args):
    places = x.shape[0] // LANES
    units = []
    for low in range(0, places, unit):
        high = min(low + unit, places)
        picked = [i for i, pair in enumerate(pairs) if low <= pair[0] < high]
        moved = [(pairs[i][0] - low, *pairs[i][1:]) for i in picked]
        found = []
        units.append((picked, found, swin_unit(x[low * LANES : high * LANES], moved, found, *args)))
    running = dict(enumerate(units))
    tick = 0
    while running:
        for number in sorted(running):
            if tick >= number * lag and next(running[number][2], StopIteration) is StopIteration:
                del running[number]
        tick += 1
    results = [None] * len(pairs)
    for picked, found, _ in units:
        for i, result in zip(picked, found):
            results[i] = result
    return results


def windows_of(grid):
    lanes = grid.shape[2]
    return jnp.concatenate(
        [
            grid[:, w * WIN : (w + 1) * WIN].reshape(CELLS, lanes)
            for w in range(grid.shape[1] // WIN)
        ],
        axis=0,
    )


def first_kernel(heads, channels, strips, x_ref, labels_ref, bias_ref, *refs):
    ends = strips[0] == 0
    *weights, y_ref, side_a_ref, side_b_ref = refs[:8]
    held, side = refs[-2:]
    breadth = x_ref.shape[1]
    count = breadth // WIN
    tokens, lanes = held.shape
    part = tokens // len(strips)
    rows_total = labels_ref.shape[1]
    for k, strip in enumerate(strips):
        rows = x_ref[strip * WIN : (strip + 1) * WIN].astype(F32)
        held[k * part : (k + 1) * part, :channels] = windows_of(rows)
    labels = labels_ref[...].astype(F32).astype(BF16)
    row_gap = iota((CELLS, rows_total), 1) - iota((CELLS, rows_total), 0) // WIN
    col_gap = iota((CELLS, breadth), 1) - iota((CELLS, breadth), 0) % WIN
    by_row = [dot(one_hot(row_gap == strip * WIN), labels, NT) for strip in strips]
    cells = [jnp.where(col_gap == w * WIN, rows, 0.0) for rows in by_row for w in range(count)]
    label = dot(
        jnp.concatenate(cells, axis=0).astype(BF16), jnp.ones((breadth, LANES), BF16)
    )
    lane = iota((1, LANES), 1) - channels % LANES
    wanted = jnp.where((lane >= 0) & (lane < CLASSES), lane + 1, -1).astype(F32)
    fixed = jnp.where(lane == CLASSES, 1.0, jnp.where(lane == CLASSES + 1, CONSTANT, 0.0))
    tail = jnp.where(lane < 0, held[:, lanes - LANES :], jnp.where(label == wanted, 1.0, fixed))
    x = jnp.concatenate([held[:, : lanes - LANES], tail], axis=1)
    places = tokens // LANES
    pairs = [(place, v, v) for v in range(VAR_DEV) for place in range(places)]
    results = swin_block(x, pairs, x.shape[0], 1, heads, channels, lambda v: bias_ref[v], *weights)
    for v in range(VAR_DEV):
        for k in range(len(strips)):
            windows = []
            for w in range(count):
                group = k * count + w
                block = results[v * places + group // 2]
                at = group % 2 * CELLS
                windows.append(block[at : at + CELLS].reshape(WIN, WIN, lanes))
            y_ref[v, k * WIN : (k + 1) * WIN] = jnp.concatenate(windows, axis=1)
            at = k * WIN * SHIFT
            for r in range(WIN):
                rows = slice(at + r * SHIFT, at + (r + 1) * SHIFT)
                side[0, rows] = windows[0][r, :SHIFT]
                side[1, rows] = windows[-1][r, SHIFT:]
        left, right = side[0].astype(BF16), side[1].astype(BF16)
        even = is_even("tx")
        side_a_ref[v] = jnp.where(even, right, left)
        side_b_ref[v] = jnp.where(even, left, right)
    if ends:
        top, bottom = y_ref[:, :SHIFT].astype(BF16), y_ref[:, 2 * WIN - SHIFT :].astype(BF16)
        even = is_even("ty")
        refs[8][...] = jnp.where(even, bottom, top)
        if len(refs) == 12:
            refs[9][...] = jnp.where(even, top, bottom)


def tile_rows(ends_ref, middle_ref, v, first, count, columns):
    height = middle_ref.shape[1] + 2 * WIN
    pieces = []
    while count > 0:
        if first < WIN:
            ref, at, limit = ends_ref, first, WIN - first
        elif first < height - WIN:
            ref, at, limit = middle_ref, first - WIN, height - WIN - first
        else:
            ref, at, limit = ends_ref, first - height + 2 * WIN, height - first
        taken = min(count, limit)
        pieces.append(ref[v, at : at + taken, columns])
        first, count = first + taken, count - taken
    return pieces[0] if len(pieces) == 1 else jnp.concatenate(pieces, axis=0)


def inner_kernel(heads, channels, ends_ref, middle_ref, bias_ref, *refs):
    *weights, y_ref, marks_ref = refs
    breadth, lanes = middle_ref.shape[2:]
    strips = middle_ref.shape[1] // WIN + 2
    count = breadth // WIN - 1
    for strip in range(strips):
        rows = tile_rows(ends_ref, middle_ref, 0, strip * WIN, WIN, slice(None))
        marks_ref[strip] = windows_of(rows[:, :, lanes - LANES :]).astype(BF16)
    x = jnp.concatenate(
        [
            tile_rows(
                ends_ref,
                middle_ref,
                v,
                strip * WIN + SHIFT,
                WIN,
                slice(SHIFT + w * WIN, SHIFT + (w + 1) * WIN),
            ).reshape(CELLS, lanes)
            for strip in range(strips - 1)
            for w in range(count)
            for v in range(VAR_DEV)
        ],
        axis=0,
    )
    pairs = [(w, 0, 1) for w in range((strips - 1) * count)]
    results = swin_block(x, pairs, 4, 1, heads, channels, lambda v: bias_ref[v], *weights)
    for w, result in enumerate(results):
        y_ref[w] = result.astype(BF16).reshape(VAR_DEV, CELLS, lanes)


def received(refs, axis, after, place):
    value = refs[0][place].astype(F32)
    other = refs[1][place].astype(F32) if len(refs) > 1 else 0.0
    return jnp.where(is_even(axis) == after, value, other)


def edge_kernel(swaps, *refs):
    across, own, outs = refs[:swaps], refs[swaps : swaps + 4], refs[swaps + 4 :]
    breadth = across[0].shape[2]
    half = WIN * SHIFT
    corner = SHIFT * SHIFT
    for first in range(2):
        ends, middle = own[2 * first : 2 * first + 2]
        out = outs[first]
        at_right = is_even("tx") == (first == 0)
        last = out.shape[1] - corner
        for v in range(VAR_DEV):
            for start, after in ((0, False), (last, True)):
                rows = received(across, "ty", after, v)
                cells = jnp.where(at_right, rows[:, breadth - SHIFT :], rows[:, :SHIFT])
                cells = jnp.concatenate([cells[r] for r in range(SHIFT)], axis=0)
                out[v, start : start + corner] = cells.astype(BF16)
            out[v, corner : corner + half] = ends[v, :half]
            out[v, corner + half : last - half] = middle[v]
            out[v, last - half : last] = ends[v, half:]


def outer_kernel(
    heads,
    channels,
    swaps,
    ends_ref,
    middle_ref,
    *refs,
):
    across, sides, (inner_ref, bias_ref) = refs[:swaps], refs[swaps : swaps + 2], refs[swaps + 2 : swaps + 4]
    refs = refs[swaps + 4 :]
    *weights, w_recon, keep_ref, give_ref, rows_held, x_held, y_held, acc = refs
    lanes = middle_ref.shape[3]
    height, breadth = middle_ref.shape[1] + 2 * WIN, middle_ref.shape[2]
    tall, wide = height + 2 * SHIFT, breadth + 2 * SHIFT
    strips, count = tall // WIN, wide // WIN
    always = iota((1, lanes), 1) == channels + CLASSES + 1

    def marked(refs, axis, after, place):
        return jnp.where(always, CONSTANT, received(refs, axis, after, place))

    for v in range(VAR_DEV):
        for end in range(2):
            outside, inside = (0, SHIFT) if end == 0 else (SHIFT, 0)
            corner = 0 if end == 0 else (tall - SHIFT) * SHIFT
            first = 0 if end == 0 else 2 * WIN - SHIFT
            between = slice(SHIFT, SHIFT + breadth)
            rows_held[outside : outside + SHIFT, between] = marked(
                across, "ty", end == 1, v
            )
            rows_held[inside : inside + SHIFT, between] = ends_ref[v, first : first + SHIFT]
            side_first = SHIFT * SHIFT if end == 0 else (tall - 2 * SHIFT) * SHIFT
            for side, at in ((0, 0), (1, wide - SHIFT)):
                for rows, start in ((outside, corner), (inside, side_first)):
                    cut = (v, slice(start, start + SHIFT * SHIFT))
                    piece = marked(sides, "tx", side == 1, cut)
                    rows_held[rows : rows + SHIFT, at : at + SHIFT] = piece.reshape(
                        SHIFT, SHIFT, lanes
                    )
            for w in range(count):
                x_held[end * count + w, v] = rows_held[:, w * WIN : (w + 1) * WIN].reshape(
                    CELLS, lanes
                )
        for strip in range(1, strips - 1):
            cut = slice(strip * WIN * SHIFT, (strip + 1) * WIN * SHIFT)
            for end in range(2):
                piece = marked(sides, "tx", end == 1, (v, cut))
                piece = piece.reshape(WIN, SHIFT, lanes)
                at = 0 if end == 0 else breadth - SHIFT
                near = slice(at, at + SHIFT)
                own = tile_rows(ends_ref, middle_ref, v, strip * WIN - SHIFT, WIN, near)
                both = [piece, own] if end == 0 else [own, piece]
                slot = 2 * count + 2 * (strip - 1) + end
                x_held[slot, v] = jnp.concatenate(both, axis=1).reshape(CELLS, lanes)

    slots = x_held.shape[0]
    x = x_held[...].reshape(slots * VAR_DEV * CELLS, lanes)
    pairs = [(w, 0, 1) for w in range(slots)]
    results = swin_block(x, pairs, 6, 3, heads, channels, lambda v: bias_ref[v], *weights)
    at = channels + CLASSES
    for w in range(slots):
        valid = x[w * LANES : (w + 1) * LANES, at : at + 1]
        y_held[w] = (results[w] * valid).astype(BF16).reshape(VAR_DEV, CELLS, lanes)

    weights = w_recon[...].reshape(VAR_DEV * lanes, w_recon.shape[2])
    out_channels = keep_ref.shape[1]

    def scatter(strip, windows):
        tokens = [jnp.concatenate(windows(v), axis=0) for v in range(VAR_DEV)]
        total = dot(jnp.concatenate(tokens, axis=1), weights)
        tiles = [total[:, i : i + LANES] for i in range(0, total.shape[1], LANES)]
        spare = LANES - 2 * out_channels
        lane = iota((1, LANES), 1)
        last = jnp.where(
            lane < spare,
            pltpu.roll(tiles[3], spare, 1),
            pltpu.roll(tiles[0], 2 * spare, 1),
        )
        after = [tiles[3], pltpu.roll(tiles[3], LANES - out_channels, 1), last]
        for e in range(3):
            rows = slice(strip * WIN + 2 - e, (strip + 1) * WIN + 2 - e)
            for at, tile in ((0, tiles[e]), (LANES, after[e])):
                tile = tile.reshape(count, WIN, WIN, LANES)
                for w in range(count):
                    place = (rows, slice(w * WIN, (w + 1) * WIN), slice(at, at + LANES))
                    acc[place] = tile[w] if e == 0 else acc[place] + tile[w]

    def finish(strip):
        rows = slice(1 + SHIFT + strip * WIN, 1 + SHIFT + (strip + 1) * WIN)
        centre = acc[rows, SHIFT : SHIFT + breadth, :LANES]
        centre = pltpu.roll(centre.reshape(WIN * breadth, LANES), LANES - out_channels, 1)
        result = (
            acc[rows, SHIFT - 1 : SHIFT - 1 + breadth, :LANES]
            + centre.reshape(WIN, breadth, LANES)
            + acc[rows, SHIFT + 1 : SHIFT + 1 + breadth, LANES : 2 * LANES]
        )
        return windows_of(result).T[:out_channels].astype(BF16)

    results = []
    scatter(0, lambda v: [y_held[w, v] for w in range(count)])
    for strip in range(1, strips):
        if strip == strips - 1:
            scatter(strip, lambda v: [y_held[count + w, v] for w in range(count)])
        else:
            slot = 2 * count + 2 * (strip - 1)
            first = (strip - 1) * (count - 2)
            scatter(
                strip,
                lambda v: [
                    y_held[slot, v],
                    *[inner_ref[first + w, v] for w in range(count - 2)],
                    y_held[slot + 1, v],
                ],
            )
        results.append(finish(strip - 1))
    half = len(results) // 2
    even = is_even("var")
    for strip in range(half):
        keep_ref[strip] = jnp.where(even, results[strip], results[strip + half])
        give_ref[strip] = jnp.where(even, results[strip + half], results[strip])


def refine_kernel(
    heads, first_mark, mine_ref, other_ref, marks_ref, bias_ref, w_qvt, w_key, w_projt, out_ref, final
):
    strips, channels, strip_tokens = mine_ref.shape
    breadth = strip_tokens // WIN
    width = channels // heads
    z = jnp.concatenate(
        [mine_ref[s].astype(F32) + other_ref[s].astype(F32) for s in range(strips)], axis=1
    ) * (1.0 / CODES)
    mean = jnp.sum(z, axis=0, keepdims=True) * (1.0 / channels)
    centred = z - mean
    spread = jnp.sum(centred * centred, axis=0, keepdims=True) * (1.0 / channels)
    normed = centred * lax.rsqrt(spread + EPSILON)
    tall = jnp.concatenate([normed, jnp.zeros((LANES - channels, normed.shape[1]), F32)], axis=0)
    first = lax.axis_index("var") % 2 * strips
    marks = jnp.concatenate([marks_ref[first + s].astype(F32) for s in range(strips)], axis=0)
    lane = iota((1, LANES), 1)
    is_mark = (lane >= first_mark) & (lane < first_mark + MARKS)
    n = jnp.where(is_mark, marks, tall.T).astype(BF16)
    scores, values = heads_of(n, heads, w_qvt[...], w_key[...])
    probabilities = [soft(s + bias_ref[...]) for s in scores]
    lane = iota((channels, LANES), 1)
    branches = []
    for pair in range(len(probabilities) // 2):
        mixed = mix_pair(
            values[:, pair * LANES : (pair + 1) * LANES],
            probabilities[2 * pair],
            probabilities[2 * pair + 1],
            heads,
            width,
        )[0].astype(BF16)
        both = dot(w_projt[...][:, :HEAD_ROWS], mixed)
        even, odd = both[:channels], both[channels:]
        halves = []
        for half in range(2):
            cut = slice(half * LANES, (half + 1) * LANES)
            halves.append(even[:, cut] + pltpu.roll(odd[:, cut], CELLS, 1))
        branches.append(jnp.where(lane < CELLS, halves[0], pltpu.roll(halves[1], CELLS, 1)))
    refined = (z + jnp.concatenate(branches, axis=1)).astype(BF16)
    stacked = jnp.concatenate(
        [refined[:, s * strip_tokens : (s + 1) * strip_tokens] for s in range(strips)], axis=0
    )
    shape = (strip_tokens, WIN * breadth * SCALE)
    cell = iota(shape, 1) // SCALE
    source = (cell % breadth // WIN) * CELLS + (cell // breadth) * WIN + cell % WIN
    wide = dot(stacked, one_hot(iota(shape, 0) == source))
    own = iota(wide.shape, 1) % SCALE == iota(wide.shape, 0) % SCALE
    wide = jnp.where(own, wide, 0.0).astype(BF16)
    shape = (wide.shape[0] // SCALE, wide.shape[0])
    folded = dot(one_hot(iota(shape, 1) // SCALE == iota(shape, 0)), wide)
    colours = channels // (SCALE * SCALE)
    row_lanes = breadth * SCALE
    for s in range(strips):
        for c in range(colours):
            first = (s * colours + c) * SCALE
            for y in range(WIN):
                start = (s * WIN + y) * SCALE
                final[c, start : start + SCALE] = folded[
                    first : first + SCALE, y * row_lanes : (y + 1) * row_lanes
                ]
    out_ref[...] = final[...].astype(BF16)


def is_even(axis):
    return lax.axis_index(axis) % 2 == 0


def swap_pairs(strip, axis, first):
    count = lax.axis_size(axis)
    pairs = [(i, i + 1) for i in range(first, count - 1, 2)]
    return lax.ppermute(strip, axis, pairs + [(j, i) for i, j in pairs])


def whole_swap(a, bit):
    count = lax.axis_size("var")
    return lax.ppermute(a, "var", [(i, i ^ bit) for i in range(count)])


def whole(a):
    return pl.BlockSpec(a.shape, lambda *i: (0,) * a.ndim)


def params(mebibytes):
    return pltpu.CompilerParams(
        dimension_semantics=("arbitrary",), vmem_limit_bytes=mebibytes * 1024 * 1024
    )


def local(
    features,
    labels,
    qkv_weight,
    proj_weight,
    up_weight,
    down_weight,
    swin_bias,
    recon_weight,
    refine_qkv,
    refine_proj,
    refine_bias,
):
    height, breadth, channels = features.shape
    heads = swin_bias.shape[1]
    out_channels = recon_weight.shape[-1]
    refine_heads = refine_bias.shape[0]
    lanes = round_up(channels + MARKS, LANES)
    hidden = round_up(up_weight.shape[-1], LANES)
    operands = (
        features,
        labels.T,
        jnp.swapaxes(qkv_weight, 0, 1),
        jnp.swapaxes(proj_weight, 0, 1),
        jnp.swapaxes(up_weight, 0, 1),
        down_weight.transpose(2, 0, 1),
        jnp.swapaxes(swin_bias, 0, 1),
        jnp.swapaxes(recon_weight, 1, 2),
    )
    head_rows, refine_rows = heads * HEAD_ROWS, refine_heads * HEAD_ROWS
    shapes = [
        ((2, 2 * head_rows + 16, lanes), BF16),
        ((2, lanes, lanes), BF16),
        ((2, 2 * LANES, lanes), BF16),
        ((2, lanes, hidden), BF16),
        ((2, hidden, lanes), BF16),
        ((VAR_DEV, lanes, 4 * LANES), BF16),
        ((2, VAR_DEV, CELLS, heads * CELLS), F32),
        (features.shape, BF16),
        (operands[1].shape, jnp.int32),
    ]
    shapes = [jax.ShapeDtypeStruct(*s) for s in shapes]
    prepared = pl.pallas_call(
        functools.partial(prepare_kernel, heads),
        grid=(1,),
        in_specs=[pl.BlockSpec(memory_space=pltpu.HBM)] * len(operands),
        out_specs=[whole(s) for s in shapes],
        out_shape=shapes,
        scratch_shapes=[
            *[pltpu.VMEM(a.shape, a.dtype) for a in operands[2:]],
            *[
                pltpu.VMEM((round_up(a.shape[2], LANES) // LANES, 2 * lanes, LANES), F32)
                for a in operands[2:6]
            ],
            pltpu.VMEM((heads, WIN, LANES), F32),
            pltpu.VMEM((round_up(2 * heads, 8), swin_bias.shape[2]), F32),
            pltpu.SemaphoreType.DMA((len(operands),)),
        ],
        compiler_params=params(16),
        name="prepare",
    )(*[pltpu.with_memory_space_constraint(a, pltpu.HBM) for a in operands])
    *swin, recon, bias, features, labels_across = prepared

    def block_specs(i):
        arrays = (bias, *swin)
        return arrays, [
            pl.BlockSpec((None,) + a.shape[1:], lambda *_, n=a.ndim: (i,) + (0,) * (n - 1))
            for a in arrays
        ]

    def cost(windows):
        return pl.CostEstimate(
            flops=windows * 400_000_000, bytes_accessed=windows * 200_000, transcendentals=0
        )

    arrays, specs = block_specs(0)
    strips = height // WIN
    tokens = WIN * breadth

    pair_axis = lax.axis_size("ty") == 2

    def block_one(places, name):
        rows = len(places) * WIN
        outs = [
            ((VAR_DEV, rows, breadth, lanes), F32),
            ((VAR_DEV, rows * SHIFT, lanes), BF16),
            ((VAR_DEV, rows * SHIFT, lanes), BF16),
        ]
        if places[0] == 0:
            outs += [((VAR_DEV, SHIFT, breadth, lanes), BF16)] * (1 if pair_axis else 2)
        outs = [jax.ShapeDtypeStruct(*o) for o in outs]
        return pl.pallas_call(
            functools.partial(first_kernel, heads, channels, places),
            grid=(1,),
            in_specs=[whole(features), whole(labels_across), *specs],
            out_specs=[whole(o) for o in outs],
            out_shape=outs,
            scratch_shapes=[
                pltpu.VMEM((len(places) * tokens, lanes), F32),
                pltpu.VMEM((2, rows * SHIFT, lanes), F32),
            ],
            compiler_params=params(12 if places[0] == 0 else 18),
            cost_estimate=cost(len(places) * breadth // WIN * VAR_DEV),
            name=name,
        )(features, labels_across, *arrays)

    y_ends, a_ends, b_ends, *own_ends = block_one((0, strips - 1), "block_one_ends")
    across = [swap_pairs(own, "ty", first) for first, own in enumerate(own_ends)]
    y_middle, a_middle, b_middle = block_one(tuple(range(1, strips - 1)), "block_one_middle")
    operands = (*across, a_ends, a_middle, b_ends, b_middle)
    strip_shape = jax.ShapeDtypeStruct((VAR_DEV, (height + 2 * SHIFT) * SHIFT, lanes), BF16)
    strips_out = pl.pallas_call(
        functools.partial(edge_kernel, len(across)),
        grid=(1,),
        in_specs=[whole(a) for a in operands],
        out_specs=[whole(strip_shape)] * 2,
        out_shape=[strip_shape] * 2,
        compiler_params=params(6),
        name="edges",
    )(*operands)
    sides = [swap_pairs(strip, "tx", first) for first, strip in enumerate(strips_out)]

    arrays, specs = block_specs(1)
    inner_count = (strips - 1) * (breadth // WIN - 1)
    outs = [
        jax.ShapeDtypeStruct((inner_count, VAR_DEV, CELLS, lanes), BF16),
        jax.ShapeDtypeStruct((strips, tokens, LANES), BF16),
    ]
    inner, marks = pl.pallas_call(
        functools.partial(inner_kernel, heads, channels),
        grid=(1,),
        in_specs=[whole(y_ends), whole(y_middle), *specs],
        out_specs=[whole(o) for o in outs],
        out_shape=outs,
        compiler_params=params(20),
        cost_estimate=cost(inner_count * VAR_DEV),
        name="block_two_inner",
    )(y_ends, y_middle, *arrays)

    tall, wide = height + 2 * SHIFT, breadth + 2 * SHIFT
    slots = 2 * (tall + wide) // WIN - 4
    operands = (y_ends, y_middle, *across, *sides, inner)
    half_shape = jax.ShapeDtypeStruct((strips // 2, out_channels, tokens), BF16)
    keep, give = pl.pallas_call(
        functools.partial(outer_kernel, heads, channels, len(across)),
        grid=(1,),
        in_specs=[*[whole(a) for a in operands], *specs, whole(recon)],
        out_specs=[whole(half_shape)] * 2,
        out_shape=[half_shape] * 2,
        scratch_shapes=[
            pltpu.VMEM((WIN, wide, lanes), F32),
            pltpu.VMEM((slots, VAR_DEV, CELLS, lanes), F32),
            pltpu.VMEM((slots, VAR_DEV, CELLS, lanes), BF16),
            pltpu.VMEM((tall + WIN, wide, 2 * LANES), F32),
        ],
        compiler_params=params(26),
        name="block_two_border",
    )(*operands, *arrays, recon)

    mine = (keep.astype(F32) + whole_swap(give, 1).astype(F32)).astype(BF16)
    other = whole_swap(mine, 2)
    shapes = [
        ((2 * refine_rows + 16, LANES), BF16),
        ((LANES, LANES), BF16),
        ((refine_heads * out_channels, LANES), BF16),
        ((CELLS, refine_heads * CELLS), F32),
    ]
    shapes = [jax.ShapeDtypeStruct(*s) for s in shapes]
    operands = (mine, refine_qkv, refine_proj, refine_bias)
    refine_qvt, refine_key, refine_projt, refine_grid = pl.pallas_call(
        functools.partial(prepare_refine_kernel, channels % LANES),
        grid=(1,),
        in_specs=[pl.BlockSpec(memory_space=pl.ANY)]
        + [pl.BlockSpec(memory_space=pltpu.HBM)] * 3,
        out_specs=[whole(s) for s in shapes],
        out_shape=shapes,
        scratch_shapes=[
            *[pltpu.VMEM(a.shape, a.dtype) for a in operands[1:]],
            pltpu.VMEM((refine_heads, WIN, LANES), F32),
            pltpu.SemaphoreType.DMA((3,)),
        ],
        compiler_params=params(6),
        name="prepare_refine",
    )(mine, *[pltpu.with_memory_space_constraint(a, pltpu.HBM) for a in operands[1:]])
    colours = out_channels // (SCALE * SCALE)
    operands = (mine, other, marks, refine_grid, refine_qvt, refine_key, refine_projt)
    out_shape = (colours, height * SCALE // 2, breadth * SCALE)
    refined = pl.pallas_call(
        functools.partial(refine_kernel, refine_heads, channels % LANES),
        grid=(1,),
        in_specs=[whole(a) for a in operands],
        out_specs=pl.BlockSpec(out_shape, lambda i: (0, 0, 0)),
        out_shape=jax.ShapeDtypeStruct(out_shape, BF16),
        scratch_shapes=[pltpu.VMEM(out_shape, F32)],
        compiler_params=params(8),
        name="refinement",
    )(*operands)
    received = whole_swap(refined, 1)
    even = is_even("var")
    halves = jnp.where(even, refined, received), jnp.where(even, received, refined)
    return jnp.concatenate(halves, axis=1).astype(F32)


def solution(mesh):
    placed = (P("ty", "tx", None), P("ty", "tx"), P(), P(), P(), P(), P(), P(), P(), P(), P())
    return jax.shard_map(
        local, mesh=mesh, in_specs=placed, out_specs=P(None, "ty", "tx"), check_vma=False
    )
```

```python
import functools

import jax
import jax.numpy as jnp
from jax import lax
from jax.experimental import pallas as pl
from jax.experimental.pallas import tpu as pltpu
from jax.sharding import PartitionSpec as P

WIN = 8
CELLS = WIN * WIN
SHIFT = 4
SCALE = 4
VAR_DEV = 2
CODES = 8
LANES = 128
HEAD_ROWS = 32
CLASSES = 4
MARKS = CLASSES + 2
CONSTANT = -2.0
SIDE = 2 * WIN - 1

EPSILON = 1e-05
LOG2E = 1.4426950408889634
BIG = float(2.0**100)
ERF_TANH = (0.7975076, 0.0370060, -0.00035159)
REACH = 36.0

NN = (((1,), (0,)), ((), ()))
NT = (((1,), (1,)), ((), ()))
F32 = jnp.float32
BF16 = jnp.bfloat16


def dot(a, b, dims=NN):
    return lax.dot_general(a, b, dims, preferred_element_type=F32)


def iota(shape, dim):
    return lax.broadcasted_iota(jnp.int32, shape, dim)


def round_up(size, multiple):
    return -(-size // multiple) * multiple


def one_hot(condition):
    return jnp.where(condition, 1.0, 0.0).astype(BF16)


def exact(a, b, dims=NN):
    return dot(a, b, dims).astype(BF16)


def pick_rows(source, size):
    return one_hot(iota((1, size), 1) == source)


def pick_columns(source, size):
    return one_hot(iota((size, 1), 0) == source)


def head_source(index, heads, width, first=0):
    unit = index % HEAD_ROWS
    keep = (unit < width) & (index < heads * HEAD_ROWS)
    return jnp.where(keep, first + index // HEAD_ROWS * width + unit, -1)


def query_value_source(heads, width, channels):
    row = iota((2 * heads * HEAD_ROWS + 16, 1), 0)
    values = row - heads * HEAD_ROWS - 16
    return jnp.where(
        values < 0,
        head_source(row, heads, width),
        head_source(jnp.maximum(values, 0), heads, width, 2 * channels),
    )


def query_value_marks(heads, width, lanes, first_lane):
    row = iota((2 * heads * HEAD_ROWS + 16, 1), 0)
    lane = iota((1, lanes), 1) - first_lane
    mark = row - heads * HEAD_ROWS
    is_class = (mark >= 0) & (mark < CLASSES)
    differ = jnp.where(is_class | (mark == CLASSES), -BIG / CONSTANT, 0.0)
    unit = (mark - 16) % HEAD_ROWS
    ones = jnp.where((mark >= 16) & (unit == width), 1.0 / CONSTANT, 0.0)
    same = jnp.where(is_class & (mark == lane), BIG, 0.0)
    return same + jnp.where(lane == CLASSES + 1, differ + ones, 0.0)


def key_marks(rows, lanes, first_row, first_lane):
    row = iota((rows, 1), 0) - first_row
    lane = iota((1, lanes), 1) - first_lane
    is_class = (lane >= 0) & (lane < CLASSES)
    same = jnp.where(is_class & (row == lane), 1.0, 0.0)
    pad = jnp.where(row == CLASSES, -1.0, jnp.where(row == CLASSES + 1, 1.0 / CONSTANT, 0.0))
    return same + jnp.where(lane == CLASSES, pad, 0.0)


def bias_rows(table, turn, flip_rows, flip_cols):
    shape = (1, WIN * LANES)
    lane = iota(shape, 1)
    row_step = lane % LANES // WIN - (WIN - 1)
    col_step = lane % WIN - lane // LANES
    row_step = jnp.where(flip_rows, -row_step, row_step)
    col_step = jnp.where(flip_cols, -col_step, col_step)
    lead = jnp.where(turn, col_step, row_step)
    trail = jnp.where(turn, row_step, col_step)
    index = (lead + WIN - 1) * SIDE + trail + WIN - 1
    pick = one_hot(iota((table.shape[1], WIN * LANES), 0) == index)
    rest = table * LOG2E
    parts = []
    for _ in range(3):
        parts.append(rest.astype(BF16))
        rest = rest - parts[-1].astype(F32)
    moved = dot(jnp.concatenate(parts, axis=0), pick)
    size = table.shape[0]
    return moved[:size] + moved[size : 2 * size] + moved[2 * size :]


def bias_grid(rows, rows_ref, store):
    heads = rows.shape[0]
    for key_col in range(WIN):
        rows_ref[0:heads, key_col, :] = rows[:, key_col * LANES : (key_col + 1) * LANES]
    half = iota((WIN, LANES), 1)
    for pair in range(heads // 2):
        even, odd = rows_ref[2 * pair], rows_ref[2 * pair + 1]
        for key_row in range(WIN):
            start = (WIN - 1 - key_row) * WIN
            left = pltpu.roll(even, (LANES - start) % LANES, 1)
            right = pltpu.roll(odd, (LANES - start + CELLS) % LANES, 1)
            store(key_row, pair, jnp.where(half < CELLS, left, right))


def prepare_kernel(
    heads,
    features_ref,
    labels_ref,
    *refs,
):
    sources, outs, scratch = refs[:6], refs[6:15], refs[15:]
    held, spreads, (rows_ref, tables_ref, semaphores) = scratch[:6], scratch[6:10], scratch[10:]
    (
        qvt_out,
        key_out,
        proj_out,
        up_out,
        down_out,
        recon_out,
        bias_out,
        features_out,
        labels_out,
    ) = outs
    arrivals = [
        pltpu.make_async_copy(source, target, semaphores.at[i])
        for i, (source, target) in enumerate(
            zip(
                (*sources, features_ref, labels_ref), (*held, features_out, labels_out)
            )
        )
    ]
    for arrival in arrivals:
        arrival.start()
    (
        qkv_ref,
        proj_ref,
        up_ref,
        down_ref,
        swin_bias_ref,
        recon_ref,
    ) = held
    channels, blocks, hidden = up_ref.shape
    width = channels // heads
    lanes = key_out.shape[1]
    head_rows = heads * HEAD_ROWS
    taps, out, _ = recon_ref.shape
    both = blocks * channels

    arrivals[4].wait()
    for i in range(blocks):
        tables_ref[i * heads : (i + 1) * heads] = swin_bias_ref[:, i]
    rows = []
    for v in range(VAR_DEV):
        code = lax.axis_index("var") * VAR_DEV + v
        turn, flip_rows, flip_cols = code // 4 == 1, code // 2 % 2 == 1, code % 2 == 1
        rows.append(bias_rows(tables_ref[: blocks * heads], turn, flip_rows, flip_cols))
    row = iota((2 * LANES, 1), 0)
    head, unit = row % LANES // HEAD_ROWS * 2 + row // LANES, row % HEAD_ROWS
    proj_source = jnp.where((head < heads) & (unit < width), head * width + unit, -1)
    query_values = pick_rows(query_value_source(heads, width, channels), 3 * channels)
    keys = pick_columns(head_source(iota((1, lanes), 1), heads, width, channels), 3 * channels)
    hidden_rows = pick_rows(iota((down_out.shape[1], 1), 0), hidden)
    proj_rows = pick_rows(proj_source, lanes)
    for arrival in (*arrivals[:4], arrivals[5]):
        arrival.wait()

    def block_rows(ref, spread_ref):
        size = ref.shape[2]
        rows = ref[...].reshape(both, size).astype(F32)
        pieces = [[] for _ in range(blocks)]
        for at in range(0, size, LANES):
            used = min(LANES, size - at)
            place = at // LANES
            spread_ref[place, :both, :used] = rows[:, at : at + used]
            spread_ref[place, both:] = jnp.zeros((blocks * lanes - both, LANES), F32)
            for i in range(blocks):
                piece = spread_ref[place, pl.ds(i, lanes, stride=blocks), :]
                pieces[i].append(piece[:, :used].astype(BF16))
        return [jnp.concatenate(piece, axis=1) for piece in pieces]

    qkv, proj, up, down = (
        block_rows(ref, spread)
        for ref, spread in zip((qkv_ref, proj_ref, up_ref, down_ref), spreads)
    )

    pad = pick_rows(iota((lanes, 1), 0), channels)
    kernel = exact(pad, recon_ref[...].reshape(taps * out, channels), NT)
    row = iota((2 * head_rows + 16, 1), 0)
    scale = jnp.where(row < head_rows, width**-0.5 * LOG2E, 1.0)
    query_add = query_value_marks(heads, width, lanes, channels)
    key_add = key_marks(lanes, lanes, channels, head_rows)
    for i in range(blocks):
        qvt_out[i] = (dot(query_values, qkv[i], NT) * scale + query_add).astype(BF16)
        key_out[i] = (dot(qkv[i], keys) + key_add).astype(BF16)
        proj_out[i] = jnp.zeros(proj_out.shape[1:], BF16)
        proj_out[i, :, :channels] = exact(proj_rows, proj[i])
        up_out[i] = jnp.zeros(up_out.shape[1:], BF16)
        up_out[i, :, :hidden] = up[i]
        down_out[i] = (dot(hidden_rows, down[i], NT) * 0.5).astype(BF16)
    for v in range(VAR_DEV):
        code = lax.axis_index("var") * VAR_DEV + v
        turn, flip_rows, flip_cols = code // 4 == 1, code // 2 % 2 == 1, code % 2 == 1
        lane = iota((1, 4 * LANES), 1)
        tile, lane = lane // LANES, lane % LANES
        part = jnp.where(lane >= 2 * out, 2, jnp.where(lane >= out, 1, 0))
        is_last = tile == 3
        is_left = (tile == 0) & (part == 2)
        row_step = jnp.where(is_last, part, jnp.where(is_left, 2, tile)) - 1
        col_step = jnp.where(is_last | is_left, 2, part) - 1
        channel = lane - part * out + jnp.where(is_left, LANES - 2 * out, 0)
        used = (channel < out) & (is_last | is_left | (part < 2))
        row_step = jnp.where(flip_rows, -row_step, row_step)
        col_step = jnp.where(flip_cols, -col_step, col_step)
        tap = (jnp.where(turn, col_step, row_step) + 1) * 3
        tap = tap + jnp.where(turn, row_step, col_step) + 1
        sub_row = channel % (SCALE * SCALE) // SCALE
        sub_col = channel % SCALE
        sub_row = jnp.where(flip_rows, SCALE - 1 - sub_row, sub_row)
        sub_col = jnp.where(flip_cols, SCALE - 1 - sub_col, sub_col)
        source = channel // (SCALE * SCALE) * SCALE * SCALE
        source = source + jnp.where(turn, sub_col, sub_row) * SCALE
        source = tap * out + source + jnp.where(turn, sub_row, sub_col)
        source = jnp.where(used, source, -1)
        recon_out[v] = exact(kernel, pick_columns(source, taps * out))

    for v in range(VAR_DEV):
        for i in range(blocks):

            def store(key_row, pair, value):
                at = slice(key_row * WIN, (key_row + 1) * WIN)
                bias_out[i, v, at, pair * LANES : (pair + 1) * LANES] = value

            bias_grid(rows[v][i * heads : (i + 1) * heads], rows_ref, store)

    for arrival in arrivals[6:]:
        arrival.wait()


def prepare_refine_kernel(
    mark, after_ref, qkv_source, proj_source, bias_source, *refs
):
    refine_qvt_out, refine_key_out, refine_proj_out, refine_bias_out = refs[:4]
    refine_qkv_ref, refine_proj_ref, refine_bias_ref, rows_ref, semaphores = refs[4:]
    arrivals = [
        pltpu.make_async_copy(source, target, semaphores.at[i])
        for i, (source, target) in enumerate(
            zip((qkv_source, proj_source, bias_source), refs[4:7])
        )
    ]
    for arrival in arrivals:
        arrival.start()
    for arrival in arrivals:
        arrival.wait()
    out = refine_proj_ref.shape[0]
    refine_heads = refine_bias_ref.shape[0]
    refine_width = out // refine_heads
    refine_rows = refine_heads * HEAD_ROWS
    never = lax.axis_index("var") < 0
    refine_table = bias_rows(refine_bias_ref[...], never, never, never)
    weight = refine_qkv_ref[...]
    source = query_value_source(refine_heads, refine_width, out)
    refine_moved = exact(pick_rows(source, 3 * out), weight, NT)
    source = head_source(iota((1, LANES), 1), refine_heads, refine_width, out)
    refine_keys = exact(weight, pick_columns(source, 3 * out))
    refine_proj = []
    for h in range(refine_heads):
        row = iota((LANES, 1), 0)
        source = jnp.where(row < refine_width, row + h * refine_width, -1)
        refine_proj.append(exact(pick_rows(source, out), refine_proj_ref[...]))

    row = iota((2 * refine_rows + 16, 1), 0)
    scale = jnp.where(row < refine_rows, refine_width**-0.5 * LOG2E, 1.0)
    out_pad = pick_rows(iota((LANES, 1), 0), out)
    refine_qvt_out[...] = (
        dot(refine_moved, out_pad, NT) * scale
        + query_value_marks(refine_heads, refine_width, LANES, mark)
    ).astype(BF16)
    refine_key_out[...] = (
        dot(out_pad, refine_keys) + key_marks(LANES, LANES, mark, refine_rows)
    ).astype(BF16)
    for h in range(refine_heads):
        square = dot(refine_proj[h], out_pad, NT)
        refine_proj_out[h * out : (h + 1) * out] = square.T[:out].astype(BF16)
    def store_refine(key_row, pair, value):
        refine_bias_out[key_row * WIN : (key_row + 1) * WIN] = value

    bias_grid(refine_table, rows_ref, store_refine)


def twice_gelu(x):
    x = x.astype(BF16)
    square = jnp.minimum(x * x, BF16(REACH))
    first, second, third = (BF16(factor) for factor in ERF_TANH)
    series = (square * third + second) * square + first
    return x + x * jnp.tanh(x * series)


def normalize(x, channels, keep_marks):
    tiles = [x[:, i : i + LANES] for i in range(0, x.shape[1], LANES)]
    inside = iota((1, LANES), 1) < channels - (len(tiles) - 1) * LANES
    mean = jnp.sum(sum(tiles[1:], tiles[0]), axis=1, keepdims=True) * (1.0 / channels)
    centred = [tile - mean for tile in tiles]
    centred[-1] = jnp.where(inside, centred[-1], 0.0)
    squares = [tile * tile for tile in centred]
    spread = jnp.sum(sum(squares[1:], squares[0]), axis=1, keepdims=True) * (1.0 / channels)
    scale = lax.rsqrt(spread + EPSILON)
    result = [tile * scale for tile in centred]
    if keep_marks:
        result[-1] = jnp.where(inside, result[-1], tiles[-1])
    return jnp.concatenate(result, axis=1).astype(BF16)


def split_queries(queries, heads):
    pairs = heads // 2
    head_rows = heads * HEAD_ROWS
    left = iota((1, LANES), 1) < CELLS
    turned = pltpu.roll(queries, CELLS, 1).astype(BF16)
    queries = queries.astype(BF16)
    zero = jnp.zeros((HEAD_ROWS, LANES), BF16)
    results = []
    for even, odd in ((queries, turned), (turned, queries)):
        marks = jnp.where(left, even[head_rows:], odd[head_rows:])
        columns = []
        for pair in range(pairs):
            at = pair * 2 * HEAD_ROWS
            rows = [zero] * heads
            rows[2 * pair] = jnp.where(left, even[at : at + HEAD_ROWS], zero)
            rows[2 * pair + 1] = jnp.where(left, zero, odd[at + HEAD_ROWS : at + 2 * HEAD_ROWS])
            rows.append(marks)
            columns.append(jnp.concatenate(rows, axis=0))
        results.append(jnp.concatenate(columns, axis=1) if pairs > 1 else columns[0])
    return results


def heads_of(n, heads, w_qvt, w_key):
    mark_rows = heads * HEAD_ROWS + 16
    both = dot(w_qvt, n, NT)
    queries = both[:mark_rows]
    values = both[mark_rows:].astype(BF16)
    keys = dot(n, w_key).astype(BF16)
    scores = []
    for place in range(n.shape[0] // LANES):
        cut = slice(place * LANES, (place + 1) * LANES)
        for half, stationary in enumerate(split_queries(queries[:, cut], heads)):
            at = place * LANES + half * CELLS
            scores.append(dot(keys[at : at + CELLS, : stationary.shape[0]], stationary))
    return scores, values


def soft(scores):
    largest = jnp.max(scores, axis=0, keepdims=True)
    return jnp.exp2(scores - largest).astype(BF16)


def mix_pair(values, first, second, heads, ones_row):
    zero = jnp.zeros((CELLS, LANES), BF16)
    lane = iota((HEAD_ROWS, 2 * LANES), 1) % LANES
    mixed = []
    for pair in range(heads // 2):
        cut = slice(pair * LANES, (pair + 1) * LANES)
        stationary = jnp.concatenate(
            [
                jnp.concatenate([first[:, cut], zero], axis=1),
                jnp.concatenate([zero, second[:, cut]], axis=1),
            ],
            axis=0,
        )
        result = dot(values[pair * CELLS : (pair + 1) * CELLS], stationary)
        joined = jnp.where(lane < CELLS, result[:HEAD_ROWS], result[HEAD_ROWS:])
        mixed.append(joined * pl.reciprocal(joined[ones_row : ones_row + 1]))
    return mixed


def swin_unit(x, pairs, results, heads, channels, bias, w_qvt, w_key, w_proj, w_up, w_down):
    width = channels // heads
    mark_rows = heads * HEAD_ROWS + 16
    n = normalize(x, channels, True)
    yield
    both = dot(w_qvt[...], n, NT)
    queries = both[:mark_rows]
    values = both[mark_rows:].astype(BF16)
    keys = dot(n, w_key[...]).astype(BF16)
    yield
    scores = []
    for place in range(x.shape[0] // LANES):
        cut = slice(place * LANES, (place + 1) * LANES)
        for half, stationary in enumerate(split_queries(queries[:, cut], heads)):
            at = place * LANES + half * CELLS
            scores.append(dot(keys[at : at + CELLS, : stationary.shape[0]], stationary))
    yield
    weights = [
        (soft(scores[2 * place] + bias(a)), soft(scores[2 * place + 1] + bias(b)))
        for place, a, b in pairs
    ]
    yield
    pad = jnp.zeros((LANES - heads // 2 * HEAD_ROWS, 2 * LANES), F32)
    blocks = []
    for (place, _, _), (first, second) in zip(pairs, weights):
        cut = slice(place * LANES, (place + 1) * LANES)
        mixed = mix_pair(values[:, cut], first, second, heads, width)
        blocks.append(jnp.concatenate(mixed + [pad], axis=0).astype(BF16))
    yield
    outputs = []
    for block in blocks:
        for half in range(2):
            turned = block[:, half * LANES : (half + 1) * LANES].T
            outputs.append(jnp.concatenate([turned[:CELLS], turned[CELLS:]], axis=1))
    outputs = jnp.concatenate(outputs, axis=0)
    yield
    x = jnp.concatenate([x[place * LANES : (place + 1) * LANES] for place, _, _ in pairs], axis=0)
    h = x + dot(outputs, w_proj[...])
    yield
    n = normalize(h, channels, False)
    yield
    hidden = dot(n, w_up[...])
    yield
    hidden = twice_gelu(hidden)
    yield
    y = h + dot(hidden, w_down[...])
    results.extend(y[i * LANES : (i + 1) * LANES] for i in range(len(pairs)))


def swin_block(x, pairs, unit, lag, *args):
    places = x.shape[0] // LANES
    units = []
    for low in range(0, places, unit):
        high = min(low + unit, places)
        picked = [i for i, pair in enumerate(pairs) if low <= pair[0] < high]
        moved = [(pairs[i][0] - low, *pairs[i][1:]) for i in picked]
        found = []
        units.append((picked, found, swin_unit(x[low * LANES : high * LANES], moved, found, *args)))
    running = dict(enumerate(units))
    tick = 0
    while running:
        for number in sorted(running):
            if tick >= number * lag and next(running[number][2], StopIteration) is StopIteration:
                del running[number]
        tick += 1
    results = [None] * len(pairs)
    for picked, found, _ in units:
        for i, result in zip(picked, found):
            results[i] = result
    return results


def windows_of(grid):
    lanes = grid.shape[2]
    return jnp.concatenate(
        [
            grid[:, w * WIN : (w + 1) * WIN].reshape(CELLS, lanes)
            for w in range(grid.shape[1] // WIN)
        ],
        axis=0,
    )


def first_kernel(heads, channels, strips, x_ref, labels_ref, bias_ref, *refs):
    ends = strips[0] == 0
    *weights, y_ref, side_a_ref, side_b_ref = refs[:8]
    held, side = refs[-2:]
    breadth = x_ref.shape[1]
    count = breadth // WIN
    tokens, lanes = held.shape
    part = tokens // len(strips)
    rows_total = labels_ref.shape[1]
    for k, strip in enumerate(strips):
        rows = x_ref[strip * WIN : (strip + 1) * WIN].astype(F32)
        held[k * part : (k + 1) * part, :channels] = windows_of(rows)
    labels = labels_ref[...].astype(F32).astype(BF16)
    row_gap = iota((CELLS, rows_total), 1) - iota((CELLS, rows_total), 0) // WIN
    col_gap = iota((CELLS, breadth), 1) - iota((CELLS, breadth), 0) % WIN
    by_row = [dot(one_hot(row_gap == strip * WIN), labels, NT) for strip in strips]
    cells = [jnp.where(col_gap == w * WIN, rows, 0.0) for rows in by_row for w in range(count)]
    label = dot(
        jnp.concatenate(cells, axis=0).astype(BF16), jnp.ones((breadth, LANES), BF16)
    )
    lane = iota((1, LANES), 1) - channels % LANES
    wanted = jnp.where((lane >= 0) & (lane < CLASSES), lane + 1, -1).astype(F32)
    fixed = jnp.where(lane == CLASSES, 1.0, jnp.where(lane == CLASSES + 1, CONSTANT, 0.0))
    tail = jnp.where(lane < 0, held[:, lanes - LANES :], jnp.where(label == wanted, 1.0, fixed))
    x = jnp.concatenate([held[:, : lanes - LANES], tail], axis=1)
    places = tokens // LANES
    pairs = [(place, v, v) for v in range(VAR_DEV) for place in range(places)]
    results = swin_block(x, pairs, x.shape[0], 1, heads, channels, lambda v: bias_ref[v], *weights)
    for v in range(VAR_DEV):
        for k in range(len(strips)):
            windows = []
            for w in range(count):
                group = k * count + w
                block = results[v * places + group // 2]
                at = group % 2 * CELLS
                windows.append(block[at : at + CELLS].reshape(WIN, WIN, lanes))
            y_ref[v, k * WIN : (k + 1) * WIN] = jnp.concatenate(windows, axis=1)
            at = k * WIN * SHIFT
            for r in range(WIN):
                rows = slice(at + r * SHIFT, at + (r + 1) * SHIFT)
                side[0, rows] = windows[0][r, :SHIFT]
                side[1, rows] = windows[-1][r, SHIFT:]
        left, right = side[0].astype(BF16), side[1].astype(BF16)
        even = is_even("tx")
        side_a_ref[v] = jnp.where(even, right, left)
        side_b_ref[v] = jnp.where(even, left, right)
    if ends:
        top, bottom = y_ref[:, :SHIFT].astype(BF16), y_ref[:, 2 * WIN - SHIFT :].astype(BF16)
        even = is_even("ty")
        refs[8][...] = jnp.where(even, bottom, top)
        if len(refs) == 12:
            refs[9][...] = jnp.where(even, top, bottom)


def tile_rows(ends_ref, middle_ref, v, first, count, columns):
    height = middle_ref.shape[1] + 2 * WIN
    pieces = []
    while count > 0:
        if first < WIN:
            ref, at, limit = ends_ref, first, WIN - first
        elif first < height - WIN:
            ref, at, limit = middle_ref, first - WIN, height - WIN - first
        else:
            ref, at, limit = ends_ref, first - height + 2 * WIN, height - first
        taken = min(count, limit)
        pieces.append(ref[v, at : at + taken, columns])
        first, count = first + taken, count - taken
    return pieces[0] if len(pieces) == 1 else jnp.concatenate(pieces, axis=0)


def inner_kernel(heads, channels, ends_ref, middle_ref, bias_ref, *refs):
    *weights, y_ref, marks_ref = refs
    breadth, lanes = middle_ref.shape[2:]
    strips = middle_ref.shape[1] // WIN + 2
    count = breadth // WIN - 1
    for strip in range(strips):
        rows = tile_rows(ends_ref, middle_ref, 0, strip * WIN, WIN, slice(None))
        marks_ref[strip] = windows_of(rows[:, :, lanes - LANES :]).astype(BF16)
    x = jnp.concatenate(
        [
            tile_rows(
                ends_ref,
                middle_ref,
                v,
                strip * WIN + SHIFT,
                WIN,
                slice(SHIFT + w * WIN, SHIFT + (w + 1) * WIN),
            ).reshape(CELLS, lanes)
            for strip in range(strips - 1)
            for w in range(count)
            for v in range(VAR_DEV)
        ],
        axis=0,
    )
    pairs = [(w, 0, 1) for w in range((strips - 1) * count)]
    results = swin_block(x, pairs, 4, 1, heads, channels, lambda v: bias_ref[v], *weights)
    for w, result in enumerate(results):
        y_ref[w] = result.astype(BF16).reshape(VAR_DEV, CELLS, lanes)


def received(refs, axis, after, place):
    value = refs[0][place].astype(F32)
    other = refs[1][place].astype(F32) if len(refs) > 1 else 0.0
    return jnp.where(is_even(axis) == after, value, other)


def edge_kernel(swaps, *refs):
    across, own, outs = refs[:swaps], refs[swaps : swaps + 4], refs[swaps + 4 :]
    breadth = across[0].shape[2]
    half = WIN * SHIFT
    corner = SHIFT * SHIFT
    for first in range(2):
        ends, middle = own[2 * first : 2 * first + 2]
        out = outs[first]
        at_right = is_even("tx") == (first == 0)
        last = out.shape[1] - corner
        for v in range(VAR_DEV):
            for start, after in ((0, False), (last, True)):
                rows = received(across, "ty", after, v)
                cells = jnp.where(at_right, rows[:, breadth - SHIFT :], rows[:, :SHIFT])
                cells = jnp.concatenate([cells[r] for r in range(SHIFT)], axis=0)
                out[v, start : start + corner] = cells.astype(BF16)
            out[v, corner : corner + half] = ends[v, :half]
            out[v, corner + half : last - half] = middle[v]
            out[v, last - half : last] = ends[v, half:]


def outer_kernel(
    heads,
    channels,
    swaps,
    ends_ref,
    middle_ref,
    *refs,
):
    across, sides, (inner_ref, bias_ref) = refs[:swaps], refs[swaps : swaps + 2], refs[swaps + 2 : swaps + 4]
    refs = refs[swaps + 4 :]
    *weights, w_recon, keep_ref, give_ref, rows_held, x_held, y_held, acc = refs
    lanes = middle_ref.shape[3]
    height, breadth = middle_ref.shape[1] + 2 * WIN, middle_ref.shape[2]
    tall, wide = height + 2 * SHIFT, breadth + 2 * SHIFT
    strips, count = tall // WIN, wide // WIN
    always = iota((1, lanes), 1) == channels + CLASSES + 1

    def marked(refs, axis, after, place):
        return jnp.where(always, CONSTANT, received(refs, axis, after, place))

    for v in range(VAR_DEV):
        for end in range(2):
            outside, inside = (0, SHIFT) if end == 0 else (SHIFT, 0)
            corner = 0 if end == 0 else (tall - SHIFT) * SHIFT
            first = 0 if end == 0 else 2 * WIN - SHIFT
            between = slice(SHIFT, SHIFT + breadth)
            rows_held[outside : outside + SHIFT, between] = marked(
                across, "ty", end == 1, v
            )
            rows_held[inside : inside + SHIFT, between] = ends_ref[v, first : first + SHIFT]
            side_first = SHIFT * SHIFT if end == 0 else (tall - 2 * SHIFT) * SHIFT
            for side, at in ((0, 0), (1, wide - SHIFT)):
                for rows, start in ((outside, corner), (inside, side_first)):
                    cut = (v, slice(start, start + SHIFT * SHIFT))
                    piece = marked(sides, "tx", side == 1, cut)
                    rows_held[rows : rows + SHIFT, at : at + SHIFT] = piece.reshape(
                        SHIFT, SHIFT, lanes
                    )
            for w in range(count):
                x_held[end * count + w, v] = rows_held[:, w * WIN : (w + 1) * WIN].reshape(
                    CELLS, lanes
                )
        for strip in range(1, strips - 1):
            cut = slice(strip * WIN * SHIFT, (strip + 1) * WIN * SHIFT)
            for end in range(2):
                piece = marked(sides, "tx", end == 1, (v, cut))
                piece = piece.reshape(WIN, SHIFT, lanes)
                at = 0 if end == 0 else breadth - SHIFT
                near = slice(at, at + SHIFT)
                own = tile_rows(ends_ref, middle_ref, v, strip * WIN - SHIFT, WIN, near)
                both = [piece, own] if end == 0 else [own, piece]
                slot = 2 * count + 2 * (strip - 1) + end
                x_held[slot, v] = jnp.concatenate(both, axis=1).reshape(CELLS, lanes)

    slots = x_held.shape[0]
    x = x_held[...].reshape(slots * VAR_DEV * CELLS, lanes)
    pairs = [(w, 0, 1) for w in range(slots)]
    results = swin_block(x, pairs, 6, 3, heads, channels, lambda v: bias_ref[v], *weights)
    at = channels + CLASSES
    for w in range(slots):
        valid = x[w * LANES : (w + 1) * LANES, at : at + 1]
        y_held[w] = (results[w] * valid).astype(BF16).reshape(VAR_DEV, CELLS, lanes)

    weights = w_recon[...].reshape(VAR_DEV * lanes, w_recon.shape[2])
    out_channels = keep_ref.shape[1]

    def scatter(strip, windows):
        tokens = [jnp.concatenate(windows(v), axis=0) for v in range(VAR_DEV)]
        total = dot(jnp.concatenate(tokens, axis=1), weights)
        tiles = [total[:, i : i + LANES] for i in range(0, total.shape[1], LANES)]
        spare = LANES - 2 * out_channels
        lane = iota((1, LANES), 1)
        last = jnp.where(
            lane < spare,
            pltpu.roll(tiles[3], spare, 1),
            pltpu.roll(tiles[0], 2 * spare, 1),
        )
        after = [tiles[3], pltpu.roll(tiles[3], LANES - out_channels, 1), last]
        for e in range(3):
            rows = slice(strip * WIN + 2 - e, (strip + 1) * WIN + 2 - e)
            for at, tile in ((0, tiles[e]), (LANES, after[e])):
                tile = tile.reshape(count, WIN, WIN, LANES)
                for w in range(count):
                    place = (rows, slice(w * WIN, (w + 1) * WIN), slice(at, at + LANES))
                    acc[place] = tile[w] if e == 0 else acc[place] + tile[w]

    def finish(strip):
        rows = slice(1 + SHIFT + strip * WIN, 1 + SHIFT + (strip + 1) * WIN)
        centre = acc[rows, SHIFT : SHIFT + breadth, :LANES]
        centre = pltpu.roll(centre.reshape(WIN * breadth, LANES), LANES - out_channels, 1)
        result = (
            acc[rows, SHIFT - 1 : SHIFT - 1 + breadth, :LANES]
            + centre.reshape(WIN, breadth, LANES)
            + acc[rows, SHIFT + 1 : SHIFT + 1 + breadth, LANES : 2 * LANES]
        )
        return windows_of(result).T[:out_channels].astype(BF16)

    results = []
    scatter(0, lambda v: [y_held[w, v] for w in range(count)])
    for strip in range(1, strips):
        if strip == strips - 1:
            scatter(strip, lambda v: [y_held[count + w, v] for w in range(count)])
        else:
            slot = 2 * count + 2 * (strip - 1)
            first = (strip - 1) * (count - 2)
            scatter(
                strip,
                lambda v: [
                    y_held[slot, v],
                    *[inner_ref[first + w, v] for w in range(count - 2)],
                    y_held[slot + 1, v],
                ],
            )
        results.append(finish(strip - 1))
    half = len(results) // 2
    even = is_even("var")
    for strip in range(half):
        keep_ref[strip] = jnp.where(even, results[strip], results[strip + half])
        give_ref[strip] = jnp.where(even, results[strip + half], results[strip])


def refine_kernel(
    heads, first_mark, mine_ref, other_ref, marks_ref, bias_ref, w_qvt, w_key, w_projt, out_ref, final
):
    strips, channels, strip_tokens = mine_ref.shape
    breadth = strip_tokens // WIN
    width = channels // heads
    z = jnp.concatenate(
        [mine_ref[s].astype(F32) + other_ref[s].astype(F32) for s in range(strips)], axis=1
    ) * (1.0 / CODES)
    mean = jnp.sum(z, axis=0, keepdims=True) * (1.0 / channels)
    centred = z - mean
    spread = jnp.sum(centred * centred, axis=0, keepdims=True) * (1.0 / channels)
    normed = centred * lax.rsqrt(spread + EPSILON)
    tall = jnp.concatenate([normed, jnp.zeros((LANES - channels, normed.shape[1]), F32)], axis=0)
    first = lax.axis_index("var") % 2 * strips
    marks = jnp.concatenate([marks_ref[first + s].astype(F32) for s in range(strips)], axis=0)
    lane = iota((1, LANES), 1)
    is_mark = (lane >= first_mark) & (lane < first_mark + MARKS)
    n = jnp.where(is_mark, marks, tall.T).astype(BF16)
    scores, values = heads_of(n, heads, w_qvt[...], w_key[...])
    probabilities = [soft(s + bias_ref[...]) for s in scores]
    lane = iota((channels, LANES), 1)
    branches = []
    for pair in range(len(probabilities) // 2):
        mixed = mix_pair(
            values[:, pair * LANES : (pair + 1) * LANES],
            probabilities[2 * pair],
            probabilities[2 * pair + 1],
            heads,
            width,
        )[0].astype(BF16)
        both = dot(w_projt[...][:, :HEAD_ROWS], mixed)
        even, odd = both[:channels], both[channels:]
        halves = []
        for half in range(2):
            cut = slice(half * LANES, (half + 1) * LANES)
            halves.append(even[:, cut] + pltpu.roll(odd[:, cut], CELLS, 1))
        branches.append(jnp.where(lane < CELLS, halves[0], pltpu.roll(halves[1], CELLS, 1)))
    refined = (z + jnp.concatenate(branches, axis=1)).astype(BF16)
    stacked = jnp.concatenate(
        [refined[:, s * strip_tokens : (s + 1) * strip_tokens] for s in range(strips)], axis=0
    )
    shape = (strip_tokens, WIN * breadth * SCALE)
    cell = iota(shape, 1) // SCALE
    source = (cell % breadth // WIN) * CELLS + (cell // breadth) * WIN + cell % WIN
    wide = dot(stacked, one_hot(iota(shape, 0) == source))
    own = iota(wide.shape, 1) % SCALE == iota(wide.shape, 0) % SCALE
    wide = jnp.where(own, wide, 0.0).astype(BF16)
    shape = (wide.shape[0] // SCALE, wide.shape[0])
    folded = dot(one_hot(iota(shape, 1) // SCALE == iota(shape, 0)), wide)
    colours = channels // (SCALE * SCALE)
    row_lanes = breadth * SCALE
    for s in range(strips):
        for c in range(colours):
            first = (s * colours + c) * SCALE
            for y in range(WIN):
                start = (s * WIN + y) * SCALE
                final[c, start : start + SCALE] = folded[
                    first : first + SCALE, y * row_lanes : (y + 1) * row_lanes
                ]
    out_ref[...] = final[...].astype(BF16)


def is_even(axis):
    return lax.axis_index(axis) % 2 == 0


def swap_pairs(strip, axis, first):
    count = lax.axis_size(axis)
    pairs = [(i, i + 1) for i in range(first, count - 1, 2)]
    return lax.ppermute(strip, axis, pairs + [(j, i) for i, j in pairs])


def whole_swap(a, bit):
    count = lax.axis_size("var")
    return lax.ppermute(a, "var", [(i, i ^ bit) for i in range(count)])


def whole(a):
    return pl.BlockSpec(a.shape, lambda *i: (0,) * a.ndim)


def params(mebibytes):
    return pltpu.CompilerParams(
        dimension_semantics=("arbitrary",), vmem_limit_bytes=mebibytes * 1024 * 1024
    )


def local(
    features,
    labels,
    qkv_weight,
    proj_weight,
    up_weight,
    down_weight,
    swin_bias,
    recon_weight,
    refine_qkv,
    refine_proj,
    refine_bias,
):
    height, breadth, channels = features.shape
    heads = swin_bias.shape[1]
    out_channels = recon_weight.shape[-1]
    refine_heads = refine_bias.shape[0]
    lanes = round_up(channels + MARKS, LANES)
    hidden = round_up(up_weight.shape[-1], LANES)
    operands = (
        features,
        labels.T,
        jnp.swapaxes(qkv_weight, 0, 1),
        jnp.swapaxes(proj_weight, 0, 1),
        jnp.swapaxes(up_weight, 0, 1),
        down_weight.transpose(2, 0, 1),
        jnp.swapaxes(swin_bias, 0, 1),
        jnp.swapaxes(recon_weight, 1, 2),
    )
    head_rows, refine_rows = heads * HEAD_ROWS, refine_heads * HEAD_ROWS
    shapes = [
        ((2, 2 * head_rows + 16, lanes), BF16),
        ((2, lanes, lanes), BF16),
        ((2, 2 * LANES, lanes), BF16),
        ((2, lanes, hidden), BF16),
        ((2, hidden, lanes), BF16),
        ((VAR_DEV, lanes, 4 * LANES), BF16),
        ((2, VAR_DEV, CELLS, heads * CELLS), F32),
        (features.shape, BF16),
        (operands[1].shape, jnp.int32),
    ]
    shapes = [jax.ShapeDtypeStruct(*s) for s in shapes]
    prepared = pl.pallas_call(
        functools.partial(prepare_kernel, heads),
        grid=(1,),
        in_specs=[pl.BlockSpec(memory_space=pltpu.HBM)] * len(operands),
        out_specs=[whole(s) for s in shapes],
        out_shape=shapes,
        scratch_shapes=[
            *[pltpu.VMEM(a.shape, a.dtype) for a in operands[2:]],
            *[
                pltpu.VMEM((round_up(a.shape[2], LANES) // LANES, 2 * lanes, LANES), F32)
                for a in operands[2:6]
            ],
            pltpu.VMEM((heads, WIN, LANES), F32),
            pltpu.VMEM((round_up(2 * heads, 8), swin_bias.shape[2]), F32),
            pltpu.SemaphoreType.DMA((len(operands),)),
        ],
        compiler_params=params(16),
        name="prepare",
    )(*[pltpu.with_memory_space_constraint(a, pltpu.HBM) for a in operands])
    *swin, recon, bias, features, labels_across = prepared

    def block_specs(i):
        arrays = (bias, *swin)
        return arrays, [
            pl.BlockSpec((None,) + a.shape[1:], lambda *_, n=a.ndim: (i,) + (0,) * (n - 1))
            for a in arrays
        ]

    def cost(windows):
        return pl.CostEstimate(
            flops=windows * 400_000_000, bytes_accessed=windows * 200_000, transcendentals=0
        )

    arrays, specs = block_specs(0)
    strips = height // WIN
    tokens = WIN * breadth

    pair_axis = lax.axis_size("ty") == 2

    def block_one(places, name):
        rows = len(places) * WIN
        outs = [
            ((VAR_DEV, rows, breadth, lanes), F32),
            ((VAR_DEV, rows * SHIFT, lanes), BF16),
            ((VAR_DEV, rows * SHIFT, lanes), BF16),
        ]
        if places[0] == 0:
            outs += [((VAR_DEV, SHIFT, breadth, lanes), BF16)] * (1 if pair_axis else 2)
        outs = [jax.ShapeDtypeStruct(*o) for o in outs]
        return pl.pallas_call(
            functools.partial(first_kernel, heads, channels, places),
            grid=(1,),
            in_specs=[whole(features), whole(labels_across), *specs],
            out_specs=[whole(o) for o in outs],
            out_shape=outs,
            scratch_shapes=[
                pltpu.VMEM((len(places) * tokens, lanes), F32),
                pltpu.VMEM((2, rows * SHIFT, lanes), F32),
            ],
            compiler_params=params(12 if places[0] == 0 else 18),
            cost_estimate=cost(len(places) * breadth // WIN * VAR_DEV),
            name=name,
        )(features, labels_across, *arrays)

    y_ends, a_ends, b_ends, *own_ends = block_one((0, strips - 1), "block_one_ends")
    across = [swap_pairs(own, "ty", first) for first, own in enumerate(own_ends)]
    y_middle, a_middle, b_middle = block_one(tuple(range(1, strips - 1)), "block_one_middle")
    operands = (*across, a_ends, a_middle, b_ends, b_middle)
    strip_shape = jax.ShapeDtypeStruct((VAR_DEV, (height + 2 * SHIFT) * SHIFT, lanes), BF16)
    strips_out = pl.pallas_call(
        functools.partial(edge_kernel, len(across)),
        grid=(1,),
        in_specs=[whole(a) for a in operands],
        out_specs=[whole(strip_shape)] * 2,
        out_shape=[strip_shape] * 2,
        compiler_params=params(6),
        name="edges",
    )(*operands)
    sides = [swap_pairs(strip, "tx", first) for first, strip in enumerate(strips_out)]

    arrays, specs = block_specs(1)
    inner_count = (strips - 1) * (breadth // WIN - 1)
    outs = [
        jax.ShapeDtypeStruct((inner_count, VAR_DEV, CELLS, lanes), BF16),
        jax.ShapeDtypeStruct((strips, tokens, LANES), BF16),
    ]
    inner, marks = pl.pallas_call(
        functools.partial(inner_kernel, heads, channels),
        grid=(1,),
        in_specs=[whole(y_ends), whole(y_middle), *specs],
        out_specs=[whole(o) for o in outs],
        out_shape=outs,
        compiler_params=params(20),
        cost_estimate=cost(inner_count * VAR_DEV),
        name="block_two_inner",
    )(y_ends, y_middle, *arrays)

    tall, wide = height + 2 * SHIFT, breadth + 2 * SHIFT
    slots = 2 * (tall + wide) // WIN - 4
    operands = (y_ends, y_middle, *across, *sides, inner)
    half_shape = jax.ShapeDtypeStruct((strips // 2, out_channels, tokens), BF16)
    keep, give = pl.pallas_call(
        functools.partial(outer_kernel, heads, channels, len(across)),
        grid=(1,),
        in_specs=[*[whole(a) for a in operands], *specs, whole(recon)],
        out_specs=[whole(half_shape)] * 2,
        out_shape=[half_shape] * 2,
        scratch_shapes=[
            pltpu.VMEM((WIN, wide, lanes), F32),
            pltpu.VMEM((slots, VAR_DEV, CELLS, lanes), F32),
            pltpu.VMEM((slots, VAR_DEV, CELLS, lanes), BF16),
            pltpu.VMEM((tall + WIN, wide, 2 * LANES), F32),
        ],
        compiler_params=params(26),
        name="block_two_border",
    )(*operands, *arrays, recon)

    mine = (keep.astype(F32) + whole_swap(give, 1).astype(F32)).astype(BF16)
    other = whole_swap(mine, 2)
    shapes = [
        ((2 * refine_rows + 16, LANES), BF16),
        ((LANES, LANES), BF16),
        ((refine_heads * out_channels, LANES), BF16),
        ((CELLS, refine_heads * CELLS), F32),
    ]
    shapes = [jax.ShapeDtypeStruct(*s) for s in shapes]
    operands = (mine, refine_qkv, refine_proj, refine_bias)
    refine_qvt, refine_key, refine_projt, refine_grid = pl.pallas_call(
        functools.partial(prepare_refine_kernel, channels % LANES),
        grid=(1,),
        in_specs=[pl.BlockSpec(memory_space=pl.ANY)]
        + [pl.BlockSpec(memory_space=pltpu.HBM)] * 3,
        out_specs=[whole(s) for s in shapes],
        out_shape=shapes,
        scratch_shapes=[
            *[pltpu.VMEM(a.shape, a.dtype) for a in operands[1:]],
            pltpu.VMEM((refine_heads, WIN, LANES), F32),
            pltpu.SemaphoreType.DMA((3,)),
        ],
        compiler_params=params(6),
        name="prepare_refine",
    )(mine, *[pltpu.with_memory_space_constraint(a, pltpu.HBM) for a in operands[1:]])
    colours = out_channels // (SCALE * SCALE)
    operands = (mine, other, marks, refine_grid, refine_qvt, refine_key, refine_projt)
    out_shape = (colours, height * SCALE // 2, breadth * SCALE)
    refined = pl.pallas_call(
        functools.partial(refine_kernel, refine_heads, channels % LANES),
        grid=(1,),
        in_specs=[whole(a) for a in operands],
        out_specs=pl.BlockSpec(out_shape, lambda i: (0, 0, 0)),
        out_shape=jax.ShapeDtypeStruct(out_shape, BF16),
        scratch_shapes=[pltpu.VMEM(out_shape, F32)],
        compiler_params=params(8),
        name="refinement",
    )(*operands)
    received = whole_swap(refined, 1)
    even = is_even("var")
    halves = jnp.where(even, refined, received), jnp.where(even, received, refined)
    return jnp.concatenate(halves, axis=1).astype(F32)


def solution(mesh):
    placed = (P("ty", "tx", None), P("ty", "tx"), P(), P(), P(), P(), P(), P(), P(), P(), P())
    return jax.shard_map(
        local, mesh=mesh, in_specs=placed, out_specs=P(None, "ty", "tx"), check_vma=False
    )
```
